32 devices in a mesh: dp: 8 (over z, core), tensor: 4 (over y, x).
Axes of the slice: x: 2, y: 2, z: 4, core: 2. Of those that a mesh axis runs over, the one named last changes fastest.
Arguments:
- tokens: bfloat16 [8192, 2048], P('dp'), may hold values from -6 to 6
- segments: int32 [8, 1024], P('dp'), may hold values from 0 to 3, never falling along the last dimension, each value on 1 to 800 neighbouring positions
- cotangent: bfloat16 [8192, 2048], P('dp'), may hold values from -6 to 6
- norm_params: float32 [4, 2048], replicated, may hold values from -2 to 2
- norm_m: float32 [4, 2048], replicated
- norm_v: float32 [4, 2048], replicated, as said below
- qkv_bias: float32 [3, 32, 64], P(None, 'tensor', 'dp'), may hold values from -1.5 to 1.5
- bias_m: float32 [3, 32, 64], P(None, 'tensor', 'dp')
- bias_v: float32 [3, 32, 64], P(None, 'tensor', 'dp'), as said below
- w_qkv: float32 [2048, 3, 2048], P('dp', None, 'tensor'), may hold values from -0.125 to 0.125
- qkv_m: float32 [2048, 3, 2048], P('dp', None, 'tensor')
- qkv_v: float32 [2048, 3, 2048], P('dp', None, 'tensor'), as said below
- w_out: float32 [2048, 2048], P('tensor', 'dp'), may hold values from -0.75 to 0.75
- out_m: float32 [2048, 2048], P('tensor', 'dp')
- out_v: float32 [2048, 2048], P('tensor', 'dp'), as said below
- w_gateup: float32 [2048, 2, 5632], P('dp', None, 'tensor'), may hold values from -0.125 to 0.125
- gateup_m: float32 [2048, 2, 5632], P('dp', None, 'tensor')
- gateup_v: float32 [2048, 2, 5632], P('dp', None, 'tensor'), as said below
- w_down: float32 [5632, 2048], P('tensor', 'dp'), may hold values from -0.078125 to 0.078125
- down_m: float32 [5632, 2048], P('tensor', 'dp')
- down_v: float32 [5632, 2048], P('tensor', 'dp'), as said below
Outputs:
- block_out: bfloat16 [8192, 2048], P(('dp', 'tensor'))
- input_grad: float32 [8192, 2048], P(('dp', 'tensor'))
- norm_first: float32 [4, 2048], replicated
- norm_second: float32 [4, 2048], replicated
- norm_new: float32 [4, 2048], replicated
- bias_first: float32 [3, 32, 64], P(None, 'tensor', 'dp')
- bias_second: float32 [3, 32, 64], P(None, 'tensor', 'dp')
- bias_new: float32 [3, 32, 64], P(None, 'tensor', 'dp')
- qkv_first: float32 [2048, 3, 2048], P('dp', None, 'tensor')
- qkv_second: float32 [2048, 3, 2048], P('dp', None, 'tensor')
- qkv_new: float32 [2048, 3, 2048], P('dp', None, 'tensor')
- out_first: float32 [2048, 2048], P('tensor', 'dp')
- out_second: float32 [2048, 2048], P('tensor', 'dp')
- out_new: float32 [2048, 2048], P('tensor', 'dp')
- gateup_first: float32 [2048, 2, 5632], P('dp', None, 'tensor')
- gateup_second: float32 [2048, 2, 5632], P('dp', None, 'tensor')
- gateup_new: float32 [2048, 2, 5632], P('dp', None, 'tensor')
- down_first: float32 [5632, 2048], P('tensor', 'dp')
- down_second: float32 [5632, 2048], P('tensor', 'dp')
- down_new: float32 [5632, 2048], P('tensor', 'dp')
The draws below stay inside these ranges and needn't reach their ends.
Inputs may be any that keep to these rules, and one draw needn't show every extreme that they name: `norm_v`: entries positive. `bias_v`: entries positive. `qkv_v`: entries positive. `out_v`: entries positive. `gateup_v`: entries positive. `down_v`: entries positive.
All inputs are finite; a program needn't handle non-finite values.
Results may differ from the reference program's by a relative error of at most 0.015.
Values may be sent and summed in bfloat16 or wider, within the bound.
A program may use at most 320 MiB of HBM per device.

```python
import math
import jax
import jax.numpy as jnp
import numpy as np
from jax import lax

D = 2048
H = 32
HD = 64
FF = 5632
LEN = 1024
STEP = 10
NSEQ = 8
TOKENS = 8192


def first_moment(key, shape, factor):
    size = factor * math.sqrt(TOKENS)
    return jax.random.truncated_normal(key, -4.0, 4.0, shape, jnp.float32) * (size / 9.0)


def second_moment(key, shape, factor):
    size = factor * math.sqrt(TOKENS)
    return jnp.exp(jax.random.uniform(key, shape, jnp.float32, 0.0, math.log(4.0))) * (size * size / 19.0)


def draw_norm_params(key, part):
    key = jax.random.fold_in(key, 1)
    gains = jax.random.uniform(jax.random.fold_in(key, 0), (2, D), jnp.float32, 0.6, 1.4)
    shifts = jax.random.truncated_normal(jax.random.fold_in(key, 1), -4.0, 4.0, (2, D), jnp.float32) * 0.3
    return jnp.stack([gains[0], shifts[0], gains[1], shifts[1]])


def draw_norm_m(key, part):
    key = jax.random.fold_in(key, 2)
    return first_moment(key, (4, D), 1.0)


def draw_norm_v(key, part):
    key = jax.random.fold_in(key, 3)
    return second_moment(key, (4, D), 1.0)


def draw_bias_m(key, part):
    key = jax.random.fold_in(key, 4)
    return first_moment(key, (3, H, HD), 0.7)


def draw_bias_v(key, part):
    key = jax.random.fold_in(key, 5)
    return second_moment(key, (3, H, HD), 0.7)


def draw_qkv_m(key, part):
    key = jax.random.fold_in(key, 6)
    return first_moment(key, (D, 3, D), 0.7)


def draw_qkv_v(key, part):
    key = jax.random.fold_in(key, 7)
    return second_moment(key, (D, 3, D), 0.7)


def draw_out_m(key, part):
    key = jax.random.fold_in(key, 8)
    return first_moment(key, (D, D), 0.2)


def draw_out_v(key, part):
    key = jax.random.fold_in(key, 9)
    return second_moment(key, (D, D), 0.2)


def draw_gateup_m(key, part):
    key = jax.random.fold_in(key, 10)
    return first_moment(key, (D, 2, FF), 0.35)


def draw_gateup_v(key, part):
    key = jax.random.fold_in(key, 11)
    return second_moment(key, (D, 2, FF), 0.35)


def draw_down_m(key, part):
    key = jax.random.fold_in(key, 12)
    return first_moment(key, (FF, D), 0.6)


def draw_down_v(key, part):
    key = jax.random.fold_in(key, 13)
    return second_moment(key, (FF, D), 0.6)


def steps_of(key, shape, split, low, high):
    def one(position, shards_of):
        heights = jax.random.uniform(jax.random.fold_in(jax.random.fold_in(key, 6), position), (shards_of,), jnp.float32, low / len(split), high / len(split))
        return jnp.repeat(jnp.exp(heights), shape[position] // shards_of).reshape((-1,) + (1,) * (len(shape) - position - 1))

    level = one(*split[0])
    for cut in split[1:]:
        level = level * one(*cut)
    return level


def split_up(number_of, total, most, skew):
    loads = [(1 << 20) // math.isqrt(rank ** skew) + 1 for rank in range(2, number_of + 1)]
    surplus, holding = total - most - (number_of - 1), [1] * (number_of - 1)
    while surplus > 0:
        movable = [i for i in range(number_of - 1) if holding[i] < most]
        mass, remaining = sum([loads[i] for i in movable]), surplus
        for i in movable:
            extra = min(most - holding[i], max(1, remaining * loads[i] // mass), surplus)
            holding[i] = holding[i] + extra
            surplus = surplus - extra
    return np.array([most] + holding)


def uneven_parts(own_key, count, total, most, slope):
    if count == 2:
        one = jax.random.randint(own_key, (), max(1, total - most), min(most, total - 1) + 1)
        return jnp.stack([one, total - one])
    sizes = jnp.asarray(split_up(count, total, most, slope), jnp.int32)
    couples = (count - 1) // 2
    source_of, receiver = sizes[1:1 + 2 * couples:2], sizes[2:2 + 2 * couples:2]
    room = jnp.minimum(source_of - 1, most - receiver)
    shifted = jax.random.randint(jax.random.fold_in(own_key, 1), (couples,), 0, 1 << 20) % (room + 1)
    sizes = sizes.at[1:1 + 2 * couples:2].set(source_of - shifted).at[2:2 + 2 * couples:2].set(receiver + shifted)
    return sizes[jax.random.permutation(jax.random.fold_in(own_key, 2), count)]


def noise(key, shape, spread, reach, pieces=(), kind=jnp.bfloat16):
    values = jax.random.normal(key, shape, jnp.float32) * spread
    if len(pieces) > 0:
        values = steps_of(key, shape, pieces, -0.22, 0.18) * values
    return jnp.clip(values, min=-reach, max=reach).astype(kind)


def setup_inputs(seed: int = 0) -> dict:
    key_of = jax.random.split(jax.random.key(seed), 22)
    return {
        "tokens": noise(key_of[0], (TOKENS, D), 1.0, 6.0, ((0, 8),)),
        "segments": jax.vmap(lambda own: jnp.searchsorted(jnp.cumsum(uneven_parts(own, max(LEN // 256, 3), LEN, LEN * 25 // 32, 2)), jnp.arange(LEN), side="right"))(jax.random.split(key_of[1], NSEQ)).reshape((NSEQ, LEN)).astype(jnp.int32),
        "cotangent": noise(key_of[2], (TOKENS, D), 1.0, 6.0, ((0, 8),)),
        "norm_params": draw_norm_params(jax.random.fold_in(key_of[21], 71), 0),
        "norm_m": draw_norm_m(jax.random.fold_in(key_of[21], 71), 0),
        "norm_v": draw_norm_v(jax.random.fold_in(key_of[21], 71), 0),
        "qkv_bias": noise(key_of[6], (3, H, HD), 0.3, 1.5, ((1, 4), (2, 8)), jnp.float32),
        "bias_m": draw_bias_m(jax.random.fold_in(key_of[21], 71), 0),
        "bias_v": draw_bias_v(jax.random.fold_in(key_of[21], 71), 0),
        "w_qkv": noise(key_of[9], (D, 3, D), D ** -0.5, 0.125, ((0, 8), (2, 4)), jnp.float32),
        "qkv_m": draw_qkv_m(jax.random.fold_in(key_of[21], 71), 0),
        "qkv_v": draw_qkv_v(jax.random.fold_in(key_of[21], 71), 0),
        "w_out": noise(key_of[12], (D, D), HD ** -0.5, 0.75, ((0, 4), (1, 8)), jnp.float32),
        "out_m": draw_out_m(jax.random.fold_in(key_of[21], 71), 0),
        "out_v": draw_out_v(jax.random.fold_in(key_of[21], 71), 0),
        "w_gateup": noise(key_of[15], (D, 2, FF), D ** -0.5, 0.125, ((0, 8), (2, 4)), jnp.float32),
        "gateup_m": draw_gateup_m(jax.random.fold_in(key_of[21], 71), 0),
        "gateup_v": draw_gateup_v(jax.random.fold_in(key_of[21], 71), 0),
        "w_down": noise(key_of[18], (FF, D), FF ** -0.5, 0.078125, ((0, 4), (1, 8)), jnp.float32),
        "down_m": draw_down_m(jax.random.fold_in(key_of[21], 71), 0),
        "down_v": draw_down_v(jax.random.fold_in(key_of[21], 71), 0),
    }


@jax.custom_vjp
def low(v):
    return lax.optimization_barrier(v.astype(jnp.bfloat16)).astype(jnp.float32)

@jax.custom_vjp
def low_back(v):
    return v

def low_keep(v):
    return (low(v), None)

def low_pass(kept, grad):
    return (grad,)

def back_keep(v):
    return (v, None)

def back_low(kept, grad):
    return (low(grad),)
low.defvjp(low_keep, low_pass)
low_back.defvjp(back_keep, back_low)
NORM_EPS = 1e-05
BETA_ONE = 0.9
BETA_TWO = 0.95
ADAM_EPS = 1e-08
DECAY = 0.1
ROPE_BASE = 10000.0

def matmul_high(left, right):
    return jnp.dot(left, right, precision=lax.Precision.HIGHEST, preferred_element_type=jnp.float32)

def layer_norm(values, gain, shift):
    centre = values - lax.optimization_barrier(jnp.mean(values, axis=1, keepdims=True))
    inv_std = lax.rsqrt(lax.optimization_barrier(jnp.mean(centre * centre, axis=1, keepdims=True)) + NORM_EPS)
    return centre * inv_std * gain[None, :] + shift[None, :]

def doc_positions(segments):
    length = segments.shape[1]
    index = jnp.arange(length, dtype=jnp.int32)
    starts = jnp.concatenate([jnp.ones((segments.shape[0], 1), jnp.bool_), segments[:, 1:] != segments[:, :-1]], axis=1)
    marker = jnp.where(starts, index[None, :], jnp.zeros_like(segments))
    return index[None, :] - lax.cummax(marker, axis=1)

def rope_angles(positions):
    half_dim = HD // 8
    freqs = ROPE_BASE ** (-2.0 * jnp.arange(half_dim, dtype=jnp.float32) / (HD // 4))
    return positions.astype(jnp.float32)[:, None] * freqs[None, :]

def rotate(values, angles):
    n_tok = values.shape[0]
    half_dim = HD // 8
    heads = values.reshape(n_tok, -1, HD)
    cosine = jnp.cos(angles)[:, None, :]
    sine_term = jnp.sin(angles)[:, None, :]
    lead_part = heads[:, :, :half_dim]
    next_part = heads[:, :, half_dim:2 * half_dim]
    turned = jnp.concatenate([lead_part * cosine - next_part * sine_term, next_part * cosine + lead_part * sine_term, heads[:, :, 2 * half_dim:]], axis=2)
    return turned.reshape(n_tok, -1)

def doc_mask(seg_ids):
    index = jnp.arange(seg_ids.shape[0], dtype=jnp.int32)
    return (seg_ids[:, None] == seg_ids[None, :]) & (index[None, :] <= index[:, None])

def attend_one(queries, key_rows, value_rows, seg_ids):
    scores = low_back(jnp.einsum('qhe,khe->hqk', queries, key_rows, precision=lax.Precision.HIGHEST) * HD ** (-0.5))
    allowed = doc_mask(seg_ids)[None]
    top_score = lax.optimization_barrier(jnp.max(jnp.where(allowed, scores, -1e+30), axis=2, keepdims=True))
    expo = jnp.where(allowed, jnp.exp(scores - top_score), 0.0)
    probs = low(expo / lax.optimization_barrier(jnp.sum(expo, axis=2, keepdims=True)))
    return jnp.einsum('hqk,khe->qhe', probs, value_rows, precision=lax.Precision.HIGHEST)

def attend_all(queries, key_rows, value_rows, segments):
    n_seq, seq_len = segments.shape
    checked = jax.checkpoint(attend_one)

    def one_sequence(carry, parts):
        return (carry, checked(*parts))
    shape = (n_seq, seq_len, H, HD)
    _, mixed = lax.scan(one_sequence, None, (queries.reshape(shape), key_rows.reshape(shape), value_rows.reshape(shape), segments))
    return mixed.reshape(n_seq * seq_len, D)

def forward(inputs, segments, norm_params, bias, w_qkv, w_out, w_gateup, w_down):
    n_tok = inputs.shape[0]
    h_one = low(layer_norm(inputs, norm_params[0], norm_params[1]))
    projected = low_back(matmul_high(h_one, w_qkv.reshape(D, 3 * D)) + bias.reshape(1, 3 * D)).reshape(n_tok, 3, D)
    angles = rope_angles(doc_positions(segments).reshape(n_tok))
    queries = low(rotate(projected[:, 0], angles))
    key_rows = low(rotate(projected[:, 1], angles))
    value_rows = low(projected[:, 2])
    mixed = low_back(low(attend_all(queries, key_rows, value_rows, segments)))
    resid = inputs + low_back(matmul_high(mixed, w_out))
    h_two = low(layer_norm(resid, norm_params[2], norm_params[3]))
    gate_up = low_back(matmul_high(h_two, w_gateup.reshape(D, 2 * FF))).reshape(n_tok, 2, FF)
    hidden = low(jax.nn.silu(gate_up[:, 0]) * gate_up[:, 1])
    return resid + low_back(matmul_high(hidden, w_down))

def adamw(weight, first, second, grad, rate, decay):
    new_first = BETA_ONE * first + (1.0 - BETA_ONE) * grad
    new_second = BETA_TWO * second + (1.0 - BETA_TWO) * grad * grad
    direction = new_first / (1.0 - BETA_ONE ** STEP) / (jnp.sqrt(new_second / (1.0 - BETA_TWO ** STEP)) + ADAM_EPS)
    return (new_first, new_second, weight - rate * (direction + decay * weight))

def working(weight):
    return weight.astype(jnp.bfloat16).astype(jnp.float32)

def reference(tokens, segments, cotangent, norm_params, norm_m, norm_v, qkv_bias, bias_m, bias_v, w_qkv, qkv_m, qkv_v, w_out, out_m, out_v, w_gateup, gateup_m, gateup_v, w_down, down_m, down_v):

    def block(inputs, norms, bias, weight_qkv, weight_out, weight_gu, weight_down):
        return forward(inputs, segments, norms, bias, weight_qkv, weight_out, weight_gu, weight_down)
    result, pullback = jax.vjp(block, tokens.astype(jnp.float32), norm_params, working(qkv_bias), working(w_qkv), working(w_out), working(w_gateup), working(w_down))
    grads = pullback(cotangent.astype(jnp.float32))
    norm_first, norm_second, norm_new = adamw(norm_params, norm_m, norm_v, grads[1], 0.5, 0.0)
    bias_first, bias_second, bias_new = adamw(qkv_bias, bias_m, bias_v, grads[2], 0.3, 0.0)
    qkv_first, qkv_second, qkv_new = adamw(w_qkv, qkv_m, qkv_v, grads[3], D ** (-0.5), DECAY)
    out_first, out_second, out_new = adamw(w_out, out_m, out_v, grads[4], HD ** (-0.5), DECAY)
    gateup_first, gateup_second, gateup_new = adamw(w_gateup, gateup_m, gateup_v, grads[5], D ** (-0.5), DECAY)
    down_first, down_second, down_new = adamw(w_down, down_m, down_v, grads[6], FF ** (-0.5), DECAY)
    return (result.astype(jnp.bfloat16), grads[0], norm_first, norm_second, norm_new, bias_first, bias_second, bias_new, qkv_first, qkv_second, qkv_new, out_first, out_second, out_new, gateup_first, gateup_second, gateup_new, down_first, down_second, down_new)
```

```python
from types import SimpleNamespace

import numpy as np
import jax
import jax.numpy as jnp
from jax import lax
from jax.experimental import pallas as pl
from jax.experimental.pallas import tpu as pltpu
from jax.sharding import PartitionSpec as P

D = 2048
HD = 64
FF = 5632
STEP = 10

NORM_EPS = 1e-05
BETA_ONE = 0.9
BETA_TWO = 0.95
ADAM_EPS = 1e-08
DECAY = 0.1
ROPE_BASE = 10000.0

BF = jnp.bfloat16
F32 = jnp.float32
MESH = pl.DeviceIdType.MESH
LANES = 128
MASKED = -1e30

QKV, OUT, GU0, GU1, DOWN = range(5)


def dot_nn(a, b):
    return lax.dot_general(a, b, (((1,), (0,)), ((), ())), preferred_element_type=F32)


def dot_nt(a, b):
    return lax.dot_general(a, b, (((1,), (1,)), ((), ())), preferred_element_type=F32)


def dot_tn(a, b):
    return lax.dot_general(a, b, (((0,), (0,)), ((), ())), preferred_element_type=F32)


def chunks(total, step):
    return [(lo, min(step, total - lo)) for lo in range(0, total, step)]


def normed(values):
    centre = values - jnp.mean(values, axis=1, keepdims=True)
    inv = lax.rsqrt(jnp.mean(centre * centre, axis=1, keepdims=True) + NORM_EPS)
    return centre * inv, inv


def norm_back(grad, hat, inv, gain):
    e = grad * gain
    return inv * (
        e - jnp.mean(e, axis=1, keepdims=True) - hat * jnp.mean(e * hat, axis=1, keepdims=True)
    )


def make_kernel(names, n, wl, fl, dpn, tpn, cast):
    nc = dpn // 2
    ds = D // dpn
    sr = n // tpn
    w3 = 3 * wl
    f2 = 2 * fl
    half = ds // 2
    qb = min(256, n)
    nq = n // qb
    rt = min(256, sr)
    lt = min(128, sr)
    pairs = wl // LANES
    gl = wl // 2
    g3 = 3 * gl
    hr = sr // 2
    square = tpn == 4
    turned = w3 + n <= f2
    scale = HD ** (-0.5)
    has_via = nc >= 3

    def kern(*refs):
        R = SimpleNamespace(**dict(zip(names, refs, strict=True)))
        dpi = lax.axis_index("dp")
        t = lax.axis_index("tensor")
        z = lax.div(dpi, 2)
        c = lax.rem(dpi, 2)
        oc = 1 - c
        sib = dpi + 1 - 2 * c

        def chip(k):
            return lax.rem(z + k, nc)

        def dp_of(s):
            return 2 * s + c

        def flip(i, k):
            return lax.rem(i + k, 2) + 2 * lax.rem(lax.div(i, 2) + lax.div(k, 2), 2)

        def peer(k):
            k = jnp.asarray(k, jnp.int32)
            return flip(t, k) if square else lax.rem(t + k, tpn)

        def source(k):
            k = jnp.asarray(k, jnp.int32)
            return flip(t, k) if square else lax.rem(t + tpn - k, tpn)

        def remote(src, dst, ss, rs, dp, tn):
            return pltpu.make_async_remote_copy(
                src_ref=src,
                dst_ref=dst,
                send_sem=ss,
                recv_sem=rs,
                device_id=(dp, tn),
                device_id_type=MESH,
            )

        def arrived(dst, rs):
            remote(dst, dst, R.dum.at[0], rs, sib, t).wait_recv()

        def sent(src, ss):
            remote(src, src, ss, R.dum.at[0], sib, t).wait_send()

        def local(src, dst, i):
            cp = pltpu.make_async_copy(src, dst, R.loc.at[i])
            cp.start()
            return cp

        def local_now(src, dst):
            local(src, dst, 0).wait()

        def rows_of(i, size):
            return pl.ds(pl.multiple_of(i * size, size), size)

        own_rows = rows_of(t, sr)

        bar = pltpu.get_barrier_semaphore()
        pl.semaphore_signal(bar, inc=1, device_id=(sib, t), device_id_type=MESH)
        for k in range(1, nc):
            pl.semaphore_signal(bar, inc=1, device_id=(dp_of(chip(k)), t), device_id_type=MESH)
        for k in range(1, tpn):
            pl.semaphore_signal(bar, inc=1, device_id=(dpi, peer(k)), device_id_type=MESH)

        def all_here():
            pl.semaphore_wait(bar, 1 + (nc - 1) + (tpn - 1))

        def shard(u):
            return {
                QKV: lambda: R.wq_s,
                OUT: lambda: R.wo_s,
                GU0: lambda: R.wgu_s.at[pl.ds(0, half)],
                GU1: lambda: R.wgu_s.at[pl.ds(half, half)],
                DOWN: lambda: R.wd_s,
            }[u]()

        def place(u, j):
            return {
                QKV: lambda: R.ag_q.at[rows_of(j, ds)],
                OUT: lambda: R.wo.at[:, rows_of(j, ds)],
                GU0: lambda: R.wgu.at[pl.ds(pl.multiple_of(j * ds, ds), half)],
                GU1: lambda: R.wgu.at[pl.ds(pl.multiple_of(j * ds + half, half), half)],
                DOWN: lambda: R.ag_d.at[:, rows_of(j, ds)],
            }[u]()

        def relayed(src, dst):
            if not has_via:
                return src != src
            return ((src == 2) & (dst == 0)) | ((src == nc - 3) & (dst == nc - 1))

        def when(cond):
            return pl.when(cond)

        def within(s):
            return (s >= 0) & (s < nc)

        def apart(s):
            return (s - z >= 2) | (z - s >= 2)

        relays = ((1, 2, 0), (nc - 2, nc - 3, nc - 1)) if has_via else ()

        def ag_copy(u, d):
            return remote(
                shard(u), place(u, dpi), R.ag_s.at[u, d], R.ag_r.at[u, z], dp_of(d), t
            )

        def ag_near(u):
            for d in (z + 1, z - 1):

                @when(within(d))
                def _():
                    ag_copy(u, d).start()

            remote(shard(u), place(u, dpi), R.sb_s.at[u, z], R.sb_r.at[u, z], sib, t).start()
            local(shard(u), place(u, dpi), 22 + nc + u)

        def to_sibling(u, s):
            here = place(u, dp_of(s))
            remote(here, here, R.sb_s.at[u, s], R.sb_r.at[u, s], sib, t).start()

        def ag_far(u):
            for s in (z + 1, z - 1):

                @when(within(s))
                def _():
                    arrived(place(u, dp_of(s)), R.ag_r.at[u, s])

            for i, (mid, src, dst) in enumerate(relays):

                @when(z == mid)
                def _():
                    here = place(u, dp_of(src))
                    remote(
                        here, here, R.av_s.at[u, i], R.ag_r.at[u, src], dp_of(dst), t
                    ).start()

            for d in range(nc):

                @when(apart(d) & jnp.logical_not(relayed(z, d)))
                def _():
                    ag_copy(u, d).start()

            for s in (z + 1, z - 1):

                @when(within(s))
                def _():
                    to_sibling(u, s)

        def ag_rest(u):
            for s in range(nc):

                @when(apart(s))
                def _():
                    arrived(place(u, dp_of(s)), R.ag_r.at[u, s])
                    to_sibling(u, s)

        def ag_sent(u):
            for d in range(nc):

                @when((z != d) & jnp.logical_not(relayed(z, d)))
                def _():
                    sent(shard(u), R.ag_s.at[u, d])

        def ag_done(u):
            pltpu.make_async_copy(shard(u), place(u, dpi), R.loc.at[22 + nc + u]).wait()
            for s in range(nc):
                arrived(place(u, 2 * s + oc), R.sb_r.at[u, s])

        def ag_drain(u):
            for i, (mid, src, dst) in enumerate(relays):

                @when(z == mid)
                def _():
                    sent(place(u, dp_of(src)), R.av_s.at[u, i])

            for s in range(nc):
                sent(shard(u), R.sb_s.at[u, s])

        def rs_merged(src, dst):
            if not has_via:
                return src != src
            return ((src == 0) & (dst == nc - 1)) | ((src == nc - 1) & (dst == 0))

        def rs_held(dst):
            if not has_via:
                return z != z
            return ((z == 1) & (dst == nc - 1)) | ((z == nc - 2) & (dst == 0))

        merges = ((0, 1, nc - 1), (nc - 1, nc - 2, 0)) if has_via else ()

        def unit(i, slot, zr, vr, red, shape):
            return SimpleNamespace(i=i, slot=slot, zr=zr, vr=vr, red=red, shape=shape)

        RD = unit(0, lambda d: R.box0.at[d], R.zr0, R.vr0, R.red0, (fl, ds))
        RGU = unit(1, lambda d: R.box1.at[d], R.zr1, R.vr1, R.red1, (ds, f2))
        RO = unit(2, lambda d: R.box0.at[d, pl.ds(0, wl)], R.zr2, R.vr2, R.red2, (wl, ds))

        def RQ(g):
            lanes = pl.ds(g * g3, g3) if isinstance(g, int) else rows_of(g, g3)
            return unit(
                3 + g,
                lambda d: R.dt.at[rows_of(d, ds), lanes],
                R.zrq.at[g],
                R.vrq.at[g],
                R.redq.at[g],
                (ds, g3),
            )

        def free_signal(i):
            pl.semaphore_signal(R.free.at[i], inc=1, device_id=(sib, t), device_id_type=MESH)

        def row_loop(total, cols):
            step = 128 if cols <= 512 else 16

            def over(act):
                @pl.loop(0, total // step)
                def _(i):
                    act(rows_of(i, step))

            return over

        def rs_unit(u, compute, stage, mine, pump=None):
            def finish(d):
                box = u.slot(d)
                arrived(box, R.rb_r.at[u.i, d])

                @row_loop(*u.shape)
                def _(rows):
                    box[rows, :] = (mine[rows] + box[rows, :].astype(F32)).astype(BF)

                @when((z != d) & jnp.logical_not(rs_held(d)) & jnp.logical_not(rs_merged(z, d)))
                def _():
                    remote(
                        box, u.zr.at[z], R.rz_s.at[u.i, d], R.rz_r.at[u.i, z], dp_of(d), t
                    ).start()

                for i, (src, mid, dst) in enumerate(merges):

                    @when((z == src) & (d == dst))
                    def _():
                        remote(
                            box, u.vr.at[i], R.rz_s.at[u.i, d], R.rv_r.at[u.i, i], dp_of(mid), t
                        ).start()

            def turn(i):
                return lax.rem(i + nc - 1, nc)

            @pl.loop(0, nc)
            def _(idx):
                d = turn(idx)
                slot = lax.rem(idx, 2)

                @when(idx >= 2)
                def _():
                    sent(stage.at[slot], R.rb_s.at[u.i, turn(idx + nc - 2)])

                def to_stage(lo, size, val):
                    stage[slot, :, lo : lo + size] = val.astype(BF)

                compute(2 * d + oc, to_stage)
                remote(
                    stage.at[slot], u.slot(d), R.rb_s.at[u.i, d], R.rb_r.at[u.i, d], sib, t
                ).start()

                @when(idx >= 1)
                def _():
                    finish(turn(idx + nc - 1))

                if pump is not None:

                    @when(idx == 1)
                    def _():
                        pump()

                def to_mine(lo, size, val):
                    mine[:, lo : lo + size] = val

                compute(2 * d + c, to_mine)

            finish(jnp.int32(nc - 2 if nc > 1 else 0))
            for i in (nc - 2, nc - 1):
                sent(stage.at[0], R.rb_s.at[u.i, (i + nc - 1) % nc])

        def rs_via(u):
            for i, (src, mid, dst) in enumerate(merges):

                @when(z == mid)
                def _():
                    box = u.slot(jnp.int32(dst))
                    arrived(u.vr.at[i], R.rv_r.at[u.i, i])

                    def add(tmp):
                        local_now(u.vr.at[i], tmp)

                        @row_loop(*u.shape)
                        def _(rows):
                            box[rows, :] = (
                                box[rows, :].astype(F32) + tmp[rows].astype(F32)
                            ).astype(BF)

                    pl.run_scoped(add, pltpu.VMEM(u.shape, BF))
                    remote(
                        box, u.zr.at[mid], R.rz_s.at[u.i, dst], R.rz_r.at[u.i, mid], dp_of(dst), t
                    ).start()

        def rs_final(u):
            def add(tmp, total):
                for k in range(1, nc):
                    s = chip(k)

                    @when(jnp.logical_not(rs_merged(s, z)))
                    def _():
                        arrived(u.zr.at[s], R.rz_r.at[u.i, s])
                        local(u.zr.at[s], tmp.at[k - 1], 16 + k)

                box = u.slot(z)

                @row_loop(*u.shape)
                def _(rows):
                    total[rows] = box[rows, :].astype(F32)

                for k in range(1, nc):
                    s = chip(k)

                    @when(jnp.logical_not(rs_merged(s, z)))
                    def _():
                        pltpu.make_async_copy(u.zr.at[s], tmp.at[k - 1], R.loc.at[16 + k]).wait()

                        @row_loop(*u.shape)
                        def _(rows):
                            total[rows] += tmp[k - 1, rows].astype(F32)

                local_now(total, u.red)

            pl.run_scoped(
                add, pltpu.VMEM((nc - 1,) + u.shape, BF), pltpu.VMEM(u.shape, F32)
            )

        def rs_drain(u):
            for k in range(1, nc):
                sent(u.slot(z), R.rz_s.at[u.i, chip(k)])

        def x_send(ph, k, src, dst):
            remote(src, dst, R.x_s.at[ph, k], R.x_r.at[ph, k], dpi, peer(k)).start()

        acc, xs, xr = R.acc, R.xs, R.xr
        steps = ((2, 0, 2, 1), (2, 1, 2, 2), (0, 0, 0, 1), (1, 1, 1, 2), (1, 0, 1, 2), (0, 1, 0, 1))

        def half_of(buf, slot, h):
            return buf.at[slot, pl.ds(h * hr, hr)]

        def step_send(ph, i):
            a, h, b, k = steps[i]
            remote(
                half_of(xs, a, h),
                half_of(xr, b, h),
                R.x_s.at[ph, i],
                R.x_r.at[ph, i],
                dpi,
                peer(k),
            ).start()

        def partial_rows(ph, product):
            if ph > 0:
                xs_sent(ph - 1)

            @pl.loop(0, tpn)
            def _(i):
                k = lax.rem(3 * (i + 1), 4) if square else lax.rem(i + 1, tpn)
                value = product(rows_of(peer(k), sr))

                @when(k > 0)
                def _():
                    xs[k - 1] = value.astype(BF)

                @when(k == 0)
                def _():
                    acc[...] = value

                if square:
                    for j, first in ((3, (0, 1)), (1, (2,)), (2, (3,))):

                        @when(k == j)
                        def _():
                            for m in first:
                                step_send(ph, m)
                else:

                    @when(k > 0)
                    def _():
                        x_send(ph, k, xs.at[k - 1], xr.at[k - 1])

        def sum_relay(ph):
            if not square:
                return
            for i, (slot, h) in ((0, (1, 0)), (1, (0, 1))):
                arrived(half_of(xr, 2, h), R.x_r.at[ph, i])
                rows = pl.ds(h * hr, hr)
                xs[slot, rows] = (xs[slot, rows].astype(F32) + xr[2, rows].astype(F32)).astype(BF)
                step_send(ph, 4 + i)

        def sum_arrived(ph):
            if square:
                for i in range(2, 6):
                    arrived(half_of(xr, 0, 0), R.x_r.at[ph, i])
            else:
                for k in range(1, tpn):
                    arrived(xr.at[k - 1], R.x_r.at[ph, k])

        def xs_sent(ph):
            if square:
                for i in range(6):
                    sent(half_of(xs, 0, 0), R.x_s.at[ph, i])
            else:
                for k in range(1, tpn):
                    sent(xs.at[k - 1], R.x_s.at[ph, k])

        def add_peers(rows):
            total = acc[rows]
            for k in range(2 if square else tpn - 1):
                total = total + xr[k, rows].astype(F32)
            return total

        def some_rows(buf, k, h):
            return buf.at[pl.ds(pl.multiple_of(source(k) * sr + h * hr, hr), hr)]

        def rows_copy(ph, buf, i, k, h, to):
            rows = some_rows(buf, k, h)
            return remote(rows, rows, R.g_s.at[ph, i], R.g_r.at[ph, i], dpi, peer(to))

        def rows_gather(ph, buf):
            if square:
                for i, (h, to) in enumerate(((0, 1), (1, 1), (1, 2), (0, 2))):
                    rows_copy(ph, buf, i, 0, h, to).start()
            else:
                mine = buf.at[own_rows]
                for k in range(1, tpn):
                    remote(mine, mine, R.g_s.at[ph, k], R.g_r.at[ph, k], dpi, peer(k)).start()

        def rows_relay(ph, buf):
            if square:
                arrived(some_rows(buf, 1, 0), R.g_r.at[ph, 0])
                rows_copy(ph, buf, 4, 1, 0, 2).start()
                arrived(some_rows(buf, 2, 1), R.g_r.at[ph, 2])
                rows_copy(ph, buf, 5, 2, 1, 1).start()

        def rows_arrived(ph, buf, k):
            if square:
                for j, h, i in ((1, 1, 1), (2, 0, 3), (3, 0, 4), (3, 1, 5)):

                    @when(k == j)
                    def _():
                        arrived(some_rows(buf, j, h), R.g_r.at[ph, i])
            else:

                @when(k > 0)
                def _():
                    arrived(buf.at[rows_of(source(k), sr)], R.g_r.at[ph, k])

            return rows_of(source(k), sr)

        def rows_sent(ph, buf):
            if square:
                for i in range(6):
                    sent(some_rows(buf, 0, 0), R.g_s.at[ph, i])
            else:
                for k in range(1, tpn):
                    sent(buf.at[own_rows], R.g_s.at[ph, k])

        def prepare(fq, fo, fg, fd, bq, bo, bg, bd):
            loads = [local(R.wq_f, fq, 8), local(R.wo_f, fo, 9)]
            loads += [local(R.wgu_f.at[:, h], fg.at[h], 10 + h) for h in range(2)]
            loads.append(local(R.wd_f, fd, 12))
            loads[0].wait()
            for m in range(3):
                bq[:, m * wl : (m + 1) * wl] = fq[m].astype(BF)
            local_now(bq, R.wq_s)
            all_here()
            ag_near(QKV)
            for cp in loads[1:]:
                cp.wait()
            bo[...] = fo[...].astype(BF)
            for h in range(2):
                bg[:, h * fl : (h + 1) * fl] = fg[h].astype(BF)
            bd[...] = fd[...].astype(BF)
            stores = [local(bo, R.wo_s, 13), local(bg, R.wgu_s, 14), local(bd, R.wd_s, 15)]
            for cp in stores:
                cp.wait()

        if cast:
            pl.run_scoped(
                prepare,
                pltpu.VMEM((3, ds, wl), F32),
                pltpu.VMEM((wl, ds), F32),
                pltpu.VMEM((2, ds, fl), F32),
                pltpu.VMEM((fl, ds), F32),
                pltpu.VMEM((ds, w3), BF),
                pltpu.VMEM((wl, ds), BF),
                pltpu.VMEM((ds, f2), BF),
                pltpu.VMEM((fl, ds), BF),
            )
        else:
            all_here()
            ag_near(QKV)

        load_x = local(R.x, R.h2, 1)
        load_y = local(R.cot, R.dt, 2)

        bs = R.bslot
        bs[z] = R.brow[...]
        for k in range(1, nc):
            remote(
                R.brow, bs.at[z], R.b_s.at[chip(k)], R.b_r.at[z], dp_of(chip(k)), t
            ).start()

        seg = jnp.broadcast_to(R.seg[...].astype(F32), (LANES, n)).T
        start = jnp.zeros((1, LANES), F32)
        lane = lax.broadcasted_iota(jnp.int32, (n, LANES), 1)
        first = jnp.zeros((n, LANES), F32)
        for v in range(4):
            here = jnp.sum(jnp.where(seg == float(v), 1.0, 0.0), axis=0, keepdims=True)
            first = jnp.where(seg == float(v), start, first)
            start = start + here
        pos = lax.broadcasted_iota(jnp.int32, (n, LANES), 0).astype(F32) - first
        angle = pos * R.freq[...]
        entry = lax.rem(lane, HD)
        cosine = jnp.cos(angle)
        sine = jnp.sin(angle)
        part = HD // 8
        R.tc[...] = jnp.where(entry < 2 * part, cosine, 1.0)
        R.ts[...] = jnp.where(entry < part, -sine, jnp.where(entry < 2 * part, sine, 0.0))
        same = seg == lane.astype(F32)
        R.kseg[...] = jnp.where(same, 1.0, 0.0).astype(BF)
        R.qseg[...] = jnp.where(same | (lane >= 4), 0.0, MASKED).astype(BF)

        lane_row = lax.broadcasted_iota(jnp.int32, (1, LANES), 1)
        def rotate(values, rows, sign):
            up = pltpu.roll(values, LANES - part, 1)
            down = pltpu.roll(values, part, 1)
            other = jnp.where(lane_row < part, up, down)
            other = jnp.where((lane_row >= HD) & (lane_row < HD + part), up, other)
            return values * R.tc[rows] + other * (R.ts[rows] * sign)

        head_mask = [
            jnp.where((lane_row >= h * HD) & (lane_row < (h + 1) * HD), 1.0, 0.0).astype(BF)
            for h in range(2)
        ]

        def gain(i):
            return R.norm[i : i + 1, :]

        def project(h1, wq):
            load_x.wait()

            @pl.loop(0, n // lt)
            def _(i):
                rows = rows_of(i, lt)
                hat, _inv = normed(R.h2[rows].astype(F32))
                h1[rows] = (hat * gain(0) + gain(1)).astype(BF)

            keep = local(h1, R.sp_h1, 1)
            ag_far(QKV)
            ag_near(OUT)
            for k in range(1, nc):
                arrived(bs.at[chip(k)], R.b_r.at[chip(k)])
            total = bs[0]
            for s in range(1, nc):
                total = total + bs[s]
            R.bsum[0] = total
            remote(R.bsum.at[0], R.bsum.at[1], R.b_s.at[nc], R.b_r.at[nc], sib, t).start()
            ag_rest(QKV)
            arrived(R.bsum.at[1], R.b_r.at[nc])
            ag_far(OUT)
            ag_near(GU0)
            ag_done(QKV)
            local_now(R.ag_q, wq)
            bias = (R.bsum[0] + R.bsum[1])[0:1]

            @pl.loop(0, n // qb)
            def _(i):
                rows = rows_of(i, qb)
                for m in range(3):
                    for lo, size in chunks(wl, 512):
                        at = m * wl + lo
                        got = dot_nn(h1[rows], wq[:, at : at + size]) + bias[:, at : at + size]
                        if m == 2:
                            R.qkv[rows, at : at + size] = got.astype(BF)
                        else:
                            for p in range(size // LANES):
                                R.qkv[rows, at + p * LANES : at + (p + 1) * LANES] = rotate(
                                    got[:, p * LANES : (p + 1) * LANES], rows, 1.0
                                ).astype(BF)

            keep.wait()

        def scores(p, i, h):
            length = (i + 1) * qb
            rows = pl.ds(i * qb, qb)
            qkv = R.qkv
            lanes = rows_of(p, LANES)
            klanes = pl.ds(pl.multiple_of(wl + p * LANES, LANES), LANES)
            keys = jnp.concatenate([qkv[0:length, klanes], R.kseg[0:length]], axis=1)
            query = qkv[rows, lanes] * head_mask[h] * jnp.asarray(scale, BF)
            s = dot_nt(keys, jnp.concatenate([query, R.qseg[rows]], axis=1))
            low = s[length - qb :]
            causal = lax.broadcasted_iota(jnp.int32, (qb, qb), 0) <= lax.broadcasted_iota(
                jnp.int32, (qb, qb), 1
            )
            low = jnp.where(causal, low, MASKED)
            s = low if i == 0 else jnp.concatenate([s[: length - qb], low], axis=0)
            return s, query

        def attend(p):
            qkv = R.qkv
            lanes = rows_of(p, LANES)
            vlanes = pl.ds(pl.multiple_of(2 * wl + p * LANES, LANES), LANES)
            vt = qkv[:, vlanes].T
            for i in range(nq):
                length = (i + 1) * qb
                outs = []
                for h in range(2):
                    s, _query = scores(p, i, h)
                    top = jnp.max(s, axis=0, keepdims=True)
                    expo = jnp.exp(s - top)
                    total = jnp.sum(expo, axis=0, keepdims=True)
                    mixed = dot_nn(vt[h * HD : (h + 1) * HD, 0:length], expo.astype(BF))
                    outs.append(mixed * (1.0 / total))
                    R.lse[p, h : h + 1, i * qb : (i + 1) * qb] = top + jnp.log(total)
                R.o[i * qb : (i + 1) * qb, lanes] = jnp.concatenate(outs, axis=0).T.astype(BF)

        pl.run_scoped(project, pltpu.VMEM((n, D), BF), pltpu.VMEM((D, w3), BF))
        mid_pair = pairs // 2

        @pl.loop(0, pairs)
        def _(p):
            @when(p == mid_pair)
            def _():
                ag_rest(OUT)
                ag_far(GU0)
                ag_near(GU1)

            attend(p)

        ag_done(OUT)

        partial_rows(0, lambda rows: dot_nn(R.o[rows], R.wo[...]))
        sum_relay(0)
        ag_rest(GU0)
        ag_far(GU1)
        ag_near(DOWN)
        sum_arrived(0)

        def norm_rows(xown):
            local_now(R.x.at[own_rows], xown)

            @pl.loop(0, sr // lt)
            def _(i):
                rows = rows_of(i, lt)
                resid = add_peers(rows) + xown[rows].astype(F32)
                acc[rows] = resid
                hat, _inv = normed(resid)
                R.h2[pl.ds(pl.multiple_of(t * sr + i * lt, lt), lt)] = (
                    hat * gain(2) + gain(3)
                ).astype(BF)

        pl.run_scoped(norm_rows, pltpu.VMEM((sr, D), BF))

        rows_gather(0, R.h2)
        local_now(acc, R.sp_r1)
        ag_done(GU0)
        rows_relay(0, R.h2)
        ag_rest(GU1)
        ag_far(DOWN)
        ag_done(GU1)

        def feed(sp):
            def first_half(at):
                def gate_up(a):
                    @pl.loop(0, tpn)
                    def _(k):
                        rows = rows_arrived(0, R.h2, k)
                        for lo, size in chunks(fl, 768):
                            g = dot_nn(R.h2[rows], R.wgu[:, lo : lo + size])
                            u = dot_nn(R.h2[rows], R.wgu[:, fl + lo : fl + lo + size])
                            sig = 1.0 / (1.0 + jnp.exp(-g))
                            act = g * sig
                            hidden = (act * u).astype(BF)
                            a[rows, lo : lo + size] = hidden
                            at[lo : lo + size, rows] = hidden.T
                            sp[rows, lo : lo + size] = (u * sig * (1.0 + g * (1.0 - sig))).astype(
                                BF
                            )
                            sp[rows, fl + lo : fl + lo + size] = act.astype(BF)

                    local_now(a, R.sp_a)

                pl.run_scoped(gate_up, pltpu.VMEM((n, fl), BF))
                load_y.wait()

                def down_grad(stage, mine):
                    def compute(j, put):
                        put(0, ds, dot_nn(at[...], R.dt[:, rows_of(j, ds)]))

                    rs_unit(RD, compute, stage, mine)

                pl.run_scoped(
                    down_grad, pltpu.VMEM((2, fl, ds), BF), pltpu.VMEM((fl, ds), F32)
                )

            pl.run_scoped(first_half, pltpu.VMEM((fl, n), BF))
            ag_rest(DOWN)
            ag_done(DOWN)

            def hidden_grad(wd):
                local_now(R.ag_d, wd)

                @pl.loop(0, n // rt)
                def _(i):
                    rows = rows_of(i, rt)
                    for lo, size in chunks(fl, 768):
                        da = dot_nt(R.dt[rows], wd[lo : lo + size])
                        sp[rows, lo : lo + size] = (
                            da * sp[rows, lo : lo + size].astype(F32)
                        ).astype(BF)
                        sp[rows, fl + lo : fl + lo + size] = (
                            da * sp[rows, fl + lo : fl + lo + size].astype(F32)
                        ).astype(BF)

            pl.run_scoped(hidden_grad, pltpu.VMEM((fl, D), BF))
            partial_rows(1, lambda rows: dot_nt(sp[rows], R.wgu[...]))
            rs_via(RD)

            def gu_grad(stage, mine):
                def compute(j, put):
                    left = R.h2[:, rows_of(j, ds)].T
                    for lo, size in chunks(f2, 1024):
                        put(lo, size, dot_nn(left, sp[:, lo : lo + size]))

                rs_unit(RGU, compute, stage, mine, lambda: sum_relay(1))

            pl.run_scoped(gu_grad, pltpu.VMEM((2, ds, f2), BF), pltpu.VMEM((ds, f2), F32))

        pl.run_scoped(feed, pltpu.VMEM((n, f2), BF))
        rows_sent(0, R.h2)
        ag_drain(GU0)
        ag_drain(GU1)
        load_h1 = local(R.sp_h1, R.h2, 6)
        load_wq = [
            local(
                R.ag_q.at[:, pl.ds(m * wl + g * gl, gl)],
                R.wgu.at[:, pl.ds(g * g3 + m * gl, gl)],
                16 + nc + 3 * g + m,
            )
            for g in range(2)
            for m in range(3)
        ]

        def norm_two(r1, yown):
            one = local(R.cot.at[own_rows], yown, 1)
            local_now(R.sp_r1, r1)
            one.wait()
            sum_arrived(1)
            R.gsum[...] = jnp.zeros_like(R.gsum)

            @pl.loop(0, sr // lt)
            def _(i):
                rows = rows_of(i, lt)
                grad = add_peers(rows)
                hat, inv = normed(r1[rows])
                out = yown[rows].astype(F32) + norm_back(grad, hat, inv, gain(2))
                acc[rows] = out
                R.dt[pl.ds(pl.multiple_of(t * sr + i * lt, lt), lt)] = out.astype(BF)
                R.gsum[2:3] += jnp.sum(grad * hat, axis=0, keepdims=True)
                R.gsum[3:4] += jnp.sum(grad, axis=0, keepdims=True)

            rows_gather(1, R.dt)
            local_now(acc, R.sp_dr1)

        pl.run_scoped(norm_two, pltpu.VMEM((sr, D), F32), pltpu.VMEM((sr, D), BF))

        load_h1.wait()
        if turned:

            @pl.loop(0, n // qb)
            def _(i):
                R.wgu[:, pl.ds(pl.multiple_of(w3 + i * qb, LANES), qb)] = R.h2[rows_of(i, qb)].T

        rows_relay(1, R.dt)

        def mlp_out(a, wd, out, own):
            local_now(R.ag_d, wd)

            @pl.loop(1, tpn + 1)
            def _(k):
                local_now(R.sp_a.at[rows_of(peer(k), sr)], a)
                value = dot_nn(a[...], wd[...])

                @when(k < tpn)
                def _():
                    out[...] = value.astype(BF)
                    local_now(out, R.mlp_p.at[k - 1])

                @when(k == tpn)
                def _():
                    own[...] = value
                    local_now(own, R.sp_mlp)

        pl.run_scoped(
            mlp_out,
            pltpu.VMEM((sr, fl), BF),
            pltpu.VMEM((fl, D), BF),
            pltpu.VMEM((sr, D), BF),
            pltpu.VMEM((sr, D), F32),
        )

        rs_via(RGU)
        rs_final(RD)
        rs_drain(RD)
        free_signal(0)

        def attention_back(dp):
            def back(do, dk, dv):
                @pl.loop(0, tpn)
                def _(k):
                    rows = rows_arrived(1, R.dt, k)
                    do[rows] = dot_nt(R.dt[rows], R.wo[...]).astype(BF)

                for k in range(1, tpn):
                    x_send(3, k, R.mlp_p.at[k - 1], R.mlp_r.at[k - 1])

                def out_grad(ot, stage, mine):
                    ot[...] = R.o[...].T

                    def compute(j, put):
                        put(0, ds, dot_nn(ot[...], R.dt[:, rows_of(j, ds)]))

                    pl.semaphore_wait(R.free.at[0], 1)
                    rs_unit(RO, compute, stage, mine)

                pl.run_scoped(
                    out_grad,
                    pltpu.VMEM((wl, n), BF),
                    pltpu.VMEM((2, wl, ds), BF),
                    pltpu.VMEM((wl, ds), F32),
                )

                rows_sent(1, R.dt)
                free_signal(1)
                for copy in load_wq:
                    copy.wait()

                def pair_back(g, own):
                    qkv = R.qkv
                    p = g * (pairs // 2) + own
                    lanes = rows_of(p, LANES)
                    klanes = pl.ds(pl.multiple_of(wl + p * LANES, LANES), LANES)
                    vlanes = pl.ds(pl.multiple_of(2 * wl + p * LANES, LANES), LANES)

                    def out_lanes(m):
                        return pl.ds(pl.multiple_of(g * g3 + m * gl + own * LANES, LANES), LANES)

                    kt = qkv[:, klanes].T
                    dk[...] = jnp.zeros_like(dk)
                    dv[...] = jnp.zeros_like(dv)
                    for i in range(nq):
                        length = (i + 1) * qb
                        rows = pl.ds(i * qb, qb)
                        pbs, dss, qms, doms, dqs = [], [], [], [], []
                        for h in range(2):
                            s, query = scores(p, i, h)
                            prob = jnp.exp(s - R.lse[p, h : h + 1, i * qb : (i + 1) * qb])
                            dom = do[rows, lanes] * head_mask[h]
                            dprob = dot_nt(qkv[0:length, vlanes], dom)
                            weighted = jnp.sum(prob * dprob, axis=0, keepdims=True)
                            dsc = (prob * (dprob - weighted)).astype(BF)
                            pbs.append(prob.astype(BF))
                            dss.append(dsc)
                            qms.append(query)
                            doms.append(dom)
                            dqs.append(dot_nn(kt[h * HD : (h + 1) * HD, 0:length], dsc))
                        dv[0:length] += dot_nn(
                            jnp.concatenate(pbs, axis=1), jnp.concatenate(doms, axis=0)
                        )
                        dk[0:length] += dot_nn(
                            jnp.concatenate(dss, axis=1), jnp.concatenate(qms, axis=0)
                        )
                        dq = jnp.concatenate(dqs, axis=0).T * scale
                        dp[rows, out_lanes(0)] = rotate(dq, rows, -1.0).astype(BF)
                    dp[:, out_lanes(1)] = rotate(dk[...], pl.ds(0, n), -1.0).astype(BF)
                    dp[:, out_lanes(2)] = dv[...].astype(BF)

                @pl.loop(0, 2)
                def _(g):
                    @pl.loop(0, pairs // 2)
                    def _(own):
                        pair_back(g, own)

                    @when(g == 0)
                    def _():
                        rs_via(RO)
                        pl.semaphore_wait(R.free.at[1], 1)

                    @when(g == 1)
                    def _():
                        rs_via(RQ(0))

                    def qkv_grad(stage, mine):
                        def compute(j, put):
                            if turned:
                                left = R.wgu[rows_of(j, ds), w3 : w3 + n]
                            else:
                                left = R.h2[:, rows_of(j, ds)].T
                            put(0, g3, dot_nn(left, dp[:, rows_of(g, g3)]))

                        rs_unit(RQ(g), compute, stage, mine)

                    pl.run_scoped(qkv_grad, pltpu.VMEM((2, ds, g3), BF), pltpu.VMEM((ds, g3), F32))

            pl.run_scoped(
                back,
                pltpu.VMEM((n, wl), BF),
                pltpu.VMEM((n, LANES), F32),
                pltpu.VMEM((n, LANES), F32),
            )
            sums = jnp.zeros((1, w3), F32)
            for i in range(n // qb):
                sums = sums + jnp.sum(
                    dp[i * qb : (i + 1) * qb].astype(F32), axis=0, keepdims=True
                )
            R.gbs[0] = jnp.broadcast_to(sums, (8, w3))
            remote(R.gbs.at[0], R.gbs.at[1], R.c_s.at[nc], R.c_r.at[nc], sib, t).start()

            partial_rows(2, lambda rows: dot_nt(dp[rows], R.wgu[:, 0:w3]))

        pl.run_scoped(attention_back, pltpu.VMEM((n, w3), BF))

        arrived(R.gbs.at[1], R.c_r.at[nc])
        cslot = R.cslot
        cslot[z] = R.gbs[0] + R.gbs[1]
        for k in range(1, nc):
            remote(
                cslot.at[z], cslot.at[z], R.c_s.at[chip(k)], R.c_r.at[z], dp_of(chip(k)), t
            ).start()

        sum_relay(2)

        def block_rows(r1, own, got, out):
            a = local(R.sp_r1, r1, 1)
            b = local(R.sp_mlp, own, 2)
            for k in range(1, tpn):
                arrived(R.mlp_r.at[k - 1], R.x_r.at[3, k])
            local_now(R.mlp_r, got)
            a.wait()
            b.wait()

            @pl.loop(0, sr // lt)
            def _(i):
                rows = rows_of(i, lt)
                total = own[rows]
                for k in range(1, tpn):
                    total = total + got[k - 1, rows].astype(F32)
                out[rows] = (r1[rows] + total).astype(BF)

            local_now(out, R.block_out)

        pl.run_scoped(
            block_rows,
            pltpu.VMEM((sr, D), F32),
            pltpu.VMEM((sr, D), F32),
            pltpu.VMEM((tpn - 1, sr, D), BF),
            pltpu.VMEM((sr, D), BF),
        )

        rs_via(RQ(1))
        rs_final(RO)
        rs_final(RGU)

        def norm_one(dr1, xown):
            one = local(R.x.at[own_rows], xown, 1)
            local_now(R.sp_dr1, dr1)
            one.wait()
            sum_arrived(2)

            @pl.loop(0, sr // lt)
            def _(i):
                rows = rows_of(i, lt)
                grad = add_peers(rows)
                hat, inv = normed(xown[rows].astype(F32))
                dr1[rows] = dr1[rows] + norm_back(grad, hat, inv, gain(0))
                R.gsum[0:1] += jnp.sum(grad * hat, axis=0, keepdims=True)
                R.gsum[1:2] += jnp.sum(grad, axis=0, keepdims=True)

            keep = local(dr1, R.input_grad, 1)
            ns = R.nsum
            ns[0, 0:4] = R.gsum[0:4, 0 : D // 2]
            ns[0, 4:8] = R.gsum[0:4, D // 2 :]
            remote(ns.at[0], ns.at[1], R.n_s.at[0], R.n_r.at[0], sib, t).start()
            arrived(ns.at[1], R.n_r.at[0])
            zs = R.nz
            zs[z] = ns[0] + ns[1]
            for k in range(1, nc):
                remote(
                    zs.at[z], zs.at[z], R.n_s.at[k], R.n_r.at[1 + z], dp_of(chip(k)), t
                ).start()
            for k in range(1, nc):
                arrived(zs.at[chip(k)], R.n_r.at[1 + chip(k)])
            total = zs[0]
            for s in range(1, nc):
                total = total + zs[s]
            ts = R.nt
            ts[t] = total
            for k in range(1, tpn):
                remote(
                    ts.at[t], ts.at[t], R.n_s.at[nc + k], R.n_r.at[1 + nc + t], dpi, peer(k)
                ).start()
            for k in range(1, tpn):
                arrived(ts.at[peer(k)], R.n_r.at[1 + nc + peer(k)])
            total = ts[0]
            for s in range(1, tpn):
                total = total + ts[s]
            R.gn[...] = total
            keep.wait()

        pl.run_scoped(norm_one, pltpu.VMEM((sr, D), F32), pltpu.VMEM((sr, D), BF))

        for k in range(1, nc):
            arrived(cslot.at[chip(k)], R.c_r.at[chip(k)])
        total = cslot[0]
        for s in range(1, nc):
            total = total + cslot[s]
        R.gb[...] = total

        for g in range(2):
            rs_final(RQ(g))

        for u in (QKV, OUT, GU0, GU1, DOWN):
            ag_sent(u)
        for u in (QKV, OUT, DOWN):
            ag_drain(u)
        for u in (RGU, RO, RQ(0), RQ(1)):
            rs_drain(u)
        xs_sent(2)
        for k in range(1, tpn):
            sent(R.mlp_p.at[k - 1], R.x_s.at[3, k])
            sent(R.nt.at[0], R.n_s.at[nc + k])
        for k in range(1, nc):
            sent(R.brow, R.b_s.at[chip(k)])
            sent(cslot.at[0], R.c_s.at[chip(k)])
            sent(R.nz.at[0], R.n_s.at[k])
        sent(R.bsum.at[0], R.b_s.at[nc])
        sent(R.gbs.at[0], R.c_s.at[nc])
        sent(R.nsum.at[0], R.n_s.at[0])

    return kern


def fused(x, seg, cot, norm, brow, freq, weights, dpn, tpn, cast):
    n = x.shape[0]
    wl = weights[1].shape[0]
    fl = weights[3].shape[0]
    nc = dpn // 2
    ds = D // dpn
    sr = n // tpn
    w3, f2 = 3 * wl, 2 * fl
    pairs = wl // LANES
    g3 = 3 * (wl // 2)
    hbm = pl.BlockSpec(memory_space=pl.ANY)
    vmem = pl.BlockSpec(memory_space=pltpu.VMEM)
    ins = [
        ("x", hbm),
        ("seg", vmem),
        ("cot", hbm),
        ("norm", vmem),
        ("brow", vmem),
        ("freq", vmem),
    ]
    shards = ["wq_s", "wo_s", "wgu_s", "wd_s"]
    ins += [(i, hbm) for i in (["wq_f", "wo_f", "wgu_f", "wd_f"] if cast else shards)]
    boxes = [(fl, ds), (ds, f2), (wl, ds)]
    outs = [
        ("block_out", (sr, D), BF, hbm),
        ("input_grad", (sr, D), F32, hbm),
        ("gn", (8, D // 2), F32, vmem),
        ("gb", (8, w3), F32, vmem),
    ]
    outs += [("red%d" % u, s, F32, hbm) for u, s in enumerate(boxes)]
    outs += [("redq", (2, ds, g3), F32, hbm)]
    if cast:
        sizes = [(ds, w3), (wl, ds), (ds, f2), (fl, ds)]
        outs += [(i, s, BF, hbm) for i, s in zip(shards, sizes, strict=True)]
    outs += [("zrq", (2, nc, ds, g3), BF, hbm), ("vrq", (2, 2, ds, g3), BF, hbm)]
    outs += [
        ("ag_q", (D, w3), BF, hbm),
        ("ag_d", (fl, D), BF, hbm),
        ("mlp_p", (tpn - 1, sr, D), BF, hbm),
        ("mlp_r", (tpn - 1, sr, D), BF, hbm),
        ("sp_h1", (n, D), BF, hbm),
        ("sp_a", (n, fl), BF, hbm),
        ("sp_r1", (sr, D), F32, hbm),
        ("sp_mlp", (sr, D), F32, hbm),
        ("sp_dr1", (sr, D), F32, hbm),
    ]
    outs += [("zr%d" % u, (nc,) + s, BF, hbm) for u, s in enumerate(boxes)]
    outs += [("vr%d" % u, (2,) + s, BF, hbm) for u, s in enumerate(boxes)]
    dma = pltpu.SemaphoreType.DMA
    scratch = [
        ("wgu", pltpu.VMEM((D, f2), BF)),
        ("wo", pltpu.VMEM((wl, D), BF)),
        ("h2", pltpu.VMEM((n, D), BF)),
        ("dt", pltpu.VMEM((n, D), BF)),
        ("xs", pltpu.VMEM((tpn - 1, sr, D), BF)),
        ("xr", pltpu.VMEM((tpn - 1, sr, D), BF)),
        ("acc", pltpu.VMEM((sr, D), F32)),
        ("qkv", pltpu.VMEM((n, w3), BF)),
        ("o", pltpu.VMEM((n, wl), BF)),
        ("tc", pltpu.VMEM((n, LANES), F32)),
        ("ts", pltpu.VMEM((n, LANES), F32)),
        ("kseg", pltpu.VMEM((n, LANES), BF)),
        ("qseg", pltpu.VMEM((n, LANES), BF)),
        ("lse", pltpu.VMEM((pairs, 2, n), F32)),
        ("bslot", pltpu.VMEM((nc, 8, w3), F32)),
        ("bsum", pltpu.VMEM((2, 8, w3), F32)),
        ("gbs", pltpu.VMEM((2, 8, w3), F32)),
        ("cslot", pltpu.VMEM((nc, 8, w3), F32)),
        ("gsum", pltpu.VMEM((8, D), F32)),
        ("nsum", pltpu.VMEM((2, 8, D // 2), F32)),
        ("nz", pltpu.VMEM((nc, 8, D // 2), F32)),
        ("nt", pltpu.VMEM((tpn, 8, D // 2), F32)),
    ]
    scratch += [("box%d" % u, pltpu.VMEM((nc,) + boxes[u], BF)) for u in range(2)]
    scratch += [
        ("dum", dma((1,))),
        ("loc", dma((27 + nc,))),
        ("free", pltpu.SemaphoreType.REGULAR((2,))),
        ("ag_s", dma((5, nc))),
        ("ag_r", dma((5, nc))),
        ("av_s", dma((5, 2))),
        ("sb_s", dma((5, nc))),
        ("sb_r", dma((5, nc))),
        ("rb_s", dma((5, nc))),
        ("rb_r", dma((5, nc))),
        ("rz_s", dma((5, nc))),
        ("rz_r", dma((5, nc))),
        ("rv_r", dma((5, 2))),
        ("x_s", dma((4, max(tpn, 6)))),
        ("x_r", dma((4, max(tpn, 6)))),
        ("g_s", dma((2, max(tpn, 6)))),
        ("g_r", dma((2, max(tpn, 6)))),
        ("b_s", dma((nc + 1,))),
        ("b_r", dma((nc + 1,))),
        ("c_s", dma((nc + 1,))),
        ("c_r", dma((nc + 1,))),
        ("n_s", dma((nc + tpn,))),
        ("n_r", dma((1 + nc + tpn,))),
    ]
    names = [i[0] for i in ins] + [o[0] for o in outs] + [s[0] for s in scratch]
    got = pl.pallas_call(
        make_kernel(names, n, wl, fl, dpn, tpn, cast),
        out_shape=[jax.ShapeDtypeStruct(s, d) for _, s, d, _ in outs],
        in_specs=[s for _, s in ins],
        out_specs=[m for _, _, _, m in outs],
        scratch_shapes=[s for _, s in scratch],
        compiler_params=pltpu.CompilerParams(
            collective_id=0, has_side_effects=True, vmem_limit_bytes=63 * 2**20
        ),
        name="block_step",
    )(x, seg, cot, norm, brow, freq, *weights)
    return got[:8]


def adamw(weight, first, second, grad, rate, decay):
    new_first = BETA_ONE * first + (1.0 - BETA_ONE) * grad
    new_second = BETA_TWO * second + (1.0 - BETA_TWO) * grad * grad
    direction = (
        new_first
        / (1.0 - BETA_ONE**STEP)
        / (jnp.sqrt(new_second / (1.0 - BETA_TWO**STEP)) + ADAM_EPS)
    )
    return (new_first, new_second, weight - rate * (direction + decay * weight))


def update_all(groups):
    hbm = pl.BlockSpec(memory_space=pl.ANY)
    f32 = lambda s: pltpu.VMEM(s, F32)
    n_groups = len(groups)
    scratch = []
    for grad, weight, _, _, pieces, _ in groups:
        scratch.append(f32(grad.shape))
        scratch += [f32((len(pieces),) + pieces[0][2])] * 3
    count = sum(1 + 6 * len(g[4]) for g in groups)

    def kern(*refs):
        ins, outs = refs[: 4 * n_groups], refs[4 * n_groups : 7 * n_groups]
        bufs, sem = refs[7 * n_groups : -1], refs[-1]
        at = iter(range(count))
        loads, plan = [], []

        def start(src, dst):
            cp = pltpu.make_async_copy(src, dst, sem.at[next(at)])
            cp.start()
            return cp

        for i, (_, _, _, _, pieces, rate) in enumerate(groups):
            g, *state = bufs[4 * i : 4 * i + 4]
            got = [start(ins[4 * i], g)]
            for j, (_, state_part, _) in enumerate(pieces):
                for k in range(3):
                    got.append(start(state_part(ins[4 * i + 1 + k]), state[k].at[j]))
            plan.append((got, g, state, pieces, rate, outs[3 * i : 3 * i + 3]))
        stores = []
        for got, g, state, pieces, rate, dst in plan:
            for cp in got:
                cp.wait()
            for j, (grad_part, state_part, (rows, cols)) in enumerate(pieces):
                step = 64 if cols <= 512 else 16
                gv = grad_part(g)
                w, m, v = (x.at[j] for x in state)

                @pl.loop(0, rows // step)
                def _(r):
                    at_rows = pl.ds(pl.multiple_of(r * step, step), step)
                    grad = gv[at_rows, :]
                    first, second, new = adamw(
                        w[at_rows, :], m[at_rows, :], v[at_rows, :], grad, rate, DECAY
                    )
                    m[at_rows, :] = first
                    v[at_rows, :] = second
                    w[at_rows, :] = new

                for k, buf in enumerate((m, v, w)):
                    stores.append(start(buf, state_part(dst[k])))
        for cp in stores:
            cp.wait()

    out_shape = []
    flat = []
    for grad, weight, first, second, _, _ in groups:
        flat += [grad, weight, first, second]
        out_shape += [jax.ShapeDtypeStruct(weight.shape, F32)] * 3
    got = pl.pallas_call(
        kern,
        out_shape=out_shape,
        in_specs=[hbm] * len(flat),
        out_specs=[hbm] * len(out_shape),
        scratch_shapes=scratch + [pltpu.SemaphoreType.DMA((count,))],
        compiler_params=pltpu.CompilerParams(vmem_limit_bytes=56 * 2**20),
        name="adamw",
    )(*flat)
    return [tuple(got[3 * i : 3 * i + 3]) for i in range(n_groups)]


def body(
    tokens,
    segments,
    cotangent,
    norm_params,
    norm_m,
    norm_v,
    qkv_bias,
    bias_m,
    bias_v,
    w_qkv,
    qkv_m,
    qkv_v,
    w_out,
    out_m,
    out_v,
    w_gateup,
    gateup_m,
    gateup_v,
    w_down,
    down_m,
    down_v,
):
    n_rows, model = tokens.shape
    dpn = lax.axis_size("dp")
    tpn = lax.axis_size("tensor")
    ds, _, wl = w_qkv.shape
    fl = w_down.shape[0]
    pad = -fl % LANES
    heads, cut = qkv_bias.shape[1:]
    assert segments.shape[0] == 1 and model == D
    me = lax.axis_index("dp")

    bias = qkv_bias.astype(BF).astype(F32)
    wide = lax.dynamic_update_slice(jnp.zeros((3, heads, HD), F32), bias, (0, 0, me * cut))
    brow = jnp.broadcast_to(wide.reshape(1, 3 * wl), (8, 3 * wl))
    part = HD // 8
    freq = ROPE_BASE ** (-2.0 * (np.arange(LANES) % part) / (HD // 4))
    freq = jnp.asarray(freq.reshape(1, LANES), F32)
    cast = not pad
    if cast:
        weights = (jnp.transpose(w_qkv, (1, 0, 2)), w_out, w_gateup, w_down)
    else:
        wgu = jnp.pad(w_gateup.astype(BF), ((0, 0), (0, 0), (0, pad)))
        weights = (
            w_qkv.astype(BF).reshape(ds, 3 * wl),
            w_out.astype(BF),
            wgu.reshape(ds, 2 * (fl + pad)),
            jnp.pad(w_down.astype(BF), ((0, pad), (0, 0))),
        )
    block_out, input_grad, gn, gb, red_down, red_gu, red_out, red_qkv = fused(
        tokens, segments, cotangent, norm_params, brow, freq, weights, dpn, tpn, cast
    )
    norm_grad = jnp.concatenate([gn[:4], gn[4:]], axis=1)
    red_bias = jnp.swapaxes(gb[0].reshape(2, 3, wl // 2), 0, 1).reshape(3, heads, HD)
    red_bias = lax.dynamic_slice(red_bias, (0, 0, me * cut), (3, heads, cut))
    gl = wl // 2

    def lanes(ref, lo, size):
        return ref.at[:, pl.ds(lo, size)]

    qkv_pieces = [
        (
            lambda r, g=g, m=m: r.at[g, :, pl.ds(m * gl, gl)],
            lambda r, g=g, m=m: r.at[m, :, pl.ds(g * gl, gl)],
            (ds, gl),
        )
        for g in range(2)
        for m in range(3)
    ]
    whole = lambda r: r

    def turn(x):
        return jnp.transpose(x, (1, 0, 2))

    groups = [
        (red_qkv, turn(w_qkv), turn(qkv_m), turn(qkv_v), qkv_pieces, D ** (-0.5)),
        (red_out, w_out, out_m, out_v, [(whole, whole, w_out.shape)], HD ** (-0.5)),
    ]
    if not pad:
        gu_pieces = [
            (lambda r, h=h: lanes(r, h * fl, fl), lambda r, h=h: r.at[:, h], (ds, fl))
            for h in range(2)
        ]
        groups += [
            (red_gu, w_gateup, gateup_m, gateup_v, gu_pieces, D ** (-0.5)),
            (red_down, w_down, down_m, down_v, [(whole, whole, w_down.shape)], FF ** (-0.5)),
        ]
    done = update_all(groups)
    new_qkv = tuple(turn(x) for x in done[0])
    if pad:
        red_gu = red_gu.reshape(ds, 2, fl + pad)[:, :, :fl]
        red_down = red_down[:fl]
        done += [
            adamw(w_gateup, gateup_m, gateup_v, red_gu, D ** (-0.5), DECAY),
            adamw(w_down, down_m, down_v, red_down, FF ** (-0.5), DECAY),
        ]
    return (
        (block_out, input_grad)
        + adamw(norm_params, norm_m, norm_v, norm_grad, 0.5, 0.0)
        + adamw(qkv_bias, bias_m, bias_v, red_bias, 0.3, 0.0)
        + new_qkv
        + done[1]
        + done[2]
        + done[3]
    )


def solution(mesh):
    rows = P("dp", None)
    bias = P(None, "tensor", "dp")
    wide = P("dp", None, "tensor")
    tall = P("tensor", "dp")
    split = P(("dp", "tensor"), None)
    return jax.shard_map(
        body,
        mesh=mesh,
        in_specs=(rows,) * 3 + (P(),) * 3 + (bias,) * 3 + (wide,) * 3 + (tall,) * 3 + (wide,) * 3
        + (tall,) * 3,
        out_specs=(split,) * 2 + (P(),) * 3 + (bias,) * 3 + (wide,) * 3 + (tall,) * 3 + (wide,) * 3
        + (tall,) * 3,
        check_vma=False,
    )
```

```python
from types import SimpleNamespace

import numpy as np
import jax
import jax.numpy as jnp
from jax import lax
from jax.experimental import pallas as pl
from jax.experimental.pallas import tpu as pltpu
from jax.sharding import PartitionSpec as P

D = 2048
HD = 64
FF = 5632
STEP = 10

NORM_EPS = 1e-05
BETA_ONE = 0.9
BETA_TWO = 0.95
ADAM_EPS = 1e-08
DECAY = 0.1
ROPE_BASE = 10000.0

BF = jnp.bfloat16
F32 = jnp.float32
MESH = pl.DeviceIdType.MESH
LANES = 128
MASKED = -1e30

QKV, OUT, GU0, GU1, DOWN = range(5)


def dot_nn(a, b):
    return lax.dot_general(a, b, (((1,), (0,)), ((), ())), preferred_element_type=F32)


def dot_nt(a, b):
    return lax.dot_general(a, b, (((1,), (1,)), ((), ())), preferred_element_type=F32)


def dot_tn(a, b):
    return lax.dot_general(a, b, (((0,), (0,)), ((), ())), preferred_element_type=F32)


def chunks(total, step):
    return [(lo, min(step, total - lo)) for lo in range(0, total, step)]


def normed(values):
    centre = values - jnp.mean(values, axis=1, keepdims=True)
    inv = lax.rsqrt(jnp.mean(centre * centre, axis=1, keepdims=True) + NORM_EPS)
    return centre * inv, inv


def norm_back(grad, hat, inv, gain):
    e = grad * gain
    return inv * (
        e - jnp.mean(e, axis=1, keepdims=True) - hat * jnp.mean(e * hat, axis=1, keepdims=True)
    )


def make_kernel(names, n, wl, fl, dpn, tpn, cast):
    nc = dpn // 2
    ds = D // dpn
    sr = n // tpn
    w3 = 3 * wl
    f2 = 2 * fl
    half = ds // 2
    qb = min(256, n)
    nq = n // qb
    rt = min(256, sr)
    lt = min(128, sr)
    pairs = wl // LANES
    gl = wl // 2
    g3 = 3 * gl
    hr = sr // 2
    square = tpn == 4
    turned = w3 + n <= f2
    scale = HD ** (-0.5)
    has_via = nc >= 3

    def kern(*refs):
        R = SimpleNamespace(**dict(zip(names, refs, strict=True)))
        dpi = lax.axis_index("dp")
        t = lax.axis_index("tensor")
        z = lax.div(dpi, 2)
        c = lax.rem(dpi, 2)
        oc = 1 - c
        sib = dpi + 1 - 2 * c

        def chip(k):
            return lax.rem(z + k, nc)

        def dp_of(s):
            return 2 * s + c

        def flip(i, k):
            return lax.rem(i + k, 2) + 2 * lax.rem(lax.div(i, 2) + lax.div(k, 2), 2)

        def peer(k):
            k = jnp.asarray(k, jnp.int32)
            return flip(t, k) if square else lax.rem(t + k, tpn)

        def source(k):
            k = jnp.asarray(k, jnp.int32)
            return flip(t, k) if square else lax.rem(t + tpn - k, tpn)

        def remote(src, dst, ss, rs, dp, tn):
            return pltpu.make_async_remote_copy(
                src_ref=src,
                dst_ref=dst,
                send_sem=ss,
                recv_sem=rs,
                device_id=(dp, tn),
                device_id_type=MESH,
            )

        def arrived(dst, rs):
            remote(dst, dst, R.dum.at[0], rs, sib, t).wait_recv()

        def sent(src, ss):
            remote(src, src, ss, R.dum.at[0], sib, t).wait_send()

        def local(src, dst, i):
            cp = pltpu.make_async_copy(src, dst, R.loc.at[i])
            cp.start()
            return cp

        def local_now(src, dst):
            local(src, dst, 0).wait()

        def rows_of(i, size):
            return pl.ds(pl.multiple_of(i * size, size), size)

        own_rows = rows_of(t, sr)

        bar = pltpu.get_barrier_semaphore()
        pl.semaphore_signal(bar, inc=1, device_id=(sib, t), device_id_type=MESH)
        for k in range(1, nc):
            pl.semaphore_signal(bar, inc=1, device_id=(dp_of(chip(k)), t), device_id_type=MESH)
        for k in range(1, tpn):
            pl.semaphore_signal(bar, inc=1, device_id=(dpi, peer(k)), device_id_type=MESH)

        def all_here():
            pl.semaphore_wait(bar, 1 + (nc - 1) + (tpn - 1))

        def shard(u):
            if cast:
                return place(u, dpi)
            return {
                QKV: lambda: R.wq_s,
                OUT: lambda: R.wo_s,
                GU0: lambda: R.wgu_s.at[pl.ds(0, half)],
                GU1: lambda: R.wgu_s.at[pl.ds(half, half)],
                DOWN: lambda: R.wd_s,
            }[u]()

        def place(u, j):
            return {
                QKV: lambda: R.ag_q.at[rows_of(j, ds)],
                OUT: lambda: R.wo.at[:, rows_of(j, ds)],
                GU0: lambda: R.wgu.at[pl.ds(pl.multiple_of(j * ds, ds), half)],
                GU1: lambda: R.wgu.at[pl.ds(pl.multiple_of(j * ds + half, half), half)],
                DOWN: lambda: R.ag_d.at[:, rows_of(j, ds)],
            }[u]()

        def relayed(src, dst):
            if not has_via:
                return src != src
            return ((src == 2) & (dst == 0)) | ((src == nc - 3) & (dst == nc - 1))

        def when(cond):
            return pl.when(cond)

        def within(s):
            return (s >= 0) & (s < nc)

        def apart(s):
            return (s - z >= 2) | (z - s >= 2)

        relays = ((1, 2, 0), (nc - 2, nc - 3, nc - 1)) if has_via else ()

        def ag_copy(u, d):
            return remote(
                shard(u), place(u, dpi), R.ag_s.at[u, d], R.ag_r.at[u, z], dp_of(d), t
            )

        def ag_near(u):
            for d in (z + 1, z - 1):

                @when(within(d))
                def _():
                    ag_copy(u, d).start()

            remote(shard(u), place(u, dpi), R.sb_s.at[u, z], R.sb_r.at[u, z], sib, t).start()
            if not cast:
                local(shard(u), place(u, dpi), 22 + nc + u)

        def to_sibling(u, s):
            here = place(u, dp_of(s))
            remote(here, here, R.sb_s.at[u, s], R.sb_r.at[u, s], sib, t).start()

        def ag_far(u):
            for s in (z + 1, z - 1):

                @when(within(s))
                def _():
                    arrived(place(u, dp_of(s)), R.ag_r.at[u, s])

            for i, (mid, src, dst) in enumerate(relays):

                @when(z == mid)
                def _():
                    here = place(u, dp_of(src))
                    remote(
                        here, here, R.av_s.at[u, i], R.ag_r.at[u, src], dp_of(dst), t
                    ).start()

            for d in range(nc):

                @when(apart(d) & jnp.logical_not(relayed(z, d)))
                def _():
                    ag_copy(u, d).start()

            for s in (z + 1, z - 1):

                @when(within(s))
                def _():
                    to_sibling(u, s)

        def ag_rest(u):
            for s in range(nc):

                @when(apart(s))
                def _():
                    arrived(place(u, dp_of(s)), R.ag_r.at[u, s])
                    to_sibling(u, s)

        def ag_sent(u):
            for d in range(nc):
                far = apart(d) if u == DOWN else relayed(z, d)

                @when((z != d) & jnp.logical_not(far))
                def _():
                    sent(shard(u), R.ag_s.at[u, d])

        def ag_hop(h):
            for i, way in enumerate((1, -1)):
                s = z + way * h

                @when(within(s))
                def _():
                    here = place(DOWN, dp_of(s))
                    arrived(here, R.ag_r.at[DOWN, s])

                    @when(within(z - way))
                    def _():
                        remote(
                            here, here, R.hop.at[h, i], R.ag_r.at[DOWN, s], dp_of(z - way), t
                        ).start()

                    to_sibling(DOWN, s)

        def ag_hops_sent():
            for h in range(1, nc - 1):
                for i, way in enumerate((1, -1)):

                    @when(within(z + way * h) & within(z - way))
                    def _():
                        sent(place(DOWN, dpi), R.hop.at[h, i])

        def ag_done(u):
            if not cast:
                pltpu.make_async_copy(shard(u), place(u, dpi), R.loc.at[22 + nc + u]).wait()
            for s in range(nc):
                arrived(place(u, 2 * s + oc), R.sb_r.at[u, s])

        def ag_drain(u):
            for i, (mid, src, dst) in enumerate(() if u == DOWN else relays):

                @when(z == mid)
                def _():
                    sent(place(u, dp_of(src)), R.av_s.at[u, i])

            for s in range(nc):
                sent(shard(u), R.sb_s.at[u, s])

        def rs_merged(src, dst):
            if not has_via:
                return src != src
            return ((src == 0) & (dst == nc - 1)) | ((src == nc - 1) & (dst == 0))

        def rs_held(dst):
            if not has_via:
                return z != z
            return ((z == 1) & (dst == nc - 1)) | ((z == nc - 2) & (dst == 0))

        merges = ((0, 1, nc - 1), (nc - 1, nc - 2, 0)) if has_via else ()

        def unit(i, slot, zr, vr, shape):
            return SimpleNamespace(i=i, slot=slot, zr=zr, vr=vr, shape=shape)

        RD = unit(0, lambda d: R.box0.at[d], R.zr0, R.vr0, (fl, ds))
        RGU = unit(1, lambda d: R.box1.at[d], R.zr1, R.vr1, (ds, f2))
        RO = unit(2, lambda d: R.box0.at[d, pl.ds(0, wl)], R.zr2, R.vr2, (wl, ds))

        def RQ(g):
            lanes = pl.ds(g * g3, g3) if isinstance(g, int) else rows_of(g, g3)
            return unit(
                3 + g,
                lambda d: R.dt.at[rows_of(d, ds), lanes],
                R.zrq.at[g],
                R.vrq.at[g],
                (ds, g3),
            )

        def free_signal(i):
            pl.semaphore_signal(R.free.at[i], inc=1, device_id=(sib, t), device_id_type=MESH)

        def row_loop(total, cols):
            step = 128 if cols <= 512 else 16

            def over(act):
                @pl.loop(0, total // step)
                def _(i):
                    act(rows_of(i, step))

            return over

        def rs_late(u, d):
            if not has_via:
                return z != z
            return (d == 0) | (d == nc - 1) if u is RD else (z == 0) | (z == nc - 1)

        def rs_direct(u, d):
            remote(
                u.slot(d), u.zr.at[z], R.rz_s.at[u.i, d], R.rz_r.at[u.i, z], dp_of(d), t
            ).start()

        def rs_rest(u):
            for d in range(nc):

                skip = rs_held(d) | rs_merged(z, d)

                @when(rs_late(u, d) & (z != d) & jnp.logical_not(skip))
                def _():
                    rs_direct(u, jnp.int32(d))

        def rs_unit(u, compute, stage, mine, pump=None):
            def finish(d):
                box = u.slot(d)
                arrived(box, R.rb_r.at[u.i, d])

                @row_loop(*u.shape)
                def _(rows):
                    box[rows, :] = (mine[rows] + box[rows, :].astype(F32)).astype(BF)

                @when(z == d)
                def _():
                    pltpu.make_async_copy(box, u.zr.at[z], R.self.at[u.i]).start()

                skip = rs_held(d) | rs_merged(z, d) | rs_late(u, d)

                @when((z != d) & jnp.logical_not(skip))
                def _():
                    rs_direct(u, d)

                for i, (src, mid, dst) in enumerate(merges):

                    @when((z == src) & (d == dst))
                    def _():
                        remote(
                            box, u.vr.at[i], R.rz_s.at[u.i, d], R.rv_r.at[u.i, i], dp_of(mid), t
                        ).start()

            def turn(i):
                return lax.rem(i + nc - 1, nc)

            @pl.loop(0, nc)
            def _(idx):
                d = turn(idx)
                slot = lax.rem(idx, 2)

                @when(idx >= 2)
                def _():
                    sent(stage.at[slot], R.rb_s.at[u.i, turn(idx + nc - 2)])

                def to_stage(lo, size, val):
                    stage[slot, :, lo : lo + size] = val.astype(BF)

                compute(2 * d + oc, to_stage)
                remote(
                    stage.at[slot], u.slot(d), R.rb_s.at[u.i, d], R.rb_r.at[u.i, d], sib, t
                ).start()

                @when(idx >= 1)
                def _():
                    finish(turn(idx + nc - 1))

                if pump is not None:

                    @when(idx == pump[0])
                    def _():
                        pump[1]()

                def to_mine(lo, size, val):
                    mine[:, lo : lo + size] = val

                compute(2 * d + c, to_mine)

            finish(jnp.int32(nc - 2 if nc > 1 else 0))
            for i in (nc - 2, nc - 1):
                sent(stage.at[0], R.rb_s.at[u.i, (i + nc - 1) % nc])

        def rs_via(u):
            for i, (src, mid, dst) in enumerate(merges):

                @when(z == mid)
                def _():
                    box = u.slot(jnp.int32(dst))
                    arrived(u.vr.at[i], R.rv_r.at[u.i, i])

                    def add(tmp):
                        local_now(u.vr.at[i], tmp)

                        @row_loop(*u.shape)
                        def _(rows):
                            box[rows, :] = (
                                box[rows, :].astype(F32) + tmp[rows].astype(F32)
                            ).astype(BF)

                    pl.run_scoped(add, pltpu.VMEM(u.shape, BF))
                    remote(
                        box, u.zr.at[mid], R.rz_s.at[u.i, dst], R.rz_r.at[u.i, mid], dp_of(dst), t
                    ).start()

        def rs_arrived(u):
            for k in range(1, nc):
                s = chip(k)

                @when(jnp.logical_not(rs_merged(s, z)))
                def _():
                    arrived(u.zr.at[s], R.rz_r.at[u.i, s])

        def rs_drain(u):
            for k in range(1, nc):
                sent(u.slot(z), R.rz_s.at[u.i, chip(k)])
            pltpu.make_async_copy(u.slot(z), u.zr.at[z], R.self.at[u.i]).wait()

        def x_send(ph, k, src, dst):
            remote(src, dst, R.x_s.at[ph, k], R.x_r.at[ph, k], dpi, peer(k)).start()

        acc, xs, xr = R.acc, R.xs, R.xr
        steps = ((2, 0, 2, 1), (2, 1, 2, 2), (0, 0, 0, 1), (1, 1, 1, 2), (1, 0, 1, 2), (0, 1, 0, 1))

        def half_of(buf, slot, h):
            return buf.at[slot, pl.ds(h * hr, hr)]

        def step_send(ph, i):
            a, h, b, k = steps[i]
            remote(
                half_of(xs, a, h),
                half_of(xr, b, h),
                R.x_s.at[ph, i],
                R.x_r.at[ph, i],
                dpi,
                peer(k),
            ).start()

        def partial_rows(ph, product):
            if ph > 0:
                xs_sent(ph - 1)

            @pl.loop(0, tpn)
            def _(i):
                k = lax.rem(3 * (i + 1), 4) if square else lax.rem(i + 1, tpn)
                value = product(rows_of(peer(k), sr))

                @when(k > 0)
                def _():
                    xs[k - 1] = value.astype(BF)

                @when(k == 0)
                def _():
                    acc[...] = value

                if square:
                    for j, first in ((3, (0, 1)), (1, (2,)), (2, (3,))):

                        @when(k == j)
                        def _():
                            for m in first:
                                step_send(ph, m)
                else:

                    @when(k > 0)
                    def _():
                        x_send(ph, k, xs.at[k - 1], xr.at[k - 1])

        def sum_relay(ph):
            if not square:
                return
            for i, (slot, h) in ((0, (1, 0)), (1, (0, 1))):
                arrived(half_of(xr, 2, h), R.x_r.at[ph, i])
                rows = pl.ds(h * hr, hr)
                xs[slot, rows] = (xs[slot, rows].astype(F32) + xr[2, rows].astype(F32)).astype(BF)
                step_send(ph, 4 + i)

        def sum_arrived(ph):
            if square:
                for i in range(2, 6):
                    arrived(half_of(xr, 0, 0), R.x_r.at[ph, i])
            else:
                for k in range(1, tpn):
                    arrived(xr.at[k - 1], R.x_r.at[ph, k])

        def xs_sent(ph):
            if square:
                for i in range(6):
                    sent(half_of(xs, 0, 0), R.x_s.at[ph, i])
            else:
                for k in range(1, tpn):
                    sent(xs.at[k - 1], R.x_s.at[ph, k])

        def add_peers(rows):
            total = acc[rows]
            for k in range(2 if square else tpn - 1):
                total = total + xr[k, rows].astype(F32)
            return total

        def some_rows(buf, k, h):
            return buf.at[pl.ds(pl.multiple_of(source(k) * sr + h * hr, hr), hr)]

        def rows_copy(ph, buf, i, k, h, to):
            rows = some_rows(buf, k, h)
            return remote(rows, rows, R.g_s.at[ph, i], R.g_r.at[ph, i], dpi, peer(to))

        def rows_gather(ph, buf):
            if square:
                for i, (h, to) in enumerate(((0, 1), (1, 1), (1, 2), (0, 2))):
                    rows_copy(ph, buf, i, 0, h, to).start()
            else:
                mine = buf.at[own_rows]
                for k in range(1, tpn):
                    remote(mine, mine, R.g_s.at[ph, k], R.g_r.at[ph, k], dpi, peer(k)).start()

        def rows_relay(ph, buf):
            if square:
                arrived(some_rows(buf, 1, 0), R.g_r.at[ph, 0])
                rows_copy(ph, buf, 4, 1, 0, 2).start()
                arrived(some_rows(buf, 2, 1), R.g_r.at[ph, 2])
                rows_copy(ph, buf, 5, 2, 1, 1).start()

        def rows_arrived(ph, buf, k):
            if square:
                for j, h, i in ((1, 1, 1), (2, 0, 3), (3, 0, 4), (3, 1, 5)):

                    @when(k == j)
                    def _():
                        arrived(some_rows(buf, j, h), R.g_r.at[ph, i])
            else:

                @when(k > 0)
                def _():
                    arrived(buf.at[rows_of(source(k), sr)], R.g_r.at[ph, k])

            return rows_of(source(k), sr)

        def rows_sent(ph, buf):
            if square:
                for i in range(6):
                    sent(some_rows(buf, 0, 0), R.g_s.at[ph, i])
            else:
                for k in range(1, tpn):
                    sent(buf.at[own_rows], R.g_s.at[ph, k])

        def prepare(fq, fo, fg, fd, bq, bd):
            loads = [local(R.wq_f, fq, 8), local(R.wo_f, fo, 9)]
            loads += [local(R.wgu_f.at[:, h], fg.at[h], 10 + h) for h in range(2)]
            loads.append(local(R.wd_f, fd, 12))
            loads[0].wait()
            for m in range(3):
                bq[:, m * wl : (m + 1) * wl] = fq[m].astype(BF)
            local_now(bq, place(QKV, dpi))
            all_here()
            ag_near(QKV)
            for cp in loads[1:]:
                cp.wait()
            R.wo[:, rows_of(dpi, ds)] = fo[...].astype(BF)
            for h in range(2):
                R.wgu[rows_of(dpi, ds), h * fl : (h + 1) * fl] = fg[h].astype(BF)
            bd[...] = fd[...].astype(BF)
            local_now(bd, place(DOWN, dpi))

        if cast:
            pl.run_scoped(
                prepare,
                pltpu.VMEM((3, ds, wl), F32),
                pltpu.VMEM((wl, ds), F32),
                pltpu.VMEM((2, ds, fl), F32),
                pltpu.VMEM((fl, ds), F32),
                pltpu.VMEM((ds, w3), BF),
                pltpu.VMEM((fl, ds), BF),
            )
        else:
            all_here()
            ag_near(QKV)

        if has_via:

            @when((z == 0) | (z == nc - 1))
            def _():
                other = nc - 1 - z
                R.box0[0] = jnp.zeros_like(R.box0[0])
                R.box1[0] = jnp.zeros_like(R.box1[0])
                fills = [
                    local(R.box0.at[0], R.zr0.at[other], 8),
                    local(R.box1.at[0], R.zr1.at[other], 9),
                    local(R.box0.at[0, pl.ds(0, wl)], R.zr2.at[other], 10),
                ]
                for g in range(2):
                    fills.append(
                        local(R.box1.at[0, :, pl.ds(0, g3)], R.zrq.at[g, other], 11 + g)
                    )
                for cp in fills:
                    cp.wait()

        load_x = local(R.x, R.h2, 1)
        load_y = local(R.cot, R.dt, 2)

        bs = R.bslot
        bs[z] = R.brow[...]
        for k in range(1, nc):
            remote(
                R.brow, bs.at[z], R.b_s.at[chip(k)], R.b_r.at[z], dp_of(chip(k)), t
            ).start()

        seg = jnp.broadcast_to(R.seg[...].astype(F32), (LANES, n)).T
        start = jnp.zeros((1, LANES), F32)
        lane = lax.broadcasted_iota(jnp.int32, (n, LANES), 1)
        first = jnp.zeros((n, LANES), F32)
        for v in range(4):
            here = jnp.sum(jnp.where(seg == float(v), 1.0, 0.0), axis=0, keepdims=True)
            first = jnp.where(seg == float(v), start, first)
            start = start + here
        pos = lax.broadcasted_iota(jnp.int32, (n, LANES), 0).astype(F32) - first
        angle = pos * R.freq[...]
        entry = lax.rem(lane, HD)
        cosine = jnp.cos(angle)
        sine = jnp.sin(angle)
        part = HD // 8
        R.tc[...] = jnp.where(entry < 2 * part, cosine, 1.0)
        R.ts[...] = jnp.where(entry < part, -sine, jnp.where(entry < 2 * part, sine, 0.0))
        same = seg == lane.astype(F32)
        R.kseg[...] = jnp.where(same, 1.0, 0.0).astype(BF)
        R.qseg[...] = jnp.where(same | (lane >= 4), 0.0, MASKED).astype(BF)

        lane_row = lax.broadcasted_iota(jnp.int32, (1, LANES), 1)
        def rotate(values, rows, sign):
            up = pltpu.roll(values, LANES - part, 1)
            down = pltpu.roll(values, part, 1)
            other = jnp.where(lane_row < part, up, down)
            other = jnp.where((lane_row >= HD) & (lane_row < HD + part), up, other)
            return values * R.tc[rows] + other * (R.ts[rows] * sign)

        head_mask = [
            jnp.where((lane_row >= h * HD) & (lane_row < (h + 1) * HD), 1.0, 0.0).astype(BF)
            for h in range(2)
        ]

        def gain(i):
            return R.norm[i : i + 1, :]

        def project(h1, wq):
            load_x.wait()

            @pl.loop(0, n // lt)
            def _(i):
                rows = rows_of(i, lt)
                hat, _inv = normed(R.h2[rows].astype(F32))
                h1[rows] = (hat * gain(0) + gain(1)).astype(BF)

            keep = local(h1, R.sp_h1, 1)
            ag_far(QKV)
            ag_near(OUT)
            for k in range(1, nc):
                arrived(bs.at[chip(k)], R.b_r.at[chip(k)])
            total = bs[0]
            for s in range(1, nc):
                total = total + bs[s]
            R.bsum[0] = total
            remote(R.bsum.at[0], R.bsum.at[1], R.b_s.at[nc], R.b_r.at[nc], sib, t).start()
            ag_rest(QKV)
            arrived(R.bsum.at[1], R.b_r.at[nc])
            ag_far(OUT)
            ag_near(GU0)
            ag_done(QKV)
            local_now(R.ag_q, wq)
            bias = (R.bsum[0] + R.bsum[1])[0:1]

            @pl.loop(0, n // qb)
            def _(i):
                rows = rows_of(i, qb)
                for m in range(3):
                    for lo, size in chunks(wl, 512):
                        at = m * wl + lo
                        got = dot_nn(h1[rows], wq[:, at : at + size]) + bias[:, at : at + size]
                        if m == 2:
                            R.qkv[rows, at : at + size] = got.astype(BF)
                        else:
                            for p in range(size // LANES):
                                R.qkv[rows, at + p * LANES : at + (p + 1) * LANES] = rotate(
                                    got[:, p * LANES : (p + 1) * LANES], rows, 1.0
                                ).astype(BF)

            keep.wait()

        def scores(p, i, h):
            length = (i + 1) * qb
            rows = pl.ds(i * qb, qb)
            qkv = R.qkv
            lanes = rows_of(p, LANES)
            klanes = pl.ds(pl.multiple_of(wl + p * LANES, LANES), LANES)
            keys = jnp.concatenate([qkv[0:length, klanes], R.kseg[0:length]], axis=1)
            query = qkv[rows, lanes] * head_mask[h] * jnp.asarray(scale, BF)
            s = dot_nt(keys, jnp.concatenate([query, R.qseg[rows]], axis=1))
            low = s[length - qb :]
            causal = lax.broadcasted_iota(jnp.int32, (qb, qb), 0) <= lax.broadcasted_iota(
                jnp.int32, (qb, qb), 1
            )
            low = jnp.where(causal, low, MASKED)
            s = low if i == 0 else jnp.concatenate([s[: length - qb], low], axis=0)
            return s, query

        def attend(p):
            qkv = R.qkv
            lanes = rows_of(p, LANES)
            vlanes = pl.ds(pl.multiple_of(2 * wl + p * LANES, LANES), LANES)
            vt = qkv[:, vlanes].T
            for i in range(nq):
                length = (i + 1) * qb
                outs = []
                for h in range(2):
                    s, _query = scores(p, i, h)
                    top = jnp.max(s, axis=0, keepdims=True)
                    expo = jnp.exp(s - top)
                    total = jnp.sum(expo, axis=0, keepdims=True)
                    mixed = dot_nn(vt[h * HD : (h + 1) * HD, 0:length], expo.astype(BF))
                    outs.append(mixed * (1.0 / total))
                    R.lse[p, h : h + 1, i * qb : (i + 1) * qb] = top + jnp.log(total)
                R.o[i * qb : (i + 1) * qb, lanes] = jnp.concatenate(outs, axis=0).T.astype(BF)

        pl.run_scoped(project, pltpu.VMEM((n, D), BF), pltpu.VMEM((D, w3), BF))

        @pl.loop(0, pairs)
        def _(p):
            attend(p)

        ag_rest(OUT)
        ag_far(GU0)
        ag_near(GU1)
        ag_done(OUT)

        partial_rows(0, lambda rows: dot_nn(R.o[rows], R.wo[...]))
        sum_relay(0)
        sum_arrived(0)

        def norm_rows(xown):
            local_now(R.x.at[own_rows], xown)

            @pl.loop(0, sr // lt)
            def _(i):
                rows = rows_of(i, lt)
                resid = add_peers(rows) + xown[rows].astype(F32)
                acc[rows] = resid
                hat, _inv = normed(resid)
                R.h2[pl.ds(pl.multiple_of(t * sr + i * lt, lt), lt)] = (
                    hat * gain(2) + gain(3)
                ).astype(BF)

        pl.run_scoped(norm_rows, pltpu.VMEM((sr, D), BF))

        rows_gather(0, R.h2)
        local_now(acc, R.sp_r1)
        ag_rest(GU0)
        ag_far(GU1)
        ag_done(GU0)
        rows_relay(0, R.h2)
        ag_rest(GU1)
        ag_near(DOWN)
        ag_done(GU1)

        def feed(sp):
            def first_half(at):
                def gate_up(a):
                    @pl.loop(0, tpn)
                    def _(k):
                        @when(k == 2)
                        def _():
                            ag_hop(1)

                        rows = rows_arrived(0, R.h2, k)
                        for lo, size in chunks(fl, 768):
                            g = dot_nn(R.h2[rows], R.wgu[:, lo : lo + size])
                            u = dot_nn(R.h2[rows], R.wgu[:, fl + lo : fl + lo + size])
                            sig = 1.0 / (1.0 + jnp.exp(-g))
                            act = g * sig
                            hidden = (act * u).astype(BF)
                            a[rows, lo : lo + size] = hidden
                            at[lo : lo + size, rows] = hidden.T
                            sp[rows, lo : lo + size] = (u * sig * (1.0 + g * (1.0 - sig))).astype(
                                BF
                            )
                            sp[rows, fl + lo : fl + lo + size] = act.astype(BF)

                    local_now(a, R.sp_a)

                pl.run_scoped(gate_up, pltpu.VMEM((n, fl), BF))
                load_y.wait()

                def down_grad(stage, mine):
                    def compute(j, put):
                        put(0, ds, dot_nn(at[...], R.dt[:, rows_of(j, ds)]))

                    rs_unit(RD, compute, stage, mine, (nc - 1, lambda: ag_hop(2)))

                pl.run_scoped(
                    down_grad, pltpu.VMEM((2, fl, ds), BF), pltpu.VMEM((fl, ds), F32)
                )

            pl.run_scoped(first_half, pltpu.VMEM((fl, n), BF))
            for h in range(3, nc):
                ag_hop(h)
            rs_rest(RD)
            rs_via(RD)
            ag_done(DOWN)

            def hidden_grad(wd):
                local_now(R.ag_d, wd)

                @pl.loop(0, n // rt)
                def _(i):
                    rows = rows_of(i, rt)
                    for lo, size in chunks(fl, 768):
                        da = dot_nt(R.dt[rows], wd[lo : lo + size])
                        sp[rows, lo : lo + size] = (
                            da * sp[rows, lo : lo + size].astype(F32)
                        ).astype(BF)
                        sp[rows, fl + lo : fl + lo + size] = (
                            da * sp[rows, fl + lo : fl + lo + size].astype(F32)
                        ).astype(BF)

            pl.run_scoped(hidden_grad, pltpu.VMEM((fl, D), BF))
            partial_rows(1, lambda rows: dot_nt(sp[rows], R.wgu[...]))

            def gu_grad(stage, mine):
                def compute(j, put):
                    left = R.h2[:, rows_of(j, ds)].T
                    for lo, size in chunks(f2, 1024):
                        put(lo, size, dot_nn(left, sp[:, lo : lo + size]))

                rs_unit(RGU, compute, stage, mine, (1, lambda: sum_relay(1)))

            pl.run_scoped(gu_grad, pltpu.VMEM((2, ds, f2), BF), pltpu.VMEM((ds, f2), F32))

        pl.run_scoped(feed, pltpu.VMEM((n, f2), BF))
        rows_sent(0, R.h2)
        for u in (GU0, GU1):
            ag_sent(u)
            ag_drain(u)
        load_h1 = local(R.sp_h1, R.h2, 6)
        load_wq = [
            local(
                R.ag_q.at[:, pl.ds(m * wl + g * gl, gl)],
                R.wgu.at[:, pl.ds(g * g3 + m * gl, gl)],
                16 + nc + 3 * g + m,
            )
            for g in range(2)
            for m in range(3)
        ]

        def norm_two(r1, yown):
            one = local(R.cot.at[own_rows], yown, 1)
            local_now(R.sp_r1, r1)
            one.wait()
            sum_arrived(1)
            R.gsum[...] = jnp.zeros_like(R.gsum)

            @pl.loop(0, sr // lt)
            def _(i):
                rows = rows_of(i, lt)
                grad = add_peers(rows)
                hat, inv = normed(r1[rows])
                out = yown[rows].astype(F32) + norm_back(grad, hat, inv, gain(2))
                acc[rows] = out
                R.dt[pl.ds(pl.multiple_of(t * sr + i * lt, lt), lt)] = out.astype(BF)
                R.gsum[2:3] += jnp.sum(grad * hat, axis=0, keepdims=True)
                R.gsum[3:4] += jnp.sum(grad, axis=0, keepdims=True)

            rows_gather(1, R.dt)
            rs_rest(RGU)
            local_now(acc, R.sp_dr1)

        pl.run_scoped(norm_two, pltpu.VMEM((sr, D), F32), pltpu.VMEM((sr, D), BF))

        load_h1.wait()
        if turned:

            @pl.loop(0, n // qb)
            def _(i):
                R.wgu[:, pl.ds(pl.multiple_of(w3 + i * qb, LANES), qb)] = R.h2[rows_of(i, qb)].T

        rows_relay(1, R.dt)

        def mlp_out(a, wd, out, own):
            local_now(R.ag_d, wd)

            @pl.loop(1, tpn + 1)
            def _(k):
                local_now(R.sp_a.at[rows_of(peer(k), sr)], a)
                value = dot_nn(a[...], wd[...])

                @when(k < tpn)
                def _():
                    out[...] = value.astype(BF)
                    local_now(out, R.mlp_p.at[k - 1])

                @when(k == tpn)
                def _():
                    own[...] = value
                    local_now(own, R.sp_mlp)

        pl.run_scoped(
            mlp_out,
            pltpu.VMEM((sr, fl), BF),
            pltpu.VMEM((fl, D), BF),
            pltpu.VMEM((sr, D), BF),
            pltpu.VMEM((sr, D), F32),
        )

        rs_via(RGU)
        rs_drain(RD)
        free_signal(0)

        def attention_back(dp):
            def back(do, dk, dv):
                @pl.loop(0, tpn)
                def _(k):
                    rows = rows_arrived(1, R.dt, k)
                    do[rows] = dot_nt(R.dt[rows], R.wo[...]).astype(BF)

                for k in range(1, tpn):
                    x_send(3, k, R.mlp_p.at[k - 1], R.mlp_r.at[k - 1])

                def out_grad(ot, stage, mine):
                    ot[...] = R.o[...].T

                    def compute(j, put):
                        put(0, ds, dot_nn(ot[...], R.dt[:, rows_of(j, ds)]))

                    pl.semaphore_wait(R.free.at[0], 1)
                    rs_unit(RO, compute, stage, mine)

                pl.run_scoped(
                    out_grad,
                    pltpu.VMEM((wl, n), BF),
                    pltpu.VMEM((2, wl, ds), BF),
                    pltpu.VMEM((wl, ds), F32),
                )

                rs_rest(RO)
                rows_sent(1, R.dt)
                free_signal(1)
                for copy in load_wq:
                    copy.wait()

                def pair_back(g, own):
                    qkv = R.qkv
                    p = g * (pairs // 2) + own
                    lanes = rows_of(p, LANES)
                    klanes = pl.ds(pl.multiple_of(wl + p * LANES, LANES), LANES)
                    vlanes = pl.ds(pl.multiple_of(2 * wl + p * LANES, LANES), LANES)

                    def out_lanes(m):
                        return pl.ds(pl.multiple_of(g * g3 + m * gl + own * LANES, LANES), LANES)

                    kt = qkv[:, klanes].T
                    dk[...] = jnp.zeros_like(dk)
                    dv[...] = jnp.zeros_like(dv)
                    for i in range(nq):
                        length = (i + 1) * qb
                        rows = pl.ds(i * qb, qb)
                        pbs, dss, qms, doms, dqs = [], [], [], [], []
                        for h in range(2):
                            s, query = scores(p, i, h)
                            prob = jnp.exp(s - R.lse[p, h : h + 1, i * qb : (i + 1) * qb])
                            dom = do[rows, lanes] * head_mask[h]
                            dprob = dot_nt(qkv[0:length, vlanes], dom)
                            weighted = jnp.sum(prob * dprob, axis=0, keepdims=True)
                            dsc = (prob * (dprob - weighted)).astype(BF)
                            pbs.append(prob.astype(BF))
                            dss.append(dsc)
                            qms.append(query)
                            doms.append(dom)
                            dqs.append(dot_nn(kt[h * HD : (h + 1) * HD, 0:length], dsc))
                        dv[0:length] += dot_nn(
                            jnp.concatenate(pbs, axis=1), jnp.concatenate(doms, axis=0)
                        )
                        dk[0:length] += dot_nn(
                            jnp.concatenate(dss, axis=1), jnp.concatenate(qms, axis=0)
                        )
                        dq = jnp.concatenate(dqs, axis=0).T * scale
                        dp[rows, out_lanes(0)] = rotate(dq, rows, -1.0).astype(BF)
                    dp[:, out_lanes(1)] = rotate(dk[...], pl.ds(0, n), -1.0).astype(BF)
                    dp[:, out_lanes(2)] = dv[...].astype(BF)

                @pl.loop(0, 2)
                def _(g):
                    @pl.loop(0, pairs // 2)
                    def _(own):
                        pair_back(g, own)

                    @when(g == 0)
                    def _():
                        rs_via(RO)
                        pl.semaphore_wait(R.free.at[1], 1)

                    @when(g == 1)
                    def _():
                        rs_via(RQ(0))
                        partial_rows(2, lambda rows: dot_nt(dp[rows], R.wgu[:, 0:w3]))

                    def qkv_grad(stage, mine):
                        def compute(j, put):
                            if turned:
                                left = R.wgu[rows_of(j, ds), w3 : w3 + n]
                            else:
                                left = R.h2[:, rows_of(j, ds)].T
                            put(0, g3, dot_nn(left, dp[:, rows_of(g, g3)]))

                        rs_unit(RQ(g), compute, stage, mine)

                    pl.run_scoped(qkv_grad, pltpu.VMEM((2, ds, g3), BF), pltpu.VMEM((ds, g3), F32))
                    rs_rest(RQ(g))

            pl.run_scoped(
                back,
                pltpu.VMEM((n, wl), BF),
                pltpu.VMEM((n, LANES), F32),
                pltpu.VMEM((n, LANES), F32),
            )
            sums = jnp.zeros((1, w3), F32)
            for i in range(n // qb):
                sums = sums + jnp.sum(
                    dp[i * qb : (i + 1) * qb].astype(F32), axis=0, keepdims=True
                )
            R.gbs[0] = jnp.broadcast_to(sums, (8, w3))
            remote(R.gbs.at[0], R.gbs.at[1], R.c_s.at[nc], R.c_r.at[nc], sib, t).start()


        pl.run_scoped(attention_back, pltpu.VMEM((n, w3), BF))

        arrived(R.gbs.at[1], R.c_r.at[nc])
        cslot = R.cslot
        cslot[z] = R.gbs[0] + R.gbs[1]
        for k in range(1, nc):
            remote(
                cslot.at[z], cslot.at[z], R.c_s.at[chip(k)], R.c_r.at[z], dp_of(chip(k)), t
            ).start()

        sum_relay(2)

        def block_rows(r1, own, got, out):
            a = local(R.sp_r1, r1, 1)
            b = local(R.sp_mlp, own, 2)
            for k in range(1, tpn):
                arrived(R.mlp_r.at[k - 1], R.x_r.at[3, k])
            local_now(R.mlp_r, got)
            a.wait()
            b.wait()

            @pl.loop(0, sr // lt)
            def _(i):
                rows = rows_of(i, lt)
                total = own[rows]
                for k in range(1, tpn):
                    total = total + got[k - 1, rows].astype(F32)
                out[rows] = (r1[rows] + total).astype(BF)

            local_now(out, R.block_out)

        pl.run_scoped(
            block_rows,
            pltpu.VMEM((sr, D), F32),
            pltpu.VMEM((sr, D), F32),
            pltpu.VMEM((tpn - 1, sr, D), BF),
            pltpu.VMEM((sr, D), BF),
        )

        rs_via(RQ(1))

        def norm_one(dr1, xown):
            one = local(R.x.at[own_rows], xown, 1)
            local_now(R.sp_dr1, dr1)
            one.wait()
            sum_arrived(2)

            @pl.loop(0, sr // lt)
            def _(i):
                rows = rows_of(i, lt)
                grad = add_peers(rows)
                hat, inv = normed(xown[rows].astype(F32))
                dr1[rows] = dr1[rows] + norm_back(grad, hat, inv, gain(0))
                R.gsum[0:1] += jnp.sum(grad * hat, axis=0, keepdims=True)
                R.gsum[1:2] += jnp.sum(grad, axis=0, keepdims=True)

            keep = local(dr1, R.input_grad, 1)
            ns = R.nsum
            ns[0, 0:4] = R.gsum[0:4, 0 : D // 2]
            ns[0, 4:8] = R.gsum[0:4, D // 2 :]
            remote(ns.at[0], ns.at[1], R.n_s.at[0], R.n_r.at[0], sib, t).start()
            arrived(ns.at[1], R.n_r.at[0])
            zs = R.nz
            zs[z] = ns[0] + ns[1]
            for k in range(1, nc):
                remote(
                    zs.at[z], zs.at[z], R.n_s.at[k], R.n_r.at[1 + z], dp_of(chip(k)), t
                ).start()
            for k in range(1, nc):
                arrived(zs.at[chip(k)], R.n_r.at[1 + chip(k)])
            total = zs[0]
            for s in range(1, nc):
                total = total + zs[s]
            ts = R.nt
            ts[t] = total
            for k in range(1, tpn):
                remote(
                    ts.at[t], ts.at[t], R.n_s.at[nc + k], R.n_r.at[1 + nc + t], dpi, peer(k)
                ).start()
            for k in range(1, tpn):
                arrived(ts.at[peer(k)], R.n_r.at[1 + nc + peer(k)])
            total = ts[0]
            for s in range(1, tpn):
                total = total + ts[s]
            R.gn[...] = total
            keep.wait()

        pl.run_scoped(norm_one, pltpu.VMEM((sr, D), F32), pltpu.VMEM((sr, D), BF))

        for k in range(1, nc):
            arrived(cslot.at[chip(k)], R.c_r.at[chip(k)])
        total = cslot[0]
        for s in range(1, nc):
            total = total + cslot[s]
        R.gb[...] = total

        for u in (RD, RGU, RO, RQ(0), RQ(1)):
            rs_arrived(u)

        for u in (QKV, OUT, DOWN):
            ag_sent(u)
        for u in (QKV, OUT, DOWN):
            ag_drain(u)
        ag_hops_sent()
        for u in (RGU, RO, RQ(0), RQ(1)):
            rs_drain(u)
        xs_sent(2)
        for k in range(1, tpn):
            sent(R.mlp_p.at[k - 1], R.x_s.at[3, k])
            sent(R.nt.at[0], R.n_s.at[nc + k])
        for k in range(1, nc):
            sent(R.brow, R.b_s.at[chip(k)])
            sent(cslot.at[0], R.c_s.at[chip(k)])
            sent(R.nz.at[0], R.n_s.at[k])
        sent(R.bsum.at[0], R.b_s.at[nc])
        sent(R.gbs.at[0], R.c_s.at[nc])
        sent(R.nsum.at[0], R.n_s.at[0])

    return kern


def fused(x, seg, cot, norm, brow, freq, weights, dpn, tpn, cast):
    n = x.shape[0]
    wl = weights[1].shape[0]
    fl = weights[3].shape[0]
    nc = dpn // 2
    ds = D // dpn
    sr = n // tpn
    w3, f2 = 3 * wl, 2 * fl
    pairs = wl // LANES
    g3 = 3 * (wl // 2)
    hbm = pl.BlockSpec(memory_space=pl.ANY)
    vmem = pl.BlockSpec(memory_space=pltpu.VMEM)
    ins = [
        ("x", hbm),
        ("seg", vmem),
        ("cot", hbm),
        ("norm", vmem),
        ("brow", vmem),
        ("freq", vmem),
    ]
    shards = ["wq_s", "wo_s", "wgu_s", "wd_s"]
    ins += [(i, hbm) for i in (["wq_f", "wo_f", "wgu_f", "wd_f"] if cast else shards)]
    boxes = [(fl, ds), (ds, f2), (wl, ds)]
    outs = [
        ("block_out", (sr, D), BF, hbm),
        ("input_grad", (sr, D), F32, hbm),
        ("gn", (8, D // 2), F32, vmem),
        ("gb", (8, w3), F32, vmem),
    ]
    outs += [("zr%d" % u, (nc,) + s, BF, hbm) for u, s in enumerate(boxes)]
    outs += [("zrq", (2, nc, ds, g3), BF, hbm)]
    outs += [("vrq", (2, 2, ds, g3), BF, hbm)]
    outs += [
        ("ag_q", (D, w3), BF, hbm),
        ("ag_d", (fl, D), BF, hbm),
        ("mlp_p", (tpn - 1, sr, D), BF, hbm),
        ("mlp_r", (tpn - 1, sr, D), BF, hbm),
        ("sp_h1", (n, D), BF, hbm),
        ("sp_a", (n, fl), BF, hbm),
        ("sp_r1", (sr, D), F32, hbm),
        ("sp_mlp", (sr, D), F32, hbm),
        ("sp_dr1", (sr, D), F32, hbm),
    ]
    outs += [("vr%d" % u, (2,) + s, BF, hbm) for u, s in enumerate(boxes)]
    dma = pltpu.SemaphoreType.DMA
    scratch = [
        ("wgu", pltpu.VMEM((D, f2), BF)),
        ("wo", pltpu.VMEM((wl, D), BF)),
        ("h2", pltpu.VMEM((n, D), BF)),
        ("dt", pltpu.VMEM((n, D), BF)),
        ("xs", pltpu.VMEM((tpn - 1, sr, D), BF)),
        ("xr", pltpu.VMEM((tpn - 1, sr, D), BF)),
        ("acc", pltpu.VMEM((sr, D), F32)),
        ("qkv", pltpu.VMEM((n, w3), BF)),
        ("o", pltpu.VMEM((n, wl), BF)),
        ("tc", pltpu.VMEM((n, LANES), F32)),
        ("ts", pltpu.VMEM((n, LANES), F32)),
        ("kseg", pltpu.VMEM((n, LANES), BF)),
        ("qseg", pltpu.VMEM((n, LANES), BF)),
        ("lse", pltpu.VMEM((pairs, 2, n), F32)),
        ("bslot", pltpu.VMEM((nc, 8, w3), F32)),
        ("bsum", pltpu.VMEM((2, 8, w3), F32)),
        ("gbs", pltpu.VMEM((2, 8, w3), F32)),
        ("cslot", pltpu.VMEM((nc, 8, w3), F32)),
        ("gsum", pltpu.VMEM((8, D), F32)),
        ("nsum", pltpu.VMEM((2, 8, D // 2), F32)),
        ("nz", pltpu.VMEM((nc, 8, D // 2), F32)),
        ("nt", pltpu.VMEM((tpn, 8, D // 2), F32)),
    ]
    scratch += [("box%d" % u, pltpu.VMEM((nc,) + boxes[u], BF)) for u in range(2)]
    scratch += [
        ("dum", dma((1,))),
        ("loc", dma((27 + nc,))),
        ("self", dma((5,))),
        ("hop", dma((nc, 2))),
        ("free", pltpu.SemaphoreType.REGULAR((2,))),
        ("ag_s", dma((5, nc))),
        ("ag_r", dma((5, nc))),
        ("av_s", dma((5, 2))),
        ("sb_s", dma((5, nc))),
        ("sb_r", dma((5, nc))),
        ("rb_s", dma((5, nc))),
        ("rb_r", dma((5, nc))),
        ("rz_s", dma((5, nc))),
        ("rz_r", dma((5, nc))),
        ("rv_r", dma((5, 2))),
        ("x_s", dma((4, max(tpn, 6)))),
        ("x_r", dma((4, max(tpn, 6)))),
        ("g_s", dma((2, max(tpn, 6)))),
        ("g_r", dma((2, max(tpn, 6)))),
        ("b_s", dma((nc + 1,))),
        ("b_r", dma((nc + 1,))),
        ("c_s", dma((nc + 1,))),
        ("c_r", dma((nc + 1,))),
        ("n_s", dma((nc + tpn,))),
        ("n_r", dma((1 + nc + tpn,))),
    ]
    names = [i[0] for i in ins] + [o[0] for o in outs] + [s[0] for s in scratch]
    got = pl.pallas_call(
        make_kernel(names, n, wl, fl, dpn, tpn, cast),
        out_shape=[jax.ShapeDtypeStruct(s, d) for _, s, d, _ in outs],
        in_specs=[s for _, s in ins],
        out_specs=[m for _, _, _, m in outs],
        scratch_shapes=[s for _, s in scratch],
        compiler_params=pltpu.CompilerParams(
            collective_id=0, has_side_effects=True, vmem_limit_bytes=63 * 2**20
        ),
        name="block_step",
    )(x, seg, cot, norm, brow, freq, *weights)
    return got[:8]


def adamw(weight, first, second, grad, rate, decay):
    new_first = BETA_ONE * first + (1.0 - BETA_ONE) * grad
    new_second = BETA_TWO * second + (1.0 - BETA_TWO) * grad * grad
    direction = (
        new_first
        / (1.0 - BETA_ONE**STEP)
        / (jnp.sqrt(new_second / (1.0 - BETA_TWO**STEP)) + ADAM_EPS)
    )
    return (new_first, new_second, weight - rate * (direction + decay * weight))


def update_all(groups, norm_grad, norm_state, passed):
    hbm = pl.BlockSpec(memory_space=pl.ANY)
    f32 = lambda s: pltpu.VMEM(s, F32)
    n_groups = len(groups)
    scratch = []
    for grad, weight, _, _, pieces, _ in groups:
        scratch.append(pltpu.VMEM(grad.shape, BF))
        scratch += [f32((len(pieces),) + pieces[0][2])] * 3
    count = sum(1 + 6 * len(g[4]) for g in groups) + 7 + 2 * len(passed)
    scratch += [f32(norm_grad.shape)] + [f32(x.shape) for x in norm_state]
    scratch += [pltpu.VMEM(x.shape, x.dtype) for x in passed]

    def kern(*refs):
        n_ins = 4 * n_groups + 4 + len(passed)
        n_outs = 3 * n_groups + 3 + len(passed)
        ins, outs = refs[:n_ins], refs[n_ins : n_ins + n_outs]
        bufs, sem = refs[n_ins + n_outs : -1], refs[-1]
        at = iter(range(count))
        loads, plan = [], []

        def start(src, dst):
            cp = pltpu.make_async_copy(src, dst, sem.at[next(at)])
            cp.start()
            return cp

        for i, (_, _, _, _, pieces, rate) in enumerate(groups):
            g, *state = bufs[4 * i : 4 * i + 4]
            got = [start(ins[4 * i], g)]
            for j, (_, state_part, _) in enumerate(pieces):
                for k in range(3):
                    got.append(start(state_part(ins[4 * i + 1 + k]), state[k].at[j]))
            plan.append((got, g, state, pieces, rate, outs[3 * i : 3 * i + 3]))
        small = [
            start(a, b)
            for a, b in zip(ins[4 * n_groups :], bufs[4 * n_groups :], strict=True)
        ]
        stores = []
        for got, g, state, pieces, rate, dst in plan:
            for cp in got:
                cp.wait()
            for j, (grad_part, state_part, (rows, cols)) in enumerate(pieces):
                step = 64 if cols <= 512 else 16
                terms = grad_part(g)
                w, m, v = (x.at[j] for x in state)

                @pl.loop(0, rows // step)
                def _(r):
                    at_rows = pl.ds(pl.multiple_of(r * step, step), step)
                    grad = terms[0][at_rows, :].astype(F32)
                    for term in terms[1:]:
                        grad = grad + term[at_rows, :].astype(F32)
                    first, second, new = adamw(
                        w[at_rows, :], m[at_rows, :], v[at_rows, :], grad, rate, DECAY
                    )
                    m[at_rows, :] = first
                    v[at_rows, :] = second
                    w[at_rows, :] = new

                for k, buf in enumerate((m, v, w)):
                    stores.append(start(buf, state_part(dst[k])))
        for cp in small:
            cp.wait()
        g, w, m, v = bufs[4 * n_groups : 4 * n_groups + 4]
        half = w.shape[1] // 2
        for h in range(2):
            cols = slice(h * half, (h + 1) * half)
            first, second, new = adamw(
                w[:, cols], m[:, cols], v[:, cols], g[4 * h : 4 * h + 4], 0.5, 0.0
            )
            m[:, cols] = first
            v[:, cols] = second
            w[:, cols] = new
        for a, b in zip(
            (m, v, w) + tuple(bufs[4 * n_groups + 4 :]), outs[3 * n_groups :], strict=True
        ):
            stores.append(start(a, b))
        for cp in stores:
            cp.wait()

    out_shape = []
    flat = []
    for grad, weight, first, second, _, _ in groups:
        flat += [grad, weight, first, second]
        out_shape += [jax.ShapeDtypeStruct(weight.shape, F32)] * 3
    flat += [norm_grad, *norm_state, *passed]
    out_shape += [jax.ShapeDtypeStruct(x.shape, x.dtype) for x in (*norm_state, *passed)]
    got = pl.pallas_call(
        kern,
        out_shape=out_shape,
        in_specs=[hbm] * len(flat),
        out_specs=[hbm] * len(out_shape),
        scratch_shapes=scratch + [pltpu.SemaphoreType.DMA((count,))],
        compiler_params=pltpu.CompilerParams(vmem_limit_bytes=56 * 2**20),
        name="adamw",
    )(*flat)
    return [tuple(got[3 * i : 3 * i + 3]) for i in range(n_groups + 1)], got[3 * n_groups + 3 :]


def body(
    tokens,
    segments,
    cotangent,
    norm_params,
    norm_m,
    norm_v,
    qkv_bias,
    bias_m,
    bias_v,
    w_qkv,
    qkv_m,
    qkv_v,
    w_out,
    out_m,
    out_v,
    w_gateup,
    gateup_m,
    gateup_v,
    w_down,
    down_m,
    down_v,
):
    n_rows, model = tokens.shape
    dpn = lax.axis_size("dp")
    tpn = lax.axis_size("tensor")
    ds, _, wl = w_qkv.shape
    fl = w_down.shape[0]
    pad = -fl % LANES
    heads, cut = qkv_bias.shape[1:]
    assert segments.shape[0] == 1 and model == D
    me = lax.axis_index("dp")

    bias = qkv_bias.astype(BF).astype(F32)
    wide = lax.dynamic_update_slice(jnp.zeros((3, heads, HD), F32), bias, (0, 0, me * cut))
    brow = jnp.broadcast_to(wide.reshape(1, 3 * wl), (8, 3 * wl))
    part = HD // 8
    freq = ROPE_BASE ** (-2.0 * (np.arange(LANES) % part) / (HD // 4))
    freq = jnp.asarray(freq.reshape(1, LANES), F32)
    cast = not pad
    if cast:
        weights = (jnp.transpose(w_qkv, (1, 0, 2)), w_out, w_gateup, w_down)
    else:
        wgu = jnp.pad(w_gateup.astype(BF), ((0, 0), (0, 0), (0, pad)))
        weights = (
            w_qkv.astype(BF).reshape(ds, 3 * wl),
            w_out.astype(BF),
            wgu.reshape(ds, 2 * (fl + pad)),
            jnp.pad(w_down.astype(BF), ((0, pad), (0, 0))),
        )
    block_out, input_grad, gn, gb, red_down, red_gu, red_out, red_qkv = fused(
        tokens, segments, cotangent, norm_params, brow, freq, weights, dpn, tpn, cast
    )
    red_bias = jnp.swapaxes(gb[0].reshape(2, 3, wl // 2), 0, 1).reshape(3, heads, HD)
    red_bias = lax.dynamic_slice(red_bias, (0, 0, me * cut), (3, heads, cut))
    gl = wl // 2
    nc = dpn // 2
    qkv_pieces = [
        (
            lambda r, g=g, m=m: [r.at[g, s, :, pl.ds(m * gl, gl)] for s in range(nc)],
            lambda r, g=g, m=m: r.at[m, :, pl.ds(g * gl, gl)],
            (ds, gl),
        )
        for g in range(2)
        for m in range(3)
    ]
    whole = lambda r: r
    every = lambda r: [r.at[s] for s in range(nc)]

    def turn(x):
        return jnp.transpose(x, (1, 0, 2))

    groups = [
        (red_qkv, turn(w_qkv), turn(qkv_m), turn(qkv_v), qkv_pieces, D ** (-0.5)),
        (red_out, w_out, out_m, out_v, [(every, whole, w_out.shape)], HD ** (-0.5)),
    ]
    if not pad:
        gu_pieces = [
            (
                lambda r, h=h: [r.at[s, :, pl.ds(h * fl, fl)] for s in range(nc)],
                lambda r, h=h: r.at[:, h],
                (ds, fl),
            )
            for h in range(2)
        ]
        groups += [
            (red_gu, w_gateup, gateup_m, gateup_v, gu_pieces, D ** (-0.5)),
            (red_down, w_down, down_m, down_v, [(every, whole, w_down.shape)], FF ** (-0.5)),
        ]
    done, (block_out, input_grad) = update_all(
        groups, gn, (norm_params, norm_m, norm_v), (block_out, input_grad)
    )
    new_norm = done.pop()
    new_qkv = tuple(turn(x) for x in done[0])
    if pad:
        red_gu = jnp.sum(red_gu, axis=0, dtype=F32).reshape(ds, 2, fl + pad)[:, :, :fl]
        red_down = jnp.sum(red_down, axis=0, dtype=F32)[:fl]
        done += [
            adamw(w_gateup, gateup_m, gateup_v, red_gu, D ** (-0.5), DECAY),
            adamw(w_down, down_m, down_v, red_down, FF ** (-0.5), DECAY),
        ]
    return (
        (block_out, input_grad)
        + new_norm
        + adamw(qkv_bias, bias_m, bias_v, red_bias, 0.3, 0.0)
        + new_qkv
        + done[1]
        + done[2]
        + done[3]
    )


def solution(mesh):
    rows = P("dp", None)
    bias = P(None, "tensor", "dp")
    wide = P("dp", None, "tensor")
    tall = P("tensor", "dp")
    split = P(("dp", "tensor"), None)
    return jax.shard_map(
        body,
        mesh=mesh,
        in_specs=(rows,) * 3 + (P(),) * 3 + (bias,) * 3 + (wide,) * 3 + (tall,) * 3 + (wide,) * 3
        + (tall,) * 3,
        out_specs=(split,) * 2 + (P(),) * 3 + (bias,) * 3 + (wide,) * 3 + (tall,) * 3 + (wide,) * 3
        + (tall,) * 3,
        check_vma=False,
    )
```

```python
from types import SimpleNamespace

import numpy as np
import jax
import jax.numpy as jnp
from jax import lax
from jax.experimental import pallas as pl
from jax.experimental.pallas import tpu as pltpu
from jax.sharding import PartitionSpec as P

D = 2048
HD = 64
FF = 5632
STEP = 10

NORM_EPS = 1e-05
BETA_ONE = 0.9
BETA_TWO = 0.95
ADAM_EPS = 1e-08
DECAY = 0.1
ROPE_BASE = 10000.0

BF = jnp.bfloat16
F32 = jnp.float32
MESH = pl.DeviceIdType.MESH
LANES = 128
MASKED = -1e30

QKV, OUT, GU0, GU1, DOWN = range(5)


def dot_nn(a, b):
    return lax.dot_general(a, b, (((1,), (0,)), ((), ())), preferred_element_type=F32)


def dot_nt(a, b):
    return lax.dot_general(a, b, (((1,), (1,)), ((), ())), preferred_element_type=F32)


def dot_tn(a, b):
    return lax.dot_general(a, b, (((0,), (0,)), ((), ())), preferred_element_type=F32)


def chunks(total, step):
    return [(lo, min(step, total - lo)) for lo in range(0, total, step)]


def hidden_parts(fl):
    size = (fl // LANES + 1) // 2 * LANES
    return ((0, size, 0), (size, fl - size, 2 * size))


def normed(values):
    centre = values - jnp.mean(values, axis=1, keepdims=True)
    inv = lax.rsqrt(jnp.mean(centre * centre, axis=1, keepdims=True) + NORM_EPS)
    return centre * inv, inv


def norm_back(grad, hat, inv, gain):
    e = grad * gain
    return inv * (
        e - jnp.mean(e, axis=1, keepdims=True) - hat * jnp.mean(e * hat, axis=1, keepdims=True)
    )


def make_kernel(names, n, wl, fl, dpn, tpn, cast):
    nc = dpn // 2
    ds = D // dpn
    sr = n // tpn
    w3 = 3 * wl
    f2 = 2 * fl
    parts = hidden_parts(fl)
    cols = [pl.ds(off, 2 * size) for _, size, off in parts]
    qb = min(256, n)
    nq = n // qb
    rt = min(256, sr)
    lt = min(128, sr)
    pairs = wl // LANES
    gl = wl // 2
    g3 = 3 * gl
    hr = sr // 2
    square = tpn == 4
    turned = w3 + n <= f2
    scale = HD ** (-0.5)
    has_via = nc >= 3

    def kern(*refs):
        R = SimpleNamespace(**dict(zip(names, refs, strict=True)))
        dpi = lax.axis_index("dp")
        t = lax.axis_index("tensor")
        z = lax.div(dpi, 2)
        c = lax.rem(dpi, 2)
        oc = 1 - c
        sib = dpi + 1 - 2 * c

        def chip(k):
            return lax.rem(z + k, nc)

        def dp_of(s):
            return 2 * s + c

        def flip(i, k):
            return lax.rem(i + k, 2) + 2 * lax.rem(lax.div(i, 2) + lax.div(k, 2), 2)

        def peer(k):
            k = jnp.asarray(k, jnp.int32)
            return flip(t, k) if square else lax.rem(t + k, tpn)

        def source(k):
            k = jnp.asarray(k, jnp.int32)
            return flip(t, k) if square else lax.rem(t + tpn - k, tpn)

        def remote(src, dst, ss, rs, dp, tn):
            return pltpu.make_async_remote_copy(
                src_ref=src,
                dst_ref=dst,
                send_sem=ss,
                recv_sem=rs,
                device_id=(dp, tn),
                device_id_type=MESH,
            )

        def arrived(dst, rs):
            remote(dst, dst, R.dum.at[0], rs, sib, t).wait_recv()

        def sent(src, ss):
            remote(src, src, ss, R.dum.at[0], sib, t).wait_send()

        def local(src, dst, i):
            cp = pltpu.make_async_copy(src, dst, R.loc.at[i])
            cp.start()
            return cp

        def local_now(src, dst):
            local(src, dst, 0).wait()

        def rows_of(i, size):
            return pl.ds(pl.multiple_of(i * size, size), size)

        own_rows = rows_of(t, sr)

        bar = pltpu.get_barrier_semaphore()
        pl.semaphore_signal(bar, inc=1, device_id=(sib, t), device_id_type=MESH)
        for k in range(1, nc):
            pl.semaphore_signal(bar, inc=1, device_id=(dp_of(chip(k)), t), device_id_type=MESH)
        for k in range(1, tpn):
            pl.semaphore_signal(bar, inc=1, device_id=(dpi, peer(k)), device_id_type=MESH)

        def all_here():
            pl.semaphore_wait(bar, 1 + (nc - 1) + (tpn - 1))

        def shard(u):
            if cast:
                return place(u, dpi)
            return {
                QKV: lambda: R.wq_s,
                OUT: lambda: R.wo_s,
                GU0: lambda: R.wgu_s.at[:, cols[0]],
                GU1: lambda: R.wgu_s.at[:, cols[1]],
                DOWN: lambda: R.wd_s,
            }[u]()

        def place(u, j):
            return {
                QKV: lambda: R.ag_q.at[rows_of(j, ds)],
                OUT: lambda: R.wo.at[:, rows_of(j, ds)],
                GU0: lambda: R.wgu.at[rows_of(j, ds), cols[0]],
                GU1: lambda: R.wgu.at[rows_of(j, ds), cols[1]],
                DOWN: lambda: R.ag_d.at[:, rows_of(j, ds)],
            }[u]()

        def relayed(src, dst):
            if not has_via:
                return src != src
            return ((src == 2) & (dst == 0)) | ((src == nc - 3) & (dst == nc - 1))

        def when(cond):
            return pl.when(cond)

        def within(s):
            return (s >= 0) & (s < nc)

        def apart(s):
            return (s - z >= 2) | (z - s >= 2)

        relays = ((1, 2, 0), (nc - 2, nc - 3, nc - 1)) if has_via else ()

        def ag_copy(u, d):
            return remote(
                shard(u), place(u, dpi), R.ag_s.at[u, d], R.ag_r.at[u, z], dp_of(d), t
            )

        def ag_near(u):
            for d in (z + 1, z - 1):

                @when(within(d))
                def _():
                    ag_copy(u, d).start()

            remote(shard(u), place(u, dpi), R.sb_s.at[u, z], R.sb_r.at[u, z], sib, t).start()
            if not cast:
                local(shard(u), place(u, dpi), 22 + nc + u)

        def to_sibling(u, s):
            here = place(u, dp_of(s))
            remote(here, here, R.sb_s.at[u, s], R.sb_r.at[u, s], sib, t).start()

        def ag_far(u):
            for s in (z + 1, z - 1):

                @when(within(s))
                def _():
                    arrived(place(u, dp_of(s)), R.ag_r.at[u, s])

            for i, (mid, src, dst) in enumerate(relays):

                @when(z == mid)
                def _():
                    here = place(u, dp_of(src))
                    remote(
                        here, here, R.av_s.at[u, i], R.ag_r.at[u, src], dp_of(dst), t
                    ).start()

            for d in range(nc):

                @when(apart(d) & jnp.logical_not(relayed(z, d)))
                def _():
                    ag_copy(u, d).start()

            for s in (z + 1, z - 1):

                @when(within(s))
                def _():
                    to_sibling(u, s)

        def ag_rest(u):
            for s in range(nc):

                @when(apart(s))
                def _():
                    arrived(place(u, dp_of(s)), R.ag_r.at[u, s])
                    to_sibling(u, s)

        def ag_sent(u):
            for d in range(nc):
                far = apart(d) if u == GU1 else relayed(z, d)

                @when((z != d) & jnp.logical_not(far))
                def _():
                    sent(shard(u), R.ag_s.at[u, d])

        def ag_hop(h):
            for i, way in enumerate((1, -1)):
                s = z + way * h

                @when(within(s))
                def _():
                    here = place(GU1, dp_of(s))
                    arrived(here, R.ag_r.at[GU1, s])

                    @when(within(z - way))
                    def _():
                        remote(
                            here, here, R.hop.at[h, i], R.ag_r.at[GU1, s], dp_of(z - way), t
                        ).start()

                    to_sibling(GU1, s)

        def ag_hops_sent():
            for h in range(1, nc - 1):
                for i, way in enumerate((1, -1)):

                    @when(within(z + way * h) & within(z - way))
                    def _():
                        sent(place(GU1, dpi), R.hop.at[h, i])

        def ag_done(u):
            if not cast:
                pltpu.make_async_copy(shard(u), place(u, dpi), R.loc.at[22 + nc + u]).wait()
            for s in range(nc):
                arrived(place(u, 2 * s + oc), R.sb_r.at[u, s])

        def ag_drain(u):
            for i, (mid, src, dst) in enumerate(() if u == GU1 else relays):

                @when(z == mid)
                def _():
                    sent(place(u, dp_of(src)), R.av_s.at[u, i])

            for s in range(nc):
                sent(shard(u), R.sb_s.at[u, s])

        def rs_merged(src, dst):
            if not has_via:
                return src != src
            return ((src == 0) & (dst == nc - 1)) | ((src == nc - 1) & (dst == 0))

        def rs_held(dst):
            if not has_via:
                return z != z
            return ((z == 1) & (dst == nc - 1)) | ((z == nc - 2) & (dst == 0))

        merges = ((0, 1, nc - 1), (nc - 1, nc - 2, 0)) if has_via else ()

        def unit(i, slot, zr, vr, shape):
            return SimpleNamespace(i=i, slot=slot, zr=zr, vr=vr, shape=shape)

        RD = unit(0, lambda d: R.box0.at[d], R.zr0, R.vr0, (fl, ds))
        RGA = unit(1, lambda d: R.box1.at[d, :, cols[0]], R.zr1, R.vr1, (ds, 2 * parts[0][1]))
        RGB = unit(5, lambda d: R.box1.at[d, :, cols[1]], R.zrb, R.vrb, (ds, 2 * parts[1][1]))

        def out_slot(d):
            return R.h2.at[pl.ds(0, wl), rows_of(d, ds)] if turned else R.box0.at[d, pl.ds(0, wl)]

        RO = unit(2, out_slot, R.zr2, R.vr2, (wl, ds))

        def RQ(g):
            lanes = pl.ds(g * g3, g3) if isinstance(g, int) else rows_of(g, g3)
            return unit(
                3 + g,
                lambda d: R.dt.at[rows_of(d, ds), lanes],
                R.zrq.at[g],
                R.vrq.at[g],
                (ds, g3),
            )

        def free_signal(i):
            pl.semaphore_signal(R.free.at[i], inc=1, device_id=(sib, t), device_id_type=MESH)

        def row_loop(total, cols):
            step = 128 if cols <= 512 else 16

            def over(act):
                @pl.loop(0, total // step)
                def _(i):
                    act(rows_of(i, step))

            return over

        def rs_late(u, d):
            if not has_via:
                return z != z
            if u is RGB or u is RD:
                return z != z
            return (d == 0) | (d == nc - 1) if u is RGA else (z == 0) | (z == nc - 1)

        def rs_direct(u, d):
            remote(
                u.slot(d), u.zr.at[z], R.rz_s.at[u.i, d], R.rz_r.at[u.i, z], dp_of(d), t
            ).start()

        def rs_rest(u):
            for d in range(nc):

                skip = rs_held(d) | rs_merged(z, d)

                @when(rs_late(u, d) & (z != d) & jnp.logical_not(skip))
                def _():
                    rs_direct(u, jnp.int32(d))

        def rs_unit(u, compute, stage, mine, pump=()):
            def finish(d):
                box = u.slot(d)
                arrived(box, R.rb_r.at[u.i, d])

                @row_loop(*u.shape)
                def _(rows):
                    box[rows, :] = (mine[rows] + box[rows, :].astype(F32)).astype(BF)

                @when(z == d)
                def _():
                    pltpu.make_async_copy(box, u.zr.at[z], R.self.at[u.i]).start()

                skip = rs_held(d) | rs_merged(z, d) | rs_late(u, d)

                @when((z != d) & jnp.logical_not(skip))
                def _():
                    rs_direct(u, d)

                for i, (src, mid, dst) in enumerate(merges):

                    @when((z == src) & (d == dst))
                    def _():
                        remote(
                            box, u.vr.at[i], R.rz_s.at[u.i, d], R.rv_r.at[u.i, i], dp_of(mid), t
                        ).start()

            def turn(i):
                return lax.rem(i + nc - 1, nc)

            @pl.loop(0, nc)
            def _(idx):
                d = turn(idx)
                slot = lax.rem(idx, 2)

                @when(idx >= 2)
                def _():
                    sent(stage.at[slot], R.rb_s.at[u.i, turn(idx + nc - 2)])

                def to_stage(lo, size, val):
                    stage[slot, :, lo : lo + size] = val.astype(BF)

                compute(2 * d + oc, to_stage)
                remote(
                    stage.at[slot], u.slot(d), R.rb_s.at[u.i, d], R.rb_r.at[u.i, d], sib, t
                ).start()

                @when(idx >= 1)
                def _():
                    finish(turn(idx + nc - 1))

                for i, act in pump:
                    when(idx == i)(act)

                def to_mine(lo, size, val):
                    mine[:, lo : lo + size] = val

                compute(2 * d + c, to_mine)

            finish(jnp.int32(nc - 2 if nc > 1 else 0))
            for i in (nc - 2, nc - 1):
                sent(stage.at[0], R.rb_s.at[u.i, (i + nc - 1) % nc])

        def rs_via(u):
            for i, (src, mid, dst) in enumerate(merges):

                @when(z == mid)
                def _():
                    box = u.slot(jnp.int32(dst))
                    arrived(u.vr.at[i], R.rv_r.at[u.i, i])

                    def add(tmp):
                        local_now(u.vr.at[i], tmp)

                        @row_loop(*u.shape)
                        def _(rows):
                            box[rows, :] = (
                                box[rows, :].astype(F32) + tmp[rows].astype(F32)
                            ).astype(BF)

                    pl.run_scoped(add, pltpu.VMEM(u.shape, BF))
                    remote(
                        box, u.zr.at[mid], R.rz_s.at[u.i, dst], R.rz_r.at[u.i, mid], dp_of(dst), t
                    ).start()

        def rs_arrived(u):
            for k in range(1, nc):
                s = chip(k)

                @when(jnp.logical_not(rs_merged(s, z)))
                def _():
                    arrived(u.zr.at[s], R.rz_r.at[u.i, s])

        def rs_drain(u):
            for k in range(1, nc):
                sent(u.slot(z), R.rz_s.at[u.i, chip(k)])
            pltpu.make_async_copy(u.slot(z), u.zr.at[z], R.self.at[u.i]).wait()

        def x_send(ph, k, src, dst):
            remote(src, dst, R.x_s.at[ph, k], R.x_r.at[ph, k], dpi, peer(k)).start()

        acc, xs, xr = R.acc, R.xs, R.xr
        steps = ((2, 0, 2, 1), (2, 1, 2, 2), (0, 0, 0, 1), (1, 1, 1, 2), (1, 0, 1, 2), (0, 1, 0, 1))

        def half_of(buf, slot, h):
            return buf.at[slot, pl.ds(h * hr, hr)]

        def step_send(ph, i):
            a, h, b, k = steps[i]
            remote(
                half_of(xs, a, h),
                half_of(xr, b, h),
                R.x_s.at[ph, i],
                R.x_r.at[ph, i],
                dpi,
                peer(k),
            ).start()

        def partial_rows(ph, product):
            if ph > 0:
                xs_sent(ph - 1)

            @pl.loop(0, tpn)
            def _(i):
                k = lax.rem(3 * (i + 1), 4) if square else lax.rem(i + 1, tpn)
                value = product(rows_of(peer(k), sr))

                @when(k > 0)
                def _():
                    xs[k - 1] = value.astype(BF)

                @when(k == 0)
                def _():
                    acc[...] = value

                if square:
                    for j, first in ((3, (0, 1)), (1, (2,)), (2, (3,))):

                        @when(k == j)
                        def _():
                            for m in first:
                                step_send(ph, m)
                else:

                    @when(k > 0)
                    def _():
                        x_send(ph, k, xs.at[k - 1], xr.at[k - 1])

        def sum_relay(ph):
            if not square:
                return
            for i, (slot, h) in ((0, (1, 0)), (1, (0, 1))):
                arrived(half_of(xr, 2, h), R.x_r.at[ph, i])
                rows = pl.ds(h * hr, hr)
                xs[slot, rows] = (xs[slot, rows].astype(F32) + xr[2, rows].astype(F32)).astype(BF)
                step_send(ph, 4 + i)

        def sum_arrived(ph):
            if square:
                for i in range(2, 6):
                    arrived(half_of(xr, 0, 0), R.x_r.at[ph, i])
            else:
                for k in range(1, tpn):
                    arrived(xr.at[k - 1], R.x_r.at[ph, k])

        def xs_sent(ph):
            if square:
                for i in range(6):
                    sent(half_of(xs, 0, 0), R.x_s.at[ph, i])
            else:
                for k in range(1, tpn):
                    sent(xs.at[k - 1], R.x_s.at[ph, k])

        def add_peers(rows):
            total = acc[rows]
            for k in range(2 if square else tpn - 1):
                total = total + xr[k, rows].astype(F32)
            return total

        def some_rows(buf, k, h):
            return buf.at[pl.ds(pl.multiple_of(source(k) * sr + h * hr, hr), hr)]

        def rows_copy(ph, buf, i, k, h, to):
            rows = some_rows(buf, k, h)
            return remote(rows, rows, R.g_s.at[ph, i], R.g_r.at[ph, i], dpi, peer(to))

        def rows_gather(ph, buf):
            if square:
                for i, (h, to) in enumerate(((0, 1), (1, 1), (1, 2), (0, 2))):
                    rows_copy(ph, buf, i, 0, h, to).start()
            else:
                mine = buf.at[own_rows]
                for k in range(1, tpn):
                    remote(mine, mine, R.g_s.at[ph, k], R.g_r.at[ph, k], dpi, peer(k)).start()

        def rows_relay(ph, buf):
            if square:
                arrived(some_rows(buf, 1, 0), R.g_r.at[ph, 0])
                rows_copy(ph, buf, 4, 1, 0, 2).start()
                arrived(some_rows(buf, 2, 1), R.g_r.at[ph, 2])
                rows_copy(ph, buf, 5, 2, 1, 1).start()

        def rows_arrived(ph, buf, k):
            if square:
                for j, h, i in ((1, 1, 1), (2, 0, 3), (3, 0, 4), (3, 1, 5)):

                    @when(k == j)
                    def _():
                        arrived(some_rows(buf, j, h), R.g_r.at[ph, i])
            else:

                @when(k > 0)
                def _():
                    arrived(buf.at[rows_of(source(k), sr)], R.g_r.at[ph, k])

            return rows_of(source(k), sr)

        def rows_sent(ph, buf):
            if square:
                for i in range(6):
                    sent(some_rows(buf, 0, 0), R.g_s.at[ph, i])
            else:
                for k in range(1, tpn):
                    sent(buf.at[own_rows], R.g_s.at[ph, k])

        def prepare(fq, fo, fg, fd, bq, bd):
            loads = [local(R.wq_f, fq, 8), local(R.wo_f, fo, 9)]
            loads += [local(R.wgu_f.at[:, h], fg.at[h], 10 + h) for h in range(2)]
            loads.append(local(R.wd_f, fd, 12))
            loads[0].wait()
            for m in range(3):
                bq[:, m * wl : (m + 1) * wl] = fq[m].astype(BF)
            local_now(bq, place(QKV, dpi))
            all_here()
            ag_near(QKV)
            for cp in loads[1:]:
                cp.wait()
            R.wo[:, rows_of(dpi, ds)] = fo[...].astype(BF)
            for lo, size, off in parts:
                for h in range(2):
                    to = off + h * size
                    R.wgu[rows_of(dpi, ds), to : to + size] = fg[h, :, lo : lo + size].astype(BF)
            bd[...] = fd[...].astype(BF)
            local_now(bd, place(DOWN, dpi))

        if cast:
            pl.run_scoped(
                prepare,
                pltpu.VMEM((3, ds, wl), F32),
                pltpu.VMEM((wl, ds), F32),
                pltpu.VMEM((2, ds, fl), F32),
                pltpu.VMEM((fl, ds), F32),
                pltpu.VMEM((ds, w3), BF),
                pltpu.VMEM((fl, ds), BF),
            )
        else:
            all_here()
            ag_near(QKV)

        load_x = local(R.x, R.h2, 1)
        load_y = local(R.cot, R.dt, 2)

        bs = R.bslot
        bs[z] = R.brow[...]
        for k in range(1, nc):
            remote(
                R.brow, bs.at[z], R.b_s.at[chip(k)], R.b_r.at[z], dp_of(chip(k)), t
            ).start()

        seg = jnp.broadcast_to(R.seg[...].astype(F32), (LANES, n)).T
        start = jnp.zeros((1, LANES), F32)
        lane = lax.broadcasted_iota(jnp.int32, (n, LANES), 1)
        first = jnp.zeros((n, LANES), F32)
        for v in range(4):
            here = jnp.sum(jnp.where(seg == float(v), 1.0, 0.0), axis=0, keepdims=True)
            first = jnp.where(seg == float(v), start, first)
            start = start + here
        pos = lax.broadcasted_iota(jnp.int32, (n, LANES), 0).astype(F32) - first
        angle = pos * R.freq[...]
        entry = lax.rem(lane, HD)
        cosine = jnp.cos(angle)
        sine = jnp.sin(angle)
        part = HD // 8
        R.tc[...] = jnp.where(entry < 2 * part, cosine, 1.0)
        R.ts[...] = jnp.where(entry < part, -sine, jnp.where(entry < 2 * part, sine, 0.0))
        same = seg == lane.astype(F32)
        R.kseg[...] = jnp.where(same, 1.0, 0.0).astype(BF)
        R.qseg[...] = jnp.where(same | (lane >= 4), 0.0, MASKED).astype(BF)

        lane_row = lax.broadcasted_iota(jnp.int32, (1, LANES), 1)
        def rotate(values, rows, sign):
            up = pltpu.roll(values, LANES - part, 1)
            down = pltpu.roll(values, part, 1)
            other = jnp.where(lane_row < part, up, down)
            other = jnp.where((lane_row >= HD) & (lane_row < HD + part), up, other)
            return values * R.tc[rows] + other * (R.ts[rows] * sign)

        head_mask = [
            jnp.where((lane_row >= h * HD) & (lane_row < (h + 1) * HD), 1.0, 0.0).astype(BF)
            for h in range(2)
        ]

        def gain(i):
            return R.norm[i : i + 1, :]

        def no_terms():
            if not has_via:
                return

            @when((z == 0) | (z == nc - 1))
            def _():
                other = nc - 1 - z
                R.box0[0] = jnp.zeros_like(R.box0[0])
                R.box1[0] = jnp.zeros_like(R.box1[0])
                fills = [
                    local(R.box0.at[0], R.zr0.at[other], 8),
                    local(R.box1.at[0, :, cols[0]], R.zr1.at[other], 9),
                    local(R.box1.at[0, :, cols[1]], R.zrb.at[other], 13),
                    local(R.box0.at[0, pl.ds(0, wl)], R.zr2.at[other], 10),
                ]
                for g in range(2):
                    fills.append(
                        local(R.box1.at[0, :, pl.ds(0, g3)], R.zrq.at[g, other], 11 + g)
                    )
                for cp in fills:
                    cp.wait()

        def project(h1, wq):
            ag_far(QKV)
            ag_near(OUT)
            load_x.wait()

            @pl.loop(0, n // lt)
            def _(i):
                rows = rows_of(i, lt)
                hat, _inv = normed(R.h2[rows].astype(F32))
                h1[rows] = (hat * gain(0) + gain(1)).astype(BF)

            keep = local(h1, R.sp_h1, 1)
            no_terms()
            for k in range(1, nc):
                arrived(bs.at[chip(k)], R.b_r.at[chip(k)])
            total = bs[0]
            for s in range(1, nc):
                total = total + bs[s]
            R.bsum[0] = total
            remote(R.bsum.at[0], R.bsum.at[1], R.b_s.at[nc], R.b_r.at[nc], sib, t).start()
            ag_rest(QKV)
            arrived(R.bsum.at[1], R.b_r.at[nc])
            ag_far(OUT)
            ag_near(GU0)
            ag_done(QKV)
            local_now(R.ag_q, wq)
            bias = (R.bsum[0] + R.bsum[1])[0:1]

            @pl.loop(0, n // qb)
            def _(i):
                rows = rows_of(i, qb)
                for m in range(3):
                    for lo, size in chunks(wl, 512):
                        at = m * wl + lo
                        got = dot_nn(h1[rows], wq[:, at : at + size]) + bias[:, at : at + size]
                        if m == 2:
                            R.qkv[rows, at : at + size] = got.astype(BF)
                        else:
                            for p in range(size // LANES):
                                R.qkv[rows, at + p * LANES : at + (p + 1) * LANES] = rotate(
                                    got[:, p * LANES : (p + 1) * LANES], rows, 1.0
                                ).astype(BF)

            keep.wait()

        def scores(p, i, h):
            length = (i + 1) * qb
            rows = pl.ds(i * qb, qb)
            qkv = R.qkv
            lanes = rows_of(p, LANES)
            klanes = pl.ds(pl.multiple_of(wl + p * LANES, LANES), LANES)
            keys = jnp.concatenate([qkv[0:length, klanes], R.kseg[0:length]], axis=1)
            query = qkv[rows, lanes] * head_mask[h] * jnp.asarray(scale, BF)
            s = dot_nt(keys, jnp.concatenate([query, R.qseg[rows]], axis=1))
            low = s[length - qb :]
            causal = lax.broadcasted_iota(jnp.int32, (qb, qb), 0) <= lax.broadcasted_iota(
                jnp.int32, (qb, qb), 1
            )
            low = jnp.where(causal, low, MASKED)
            s = low if i == 0 else jnp.concatenate([s[: length - qb], low], axis=0)
            return s, query

        def attend(p):
            qkv = R.qkv
            lanes = rows_of(p, LANES)
            vlanes = pl.ds(pl.multiple_of(2 * wl + p * LANES, LANES), LANES)
            vt = qkv[:, vlanes].T
            for i in range(nq):
                length = (i + 1) * qb
                outs = []
                for h in range(2):
                    s, _query = scores(p, i, h)
                    top = jnp.max(s, axis=0, keepdims=True)
                    expo = jnp.exp(s - top)
                    total = jnp.sum(expo, axis=0, keepdims=True)
                    mixed = dot_nn(vt[h * HD : (h + 1) * HD, 0:length], expo.astype(BF))
                    outs.append(mixed * (1.0 / total))
                    R.lse[p, h : h + 1, i * qb : (i + 1) * qb] = top + jnp.log(total)
                R.o[i * qb : (i + 1) * qb, lanes] = jnp.concatenate(outs, axis=0).T.astype(BF)

        pl.run_scoped(project, pltpu.VMEM((n, D), BF), pltpu.VMEM((D, w3), BF))

        @pl.loop(0, pairs)
        def _(p):
            attend(p)

        ag_rest(OUT)
        ag_far(GU0)
        ag_near(DOWN)
        ag_done(OUT)

        partial_rows(0, lambda rows: dot_nn(R.o[rows], R.wo[...]))
        sum_relay(0)
        sum_arrived(0)

        def norm_rows(xown):
            local_now(R.x.at[own_rows], xown)

            @pl.loop(0, sr // lt)
            def _(i):
                rows = rows_of(i, lt)
                resid = add_peers(rows) + xown[rows].astype(F32)
                acc[rows] = resid
                hat, _inv = normed(resid)
                R.h2[pl.ds(pl.multiple_of(t * sr + i * lt, lt), lt)] = (
                    hat * gain(2) + gain(3)
                ).astype(BF)

        pl.run_scoped(norm_rows, pltpu.VMEM((sr, D), BF))

        rows_gather(0, R.h2)
        local_now(acc, R.sp_r1)
        ag_rest(GU0)
        ag_far(DOWN)
        ag_done(GU0)
        rows_relay(0, R.h2)
        ag_rest(DOWN)
        ag_near(GU1)
        ag_done(DOWN)

        def feed(sp):
            def both_parts(at):
                def forward(i):
                    lo, size, off = parts[i]

                    def run(wd):
                        load = local(R.ag_d.at[pl.ds(lo, size)], wd, 1)
                        if i == 0:
                            load_y.wait()
                        load.wait()

                        @pl.loop(0, tpn)
                        def _(k):
                            if i == 0:

                                @when(k == 2)
                                def _():
                                    ag_hop(1)

                                rows = rows_arrived(0, R.h2, k)
                            else:
                                rows = rows_of(source(k), sr)
                            for at_col, width in chunks(size, 512):
                                gc = pl.ds(off + at_col, width)
                                uc = pl.ds(off + size + at_col, width)
                                g = dot_nn(R.h2[rows], R.wgu[:, gc])
                                u = dot_nn(R.h2[rows], R.wgu[:, uc])
                                da = dot_nt(R.dt[rows], wd[at_col : at_col + width])
                                sig = 1.0 / (1.0 + jnp.exp(-g))
                                act = g * sig
                                at[pl.ds(lo + at_col, width), rows] = (act * u).astype(BF).T
                                dg = da * u * sig * (1.0 + g * (1.0 - sig))
                                sp[rows, gc] = dg.astype(BF)
                                sp[rows, uc] = (da * act).astype(BF)

                    pl.run_scoped(run, pltpu.VMEM((size, D), BF))

                def gu_grad(i, u, pump):
                    _, size, off = parts[i]

                    def run(stage, mine):
                        def compute(j, put):
                            left = R.h2[:, rows_of(j, ds)].T
                            put(0, 2 * size, dot_nn(left, sp[:, off : off + 2 * size]))

                        rs_unit(u, compute, stage, mine, pump)

                    pl.run_scoped(
                        run, pltpu.VMEM((2, ds, 2 * size), BF), pltpu.VMEM((ds, 2 * size), F32)
                    )

                def down_grad(stage, mine):
                    def compute(j, put):
                        put(0, ds, dot_nn(at[...], R.dt[:, rows_of(j, ds)]))

                    rs_unit(RD, compute, stage, mine)

                forward(0)
                gu_grad(0, RGA, [(nc - 1, lambda: ag_hop(2))])
                for h in range(3, nc):
                    ag_hop(h)
                rs_rest(RGA)
                rs_via(RGA)
                ag_done(GU1)
                forward(1)
                keep = local(at, R.sp_a, 1)
                down = pltpu.VMEM((2, fl, ds), BF), pltpu.VMEM((fl, ds), F32)
                if not square:
                    pl.run_scoped(down_grad, *down)
                partial_rows(1, lambda rows: dot_nt(sp[rows], R.wgu[...]))
                if square:
                    pl.run_scoped(down_grad, *down)
                    sum_relay(1)
                gu_grad(1, RGB, ())
                keep.wait()

            pl.run_scoped(both_parts, pltpu.VMEM((fl, n), BF))

        pl.run_scoped(feed, pltpu.VMEM((n, f2), BF))
        rs_via(RD)
        rows_sent(0, R.h2)
        ag_hops_sent()
        for u in (GU0, GU1):
            ag_sent(u)
            ag_drain(u)
        load_h1 = local(R.sp_h1, R.h2, 6)
        load_wq = [
            local(
                R.ag_q.at[:, pl.ds(m * wl + g * gl, gl)],
                R.wgu.at[:, pl.ds(g * g3 + m * gl, gl)],
                16 + nc + 3 * g + m,
            )
            for g in range(2)
            for m in range(3)
        ]

        def norm_two(r1, yown):
            one = local(R.cot.at[own_rows], yown, 1)
            local_now(R.sp_r1, r1)
            one.wait()
            sum_arrived(1)
            R.gsum[...] = jnp.zeros_like(R.gsum)

            @pl.loop(0, sr // lt)
            def _(i):
                rows = rows_of(i, lt)
                grad = add_peers(rows)
                hat, inv = normed(r1[rows])
                out = yown[rows].astype(F32) + norm_back(grad, hat, inv, gain(2))
                acc[rows] = out
                R.dt[pl.ds(pl.multiple_of(t * sr + i * lt, lt), lt)] = out.astype(BF)
                R.gsum[2:3] += jnp.sum(grad * hat, axis=0, keepdims=True)
                R.gsum[3:4] += jnp.sum(grad, axis=0, keepdims=True)

            rows_gather(1, R.dt)
            local_now(acc, R.sp_dr1)

        pl.run_scoped(norm_two, pltpu.VMEM((sr, D), F32), pltpu.VMEM((sr, D), BF))

        load_h1.wait()
        if turned:

            @pl.loop(0, n // qb)
            def _(i):
                R.wgu[:, pl.ds(pl.multiple_of(w3 + i * qb, LANES), qb)] = R.h2[rows_of(i, qb)].T

            free_signal(0)

        rows_relay(1, R.dt)

        def mlp_out(a, wd, out, own):
            local_now(R.ag_d, wd)

            @pl.loop(1, tpn + 1)
            def _(k):
                local_now(R.sp_a.at[:, rows_of(peer(k), sr)], a)
                value = dot_nn(a[...].T, wd[...])

                @when(k < tpn)
                def _():
                    out[...] = value.astype(BF)
                    local_now(out, R.mlp_p.at[k - 1])

                @when(k == tpn)
                def _():
                    own[...] = value
                    local_now(own, R.sp_mlp)

        pl.run_scoped(
            mlp_out,
            pltpu.VMEM((fl, sr), BF),
            pltpu.VMEM((fl, D), BF),
            pltpu.VMEM((sr, D), BF),
            pltpu.VMEM((sr, D), F32),
        )

        if not turned:
            rs_drain(RD)
            free_signal(0)

        def attention_back(dp):
            def back(do, dk, dv):
                @pl.loop(0, tpn)
                def _(k):
                    rows = rows_arrived(1, R.dt, k)
                    do[rows] = dot_nt(R.dt[rows], R.wo[...]).astype(BF)

                for k in range(1, tpn):
                    x_send(3, k, R.mlp_p.at[k - 1], R.mlp_r.at[k - 1])

                rs_via(RGB)

                def out_grad(ot, stage, mine):
                    ot[...] = R.o[...].T

                    def compute(j, put):
                        put(0, ds, dot_nn(ot[...], R.dt[:, rows_of(j, ds)]))

                    pl.semaphore_wait(R.free.at[0], 1)
                    rs_unit(RO, compute, stage, mine)

                pl.run_scoped(
                    out_grad,
                    pltpu.VMEM((wl, n), BF),
                    pltpu.VMEM((2, wl, ds), BF),
                    pltpu.VMEM((wl, ds), F32),
                )

                rs_rest(RO)
                rows_sent(1, R.dt)
                free_signal(1)
                for copy in load_wq:
                    copy.wait()

                def pair_back(g, own):
                    qkv = R.qkv
                    p = g * (pairs // 2) + own
                    lanes = rows_of(p, LANES)
                    klanes = pl.ds(pl.multiple_of(wl + p * LANES, LANES), LANES)
                    vlanes = pl.ds(pl.multiple_of(2 * wl + p * LANES, LANES), LANES)

                    def out_lanes(m):
                        return pl.ds(pl.multiple_of(g * g3 + m * gl + own * LANES, LANES), LANES)

                    kt = qkv[:, klanes].T
                    dk[...] = jnp.zeros_like(dk)
                    dv[...] = jnp.zeros_like(dv)
                    for i in range(nq):
                        length = (i + 1) * qb
                        rows = pl.ds(i * qb, qb)
                        pbs, dss, qms, doms, dqs = [], [], [], [], []
                        for h in range(2):
                            s, query = scores(p, i, h)
                            prob = jnp.exp(s - R.lse[p, h : h + 1, i * qb : (i + 1) * qb])
                            dom = do[rows, lanes] * head_mask[h]
                            dprob = dot_nt(qkv[0:length, vlanes], dom)
                            weighted = jnp.sum(prob * dprob, axis=0, keepdims=True)
                            dsc = (prob * (dprob - weighted)).astype(BF)
                            pbs.append(prob.astype(BF))
                            dss.append(dsc)
                            qms.append(query)
                            doms.append(dom)
                            dqs.append(dot_nn(kt[h * HD : (h + 1) * HD, 0:length], dsc))
                        dv[0:length] += dot_nn(
                            jnp.concatenate(pbs, axis=1), jnp.concatenate(doms, axis=0)
                        )
                        dk[0:length] += dot_nn(
                            jnp.concatenate(dss, axis=1), jnp.concatenate(qms, axis=0)
                        )
                        dq = jnp.concatenate(dqs, axis=0).T * scale
                        dp[rows, out_lanes(0)] = rotate(dq, rows, -1.0).astype(BF)
                    dp[:, out_lanes(1)] = rotate(dk[...], pl.ds(0, n), -1.0).astype(BF)
                    dp[:, out_lanes(2)] = dv[...].astype(BF)

                @pl.loop(0, 2)
                def _(g):
                    @pl.loop(0, pairs // 2)
                    def _(own):
                        pair_back(g, own)

                    @when(g == 0)
                    def _():
                        rs_via(RO)
                        pl.semaphore_wait(R.free.at[1], 1)

                    @when(g == 1)
                    def _():
                        rs_via(RQ(0))
                        partial_rows(2, lambda rows: dot_nt(dp[rows], R.wgu[:, 0:w3]))

                    def qkv_grad(stage, mine):
                        def compute(j, put):
                            if turned:
                                left = R.wgu[rows_of(j, ds), w3 : w3 + n]
                            else:
                                left = R.h2[:, rows_of(j, ds)].T
                            put(0, g3, dot_nn(left, dp[:, rows_of(g, g3)]))

                        rs_unit(RQ(g), compute, stage, mine)

                    pl.run_scoped(qkv_grad, pltpu.VMEM((2, ds, g3), BF), pltpu.VMEM((ds, g3), F32))
                    rs_rest(RQ(g))

            pl.run_scoped(
                back,
                pltpu.VMEM((n, wl), BF),
                pltpu.VMEM((n, LANES), F32),
                pltpu.VMEM((n, LANES), F32),
            )
            sums = jnp.zeros((1, w3), F32)
            for i in range(n // qb):
                sums = sums + jnp.sum(
                    dp[i * qb : (i + 1) * qb].astype(F32), axis=0, keepdims=True
                )
            R.gbs[0] = jnp.broadcast_to(sums, (8, w3))
            remote(R.gbs.at[0], R.gbs.at[1], R.c_s.at[nc], R.c_r.at[nc], sib, t).start()


        pl.run_scoped(attention_back, pltpu.VMEM((n, w3), BF))

        arrived(R.gbs.at[1], R.c_r.at[nc])
        cslot = R.cslot
        cslot[z] = R.gbs[0] + R.gbs[1]
        for k in range(1, nc):
            remote(
                cslot.at[z], cslot.at[z], R.c_s.at[chip(k)], R.c_r.at[z], dp_of(chip(k)), t
            ).start()

        sum_relay(2)

        def block_rows(r1, own, got, out):
            a = local(R.sp_r1, r1, 1)
            b = local(R.sp_mlp, own, 2)
            for k in range(1, tpn):
                arrived(R.mlp_r.at[k - 1], R.x_r.at[3, k])
            local_now(R.mlp_r, got)
            a.wait()
            b.wait()

            @pl.loop(0, sr // lt)
            def _(i):
                rows = rows_of(i, lt)
                total = own[rows]
                for k in range(1, tpn):
                    total = total + got[k - 1, rows].astype(F32)
                out[rows] = (r1[rows] + total).astype(BF)

            local_now(out, R.block_out)

        pl.run_scoped(
            block_rows,
            pltpu.VMEM((sr, D), F32),
            pltpu.VMEM((sr, D), F32),
            pltpu.VMEM((tpn - 1, sr, D), BF),
            pltpu.VMEM((sr, D), BF),
        )

        rs_via(RQ(1))

        def norm_one(dr1, xown):
            one = local(R.x.at[own_rows], xown, 1)
            local_now(R.sp_dr1, dr1)
            one.wait()
            sum_arrived(2)

            @pl.loop(0, sr // lt)
            def _(i):
                rows = rows_of(i, lt)
                grad = add_peers(rows)
                hat, inv = normed(xown[rows].astype(F32))
                dr1[rows] = dr1[rows] + norm_back(grad, hat, inv, gain(0))
                R.gsum[0:1] += jnp.sum(grad * hat, axis=0, keepdims=True)
                R.gsum[1:2] += jnp.sum(grad, axis=0, keepdims=True)

            keep = local(dr1, R.input_grad, 1)
            ns = R.nsum
            ns[0, 0:4] = R.gsum[0:4, 0 : D // 2]
            ns[0, 4:8] = R.gsum[0:4, D // 2 :]
            remote(ns.at[0], ns.at[1], R.n_s.at[0], R.n_r.at[0], sib, t).start()
            arrived(ns.at[1], R.n_r.at[0])
            zs = R.nz
            zs[z] = ns[0] + ns[1]
            for k in range(1, nc):
                remote(
                    zs.at[z], zs.at[z], R.n_s.at[k], R.n_r.at[1 + z], dp_of(chip(k)), t
                ).start()
            for k in range(1, nc):
                arrived(zs.at[chip(k)], R.n_r.at[1 + chip(k)])
            total = zs[0]
            for s in range(1, nc):
                total = total + zs[s]
            ts = R.nt
            ts[t] = total
            for k in range(1, tpn):
                remote(
                    ts.at[t], ts.at[t], R.n_s.at[nc + k], R.n_r.at[1 + nc + t], dpi, peer(k)
                ).start()
            for k in range(1, tpn):
                arrived(ts.at[peer(k)], R.n_r.at[1 + nc + peer(k)])
            total = ts[0]
            for s in range(1, tpn):
                total = total + ts[s]
            R.gn[...] = total
            keep.wait()

        pl.run_scoped(norm_one, pltpu.VMEM((sr, D), F32), pltpu.VMEM((sr, D), BF))

        for k in range(1, nc):
            arrived(cslot.at[chip(k)], R.c_r.at[chip(k)])
        total = cslot[0]
        for s in range(1, nc):
            total = total + cslot[s]
        R.gb[...] = total

        for u in (RD, RGA, RGB, RO, RQ(0), RQ(1)):
            rs_arrived(u)

        for u in (QKV, OUT, DOWN):
            ag_sent(u)
        for u in (QKV, OUT, DOWN):
            ag_drain(u)
        for u in ([RD] if turned else []) + [RGA, RGB, RO, RQ(0), RQ(1)]:
            rs_drain(u)
        xs_sent(2)
        for k in range(1, tpn):
            sent(R.mlp_p.at[k - 1], R.x_s.at[3, k])
            sent(R.nt.at[0], R.n_s.at[nc + k])
        for k in range(1, nc):
            sent(R.brow, R.b_s.at[chip(k)])
            sent(cslot.at[0], R.c_s.at[chip(k)])
            sent(R.nz.at[0], R.n_s.at[k])
        sent(R.bsum.at[0], R.b_s.at[nc])
        sent(R.gbs.at[0], R.c_s.at[nc])
        sent(R.nsum.at[0], R.n_s.at[0])

    return kern


def fused(x, seg, cot, norm, brow, freq, weights, dpn, tpn, cast):
    n = x.shape[0]
    wl = weights[1].shape[0]
    fl = weights[3].shape[0]
    nc = dpn // 2
    ds = D // dpn
    sr = n // tpn
    w3, f2 = 3 * wl, 2 * fl
    pairs = wl // LANES
    g3 = 3 * (wl // 2)
    hbm = pl.BlockSpec(memory_space=pl.ANY)
    vmem = pl.BlockSpec(memory_space=pltpu.VMEM)
    ins = [
        ("x", hbm),
        ("seg", vmem),
        ("cot", hbm),
        ("norm", vmem),
        ("brow", vmem),
        ("freq", vmem),
    ]
    shards = ["wq_s", "wo_s", "wgu_s", "wd_s"]
    ins += [(i, hbm) for i in (["wq_f", "wo_f", "wgu_f", "wd_f"] if cast else shards)]
    parts = hidden_parts(fl)
    boxes = [(fl, ds), (ds, 2 * parts[0][1]), (wl, ds)]
    last = (ds, 2 * parts[1][1])
    outs = [
        ("block_out", (sr, D), BF, hbm),
        ("input_grad", (sr, D), F32, hbm),
        ("gn", (8, D // 2), F32, vmem),
        ("gb", (8, w3), F32, vmem),
    ]
    outs += [("zr%d" % u, (nc,) + s, BF, hbm) for u, s in enumerate(boxes)]
    outs += [("zrq", (2, nc, ds, g3), BF, hbm), ("zrb", (nc,) + last, BF, hbm)]
    outs += [("vrq", (2, 2, ds, g3), BF, hbm), ("vrb", (2,) + last, BF, hbm)]
    outs += [
        ("ag_q", (D, w3), BF, hbm),
        ("ag_d", (fl, D), BF, hbm),
        ("mlp_p", (tpn - 1, sr, D), BF, hbm),
        ("mlp_r", (tpn - 1, sr, D), BF, hbm),
        ("sp_h1", (n, D), BF, hbm),
        ("sp_a", (fl, n), BF, hbm),
        ("sp_r1", (sr, D), F32, hbm),
        ("sp_mlp", (sr, D), F32, hbm),
        ("sp_dr1", (sr, D), F32, hbm),
    ]
    outs += [("vr%d" % u, (2,) + s, BF, hbm) for u, s in enumerate(boxes)]
    dma = pltpu.SemaphoreType.DMA
    scratch = [
        ("wgu", pltpu.VMEM((D, f2), BF)),
        ("wo", pltpu.VMEM((wl, D), BF)),
        ("h2", pltpu.VMEM((n, D), BF)),
        ("dt", pltpu.VMEM((n, D), BF)),
        ("xs", pltpu.VMEM((tpn - 1, sr, D), BF)),
        ("xr", pltpu.VMEM((tpn - 1, sr, D), BF)),
        ("acc", pltpu.VMEM((sr, D), F32)),
        ("qkv", pltpu.VMEM((n, w3), BF)),
        ("o", pltpu.VMEM((n, wl), BF)),
        ("tc", pltpu.VMEM((n, LANES), F32)),
        ("ts", pltpu.VMEM((n, LANES), F32)),
        ("kseg", pltpu.VMEM((n, LANES), BF)),
        ("qseg", pltpu.VMEM((n, LANES), BF)),
        ("lse", pltpu.VMEM((pairs, 2, n), F32)),
        ("bslot", pltpu.VMEM((nc, 8, w3), F32)),
        ("bsum", pltpu.VMEM((2, 8, w3), F32)),
        ("gbs", pltpu.VMEM((2, 8, w3), F32)),
        ("cslot", pltpu.VMEM((nc, 8, w3), F32)),
        ("gsum", pltpu.VMEM((8, D), F32)),
        ("nsum", pltpu.VMEM((2, 8, D // 2), F32)),
        ("nz", pltpu.VMEM((nc, 8, D // 2), F32)),
        ("nt", pltpu.VMEM((tpn, 8, D // 2), F32)),
    ]
    scratch += [("box0", pltpu.VMEM((nc, fl, ds), BF)), ("box1", pltpu.VMEM((nc, ds, f2), BF))]
    scratch += [
        ("dum", dma((1,))),
        ("loc", dma((27 + nc,))),
        ("self", dma((6,))),
        ("hop", dma((nc, 2))),
        ("free", pltpu.SemaphoreType.REGULAR((2,))),
        ("ag_s", dma((5, nc))),
        ("ag_r", dma((5, nc))),
        ("av_s", dma((5, 2))),
        ("sb_s", dma((5, nc))),
        ("sb_r", dma((5, nc))),
        ("rb_s", dma((6, nc))),
        ("rb_r", dma((6, nc))),
        ("rz_s", dma((6, nc))),
        ("rz_r", dma((6, nc))),
        ("rv_r", dma((6, 2))),
        ("x_s", dma((4, max(tpn, 6)))),
        ("x_r", dma((4, max(tpn, 6)))),
        ("g_s", dma((2, max(tpn, 6)))),
        ("g_r", dma((2, max(tpn, 6)))),
        ("b_s", dma((nc + 1,))),
        ("b_r", dma((nc + 1,))),
        ("c_s", dma((nc + 1,))),
        ("c_r", dma((nc + 1,))),
        ("n_s", dma((nc + tpn,))),
        ("n_r", dma((1 + nc + tpn,))),
    ]
    names = [i[0] for i in ins] + [o[0] for o in outs] + [s[0] for s in scratch]
    got = pl.pallas_call(
        make_kernel(names, n, wl, fl, dpn, tpn, cast),
        out_shape=[jax.ShapeDtypeStruct(s, d) for _, s, d, _ in outs],
        in_specs=[s for _, s in ins],
        out_specs=[m for _, _, _, m in outs],
        scratch_shapes=[s for _, s in scratch],
        compiler_params=pltpu.CompilerParams(
            collective_id=0, has_side_effects=True, vmem_limit_bytes=63 * 2**20
        ),
        name="block_step",
    )(x, seg, cot, norm, brow, freq, *weights)
    return got[:9]


def adamw(weight, first, second, grad, rate, decay):
    new_first = BETA_ONE * first + (1.0 - BETA_ONE) * grad
    new_second = BETA_TWO * second + (1.0 - BETA_TWO) * grad * grad
    direction = (
        new_first
        / (1.0 - BETA_ONE**STEP)
        / (jnp.sqrt(new_second / (1.0 - BETA_TWO**STEP)) + ADAM_EPS)
    )
    return (new_first, new_second, weight - rate * (direction + decay * weight))


def update_all(groups, norm_grad, norm_state, passed):
    hbm = pl.BlockSpec(memory_space=pl.ANY)
    f32 = lambda s: pltpu.VMEM(s, F32)
    n_groups = len(groups)
    scratch = []
    for grads, _, _, _, pieces, _ in groups:
        scratch += [pltpu.VMEM(grad.shape, BF) for grad in grads]
        scratch += [f32(piece[2]) for piece in pieces for _ in range(3)]
    n_scratch = len(scratch)
    n_arrays = sum(len(g[0]) + 3 for g in groups)
    count = sum(len(g[0]) + 6 * len(g[4]) for g in groups) + 7 + 2 * len(passed)
    scratch += [f32(norm_grad.shape)] + [f32(x.shape) for x in norm_state]
    scratch += [pltpu.VMEM(x.shape, x.dtype) for x in passed]

    def kern(*refs):
        n_ins = n_arrays + 4 + len(passed)
        n_outs = 3 * n_groups + 3 + len(passed)
        ins, outs = refs[:n_ins], refs[n_ins : n_ins + n_outs]
        bufs, sem = refs[n_ins + n_outs : -1], refs[-1]
        at = iter(range(count))
        loads, plan = [], []

        def start(src, dst):
            cp = pltpu.make_async_copy(src, dst, sem.at[next(at)])
            cp.start()
            return cp

        arrays, spaces = iter(ins[:n_arrays]), iter(bufs[:n_scratch])
        for i, (grads, _, _, _, pieces, rate) in enumerate(groups):
            terms = [next(spaces) for _ in grads]
            got = [start(next(arrays), space) for space in terms]
            whole = [next(arrays) for _ in range(3)]
            state = []
            for _, state_part, _ in pieces:
                state.append([next(spaces) for _ in range(3)])
                got += [start(state_part(a), b) for a, b in zip(whole, state[-1], strict=True)]
            plan.append((got, terms, state, pieces, rate, outs[3 * i : 3 * i + 3]))
        rest = bufs[n_scratch:]
        small = [start(a, b) for a, b in zip(ins[n_arrays:], rest, strict=True)]
        stores = []
        for got, g, state, pieces, rate, dst in plan:
            for cp in got:
                cp.wait()
            for j, (grad_part, state_part, (rows, cols)) in enumerate(pieces):
                step = 64 if cols <= 512 else 16
                terms = grad_part(g)
                w, m, v = state[j]

                @pl.loop(0, rows // step)
                def _(r):
                    at_rows = pl.ds(pl.multiple_of(r * step, step), step)
                    grad = terms[0][at_rows, :].astype(F32)
                    for term in terms[1:]:
                        grad = grad + term[at_rows, :].astype(F32)
                    first, second, new = adamw(
                        w[at_rows, :], m[at_rows, :], v[at_rows, :], grad, rate, DECAY
                    )
                    m[at_rows, :] = first
                    v[at_rows, :] = second
                    w[at_rows, :] = new

                for k, buf in enumerate((m, v, w)):
                    stores.append(start(buf, state_part(dst[k])))
        for cp in small:
            cp.wait()
        g, w, m, v = rest[:4]
        half = w.shape[1] // 2
        for h in range(2):
            cols = slice(h * half, (h + 1) * half)
            first, second, new = adamw(
                w[:, cols], m[:, cols], v[:, cols], g[4 * h : 4 * h + 4], 0.5, 0.0
            )
            m[:, cols] = first
            v[:, cols] = second
            w[:, cols] = new
        for a, b in zip(
            (m, v, w) + tuple(rest[4:]), outs[3 * n_groups :], strict=True
        ):
            stores.append(start(a, b))
        for cp in stores:
            cp.wait()

    out_shape = []
    flat = []
    for grads, weight, first, second, _, _ in groups:
        flat += [*grads, weight, first, second]
        out_shape += [jax.ShapeDtypeStruct(weight.shape, F32)] * 3
    flat += [norm_grad, *norm_state, *passed]
    out_shape += [jax.ShapeDtypeStruct(x.shape, x.dtype) for x in (*norm_state, *passed)]
    got = pl.pallas_call(
        kern,
        out_shape=out_shape,
        in_specs=[hbm] * len(flat),
        out_specs=[hbm] * len(out_shape),
        scratch_shapes=scratch + [pltpu.SemaphoreType.DMA((count,))],
        compiler_params=pltpu.CompilerParams(vmem_limit_bytes=56 * 2**20),
        name="adamw",
    )(*flat)
    return [tuple(got[3 * i : 3 * i + 3]) for i in range(n_groups + 1)], got[3 * n_groups + 3 :]


def body(
    tokens,
    segments,
    cotangent,
    norm_params,
    norm_m,
    norm_v,
    qkv_bias,
    bias_m,
    bias_v,
    w_qkv,
    qkv_m,
    qkv_v,
    w_out,
    out_m,
    out_v,
    w_gateup,
    gateup_m,
    gateup_v,
    w_down,
    down_m,
    down_v,
):
    n_rows, model = tokens.shape
    dpn = lax.axis_size("dp")
    tpn = lax.axis_size("tensor")
    ds, _, wl = w_qkv.shape
    fl = w_down.shape[0]
    pad = -fl % LANES
    heads, cut = qkv_bias.shape[1:]
    assert segments.shape[0] == 1 and model == D
    me = lax.axis_index("dp")

    bias = qkv_bias.astype(BF).astype(F32)
    wide = lax.dynamic_update_slice(jnp.zeros((3, heads, HD), F32), bias, (0, 0, me * cut))
    brow = jnp.broadcast_to(wide.reshape(1, 3 * wl), (8, 3 * wl))
    part = HD // 8
    freq = ROPE_BASE ** (-2.0 * (np.arange(LANES) % part) / (HD // 4))
    freq = jnp.asarray(freq.reshape(1, LANES), F32)
    cast = not pad
    parts = hidden_parts(fl + pad)
    if cast:
        weights = (jnp.transpose(w_qkv, (1, 0, 2)), w_out, w_gateup, w_down)
    else:
        wgu = jnp.pad(w_gateup.astype(BF), ((0, 0), (0, 0), (0, pad)))
        weights = (
            w_qkv.astype(BF).reshape(ds, 3 * wl),
            w_out.astype(BF),
            jnp.concatenate(
                [wgu[:, :, lo : lo + size].reshape(ds, 2 * size) for lo, size, _ in parts], axis=1
            ),
            jnp.pad(w_down.astype(BF), ((0, pad), (0, 0))),
        )
    block_out, input_grad, gn, gb, red_down, red_gu, red_out, red_qkv, red_gub = fused(
        tokens, segments, cotangent, norm_params, brow, freq, weights, dpn, tpn, cast
    )
    red_bias = jnp.swapaxes(gb[0].reshape(2, 3, wl // 2), 0, 1).reshape(3, heads, HD)
    red_bias = lax.dynamic_slice(red_bias, (0, 0, me * cut), (3, heads, cut))
    gl = wl // 2
    nc = dpn // 2
    qkv_pieces = [
        (
            lambda r, g=g, m=m: [r[0].at[g, s, :, pl.ds(m * gl, gl)] for s in range(nc)],
            lambda r, g=g, m=m: r.at[m, :, pl.ds(g * gl, gl)],
            (ds, gl),
        )
        for g in range(2)
        for m in range(3)
    ]
    whole = lambda r: r
    every = lambda r: [r[0].at[s] for s in range(nc)]

    def turn(x):
        return jnp.transpose(x, (1, 0, 2))

    groups = [
        ((red_qkv,), turn(w_qkv), turn(qkv_m), turn(qkv_v), qkv_pieces, D ** (-0.5)),
        ((red_out,), w_out, out_m, out_v, [(every, whole, w_out.shape)], HD ** (-0.5)),
    ]
    if not pad:
        gu_pieces = [
            (
                lambda r, i=i, h=h, c=size: [r[i].at[s, :, pl.ds(h * c, c)] for s in range(nc)],
                lambda r, h=h, lo=lo, c=size: r.at[:, h, pl.ds(lo, c)],
                (ds, size),
            )
            for i, (lo, size, _) in enumerate(parts)
            for h in range(2)
        ]
        groups += [
            ((red_gu, red_gub), w_gateup, gateup_m, gateup_v, gu_pieces, D ** (-0.5)),
            ((red_down,), w_down, down_m, down_v, [(every, whole, w_down.shape)], FF ** (-0.5)),
        ]
    done, (block_out, input_grad) = update_all(
        groups, gn, (norm_params, norm_m, norm_v), (block_out, input_grad)
    )
    new_norm = done.pop()
    new_qkv = tuple(turn(x) for x in done[0])
    if pad:
        both = [
            jnp.sum(r, axis=0, dtype=F32).reshape(ds, 2, size)
            for r, (_, size, _) in zip((red_gu, red_gub), parts, strict=True)
        ]
        red_gu = jnp.concatenate(both, axis=2)[:, :, :fl]
        red_down = jnp.sum(red_down, axis=0, dtype=F32)[:fl]
        done += [
            adamw(w_gateup, gateup_m, gateup_v, red_gu, D ** (-0.5), DECAY),
            adamw(w_down, down_m, down_v, red_down, FF ** (-0.5), DECAY),
        ]
    return (
        (block_out, input_grad)
        + new_norm
        + adamw(qkv_bias, bias_m, bias_v, red_bias, 0.3, 0.0)
        + new_qkv
        + done[1]
        + done[2]
        + done[3]
    )


def solution(mesh):
    rows = P("dp", None)
    bias = P(None, "tensor", "dp")
    wide = P("dp", None, "tensor")
    tall = P("tensor", "dp")
    split = P(("dp", "tensor"), None)
    return jax.shard_map(
        body,
        mesh=mesh,
        in_specs=(rows,) * 3 + (P(),) * 3 + (bias,) * 3 + (wide,) * 3 + (tall,) * 3 + (wide,) * 3
        + (tall,) * 3,
        out_specs=(split,) * 2 + (P(),) * 3 + (bias,) * 3 + (wide,) * 3 + (tall,) * 3 + (wide,) * 3
        + (tall,) * 3,
        check_vma=False,
    )
```

```python
from types import SimpleNamespace

import numpy as np
import jax
import jax.numpy as jnp
from jax import lax
from jax.experimental import pallas as pl
from jax.experimental.pallas import tpu as pltpu
from jax.sharding import PartitionSpec as P

D = 2048
HD = 64
FF = 5632
STEP = 10

NORM_EPS = 1e-05
BETA_ONE = 0.9
BETA_TWO = 0.95
ADAM_EPS = 1e-08
DECAY = 0.1
ROPE_BASE = 10000.0

BF = jnp.bfloat16
F32 = jnp.float32
MESH = pl.DeviceIdType.MESH
LANES = 128
MASKED = -1e30

QKV, OUT, GU0, GU1, DOWN = range(5)


def dot_nn(a, b):
    return lax.dot_general(a, b, (((1,), (0,)), ((), ())), preferred_element_type=F32)


def dot_nt(a, b):
    return lax.dot_general(a, b, (((1,), (1,)), ((), ())), preferred_element_type=F32)


def dot_tn(a, b):
    return lax.dot_general(a, b, (((0,), (0,)), ((), ())), preferred_element_type=F32)


def chunks(total, step):
    return [(lo, min(step, total - lo)) for lo in range(0, total, step)]


def hidden_parts(fl):
    size = (fl // LANES + 1) // 2 * LANES
    return ((0, size, 0), (size, fl - size, 2 * size))


def normed(values):
    centre = values - jnp.mean(values, axis=1, keepdims=True)
    inv = lax.rsqrt(jnp.mean(centre * centre, axis=1, keepdims=True) + NORM_EPS)
    return centre * inv, inv


def norm_back(grad, hat, inv, gain):
    e = grad * gain
    return inv * (
        e - jnp.mean(e, axis=1, keepdims=True) - hat * jnp.mean(e * hat, axis=1, keepdims=True)
    )


def make_kernel(names, n, wl, fl, dpn, tpn, cast):
    nc = dpn // 2
    ds = D // dpn
    sr = n // tpn
    w3 = 3 * wl
    f2 = 2 * fl
    parts = hidden_parts(fl)
    cols = [pl.ds(off, 2 * size) for _, size, off in parts]
    qb = min(256, n)
    nq = n // qb
    rt = min(256, sr)
    lt = min(128, sr)
    pairs = wl // LANES
    gl = wl // 2
    g3 = 3 * gl
    hr = sr // 2
    square = tpn == 4
    turned = w3 + n <= f2
    scale = HD ** (-0.5)
    has_via = nc >= 3

    def kern(*refs):
        R = SimpleNamespace(**dict(zip(names, refs, strict=True)))
        dpi = lax.axis_index("dp")
        t = lax.axis_index("tensor")
        z = lax.div(dpi, 2)
        c = lax.rem(dpi, 2)
        oc = 1 - c
        sib = dpi + 1 - 2 * c

        def chip(k):
            return lax.rem(z + k, nc)

        def dp_of(s):
            return 2 * s + c

        def flip(i, k):
            return lax.rem(i + k, 2) + 2 * lax.rem(lax.div(i, 2) + lax.div(k, 2), 2)

        def peer(k):
            k = jnp.asarray(k, jnp.int32)
            return flip(t, k) if square else lax.rem(t + k, tpn)

        def source(k):
            k = jnp.asarray(k, jnp.int32)
            return flip(t, k) if square else lax.rem(t + tpn - k, tpn)

        def remote(src, dst, ss, rs, dp, tn):
            return pltpu.make_async_remote_copy(
                src_ref=src,
                dst_ref=dst,
                send_sem=ss,
                recv_sem=rs,
                device_id=(dp, tn),
                device_id_type=MESH,
            )

        def arrived(dst, rs):
            remote(dst, dst, R.dum.at[0], rs, sib, t).wait_recv()

        def sent(src, ss):
            remote(src, src, ss, R.dum.at[0], sib, t).wait_send()

        def local(src, dst, i):
            cp = pltpu.make_async_copy(src, dst, R.loc.at[i])
            cp.start()
            return cp

        def local_now(src, dst):
            local(src, dst, 0).wait()

        def rows_of(i, size):
            return pl.ds(pl.multiple_of(i * size, size), size)

        own_rows = rows_of(t, sr)

        bar = pltpu.get_barrier_semaphore()
        pl.semaphore_signal(bar, inc=1, device_id=(sib, t), device_id_type=MESH)
        for k in range(1, nc):
            pl.semaphore_signal(bar, inc=1, device_id=(dp_of(chip(k)), t), device_id_type=MESH)
        for k in range(1, tpn):
            pl.semaphore_signal(bar, inc=1, device_id=(dpi, peer(k)), device_id_type=MESH)

        def all_here():
            pl.semaphore_wait(bar, 1 + (nc - 1) + (tpn - 1))

        def shard(u):
            if cast:
                return place(u, dpi)
            return {
                QKV: lambda: R.wq_s,
                OUT: lambda: R.wo_s,
                GU0: lambda: R.wgu_s.at[:, cols[0]],
                GU1: lambda: R.wgu_s.at[:, cols[1]],
                DOWN: lambda: R.wd_s,
            }[u]()

        def place(u, j):
            return {
                QKV: lambda: R.ag_q.at[rows_of(j, ds)],
                OUT: lambda: R.wo.at[:, rows_of(j, ds)],
                GU0: lambda: R.wgu.at[rows_of(j, ds), cols[0]],
                GU1: lambda: R.wgu.at[rows_of(j, ds), cols[1]],
                DOWN: lambda: R.ag_d.at[:, rows_of(j, ds)],
            }[u]()

        def relayed(src, dst):
            if not has_via:
                return src != src
            return ((src == 2) & (dst == 0)) | ((src == nc - 3) & (dst == nc - 1))

        def when(cond):
            return pl.when(cond)

        def within(s):
            return (s >= 0) & (s < nc)

        def apart(s):
            return (s - z >= 2) | (z - s >= 2)

        relays = ((1, 2, 0), (nc - 2, nc - 3, nc - 1)) if has_via else ()

        def ag_copy(u, d):
            return remote(
                shard(u), place(u, dpi), R.ag_s.at[u, d], R.ag_r.at[u, z], dp_of(d), t
            )

        def ag_near(u):
            for d in (z + 1, z - 1):

                @when(within(d))
                def _():
                    ag_copy(u, d).start()

            remote(shard(u), place(u, dpi), R.sb_s.at[u, z], R.sb_r.at[u, z], sib, t).start()
            if not cast:
                local(shard(u), place(u, dpi), 22 + nc + u)

        def to_sibling(u, s):
            here = place(u, dp_of(s))
            remote(here, here, R.sb_s.at[u, s], R.sb_r.at[u, s], sib, t).start()

        def ag_far(u):
            for s in (z + 1, z - 1):

                @when(within(s))
                def _():
                    arrived(place(u, dp_of(s)), R.ag_r.at[u, s])

            for i, (mid, src, dst) in enumerate(relays):

                @when(z == mid)
                def _():
                    here = place(u, dp_of(src))
                    remote(
                        here, here, R.av_s.at[u, i], R.ag_r.at[u, src], dp_of(dst), t
                    ).start()

            for d in range(nc):

                @when(apart(d) & jnp.logical_not(relayed(z, d)))
                def _():
                    ag_copy(u, d).start()

            for s in (z + 1, z - 1):

                @when(within(s))
                def _():
                    to_sibling(u, s)

        def ag_rest(u):
            for s in range(nc):

                @when(apart(s))
                def _():
                    arrived(place(u, dp_of(s)), R.ag_r.at[u, s])
                    to_sibling(u, s)

        def ag_sent(u):
            for d in range(nc):
                far = apart(d) if u == GU1 else relayed(z, d)

                @when((z != d) & jnp.logical_not(far))
                def _():
                    sent(shard(u), R.ag_s.at[u, d])

        def ag_hop(h):
            for i, way in enumerate((1, -1)):
                s = z + way * h

                @when(within(s))
                def _():
                    here = place(GU1, dp_of(s))
                    arrived(here, R.ag_r.at[GU1, s])

                    @when(within(z - way))
                    def _():
                        remote(
                            here, here, R.hop.at[h, i], R.ag_r.at[GU1, s], dp_of(z - way), t
                        ).start()

                    to_sibling(GU1, s)

        def ag_hops_sent():
            for h in range(1, nc - 1):
                for i, way in enumerate((1, -1)):

                    @when(within(z + way * h) & within(z - way))
                    def _():
                        sent(place(GU1, dpi), R.hop.at[h, i])

        def ag_done(u):
            if not cast:
                pltpu.make_async_copy(shard(u), place(u, dpi), R.loc.at[22 + nc + u]).wait()
            for s in range(nc):
                arrived(place(u, 2 * s + oc), R.sb_r.at[u, s])

        def ag_drain(u):
            for i, (mid, src, dst) in enumerate(() if u == GU1 else relays):

                @when(z == mid)
                def _():
                    sent(place(u, dp_of(src)), R.av_s.at[u, i])

            for s in range(nc):
                sent(shard(u), R.sb_s.at[u, s])

        def rs_merged(src, dst):
            if not has_via:
                return src != src
            return ((src == 0) & (dst == nc - 1)) | ((src == nc - 1) & (dst == 0))

        def rs_held(dst):
            if not has_via:
                return z != z
            return ((z == 1) & (dst == nc - 1)) | ((z == nc - 2) & (dst == 0))

        merges = ((0, 1, nc - 1), (nc - 1, nc - 2, 0)) if has_via else ()

        def unit(i, slot, zr, vr, shape):
            return SimpleNamespace(i=i, slot=slot, zr=zr, vr=vr, shape=shape)

        RD = unit(0, lambda d: R.box0.at[d], R.zr0, R.vr0, (fl, ds))
        RGA = unit(1, lambda d: R.box1.at[d, :, cols[0]], R.zr1, R.vr1, (ds, 2 * parts[0][1]))
        RGB = unit(5, lambda d: R.box1.at[d, :, cols[1]], R.zrb, R.vrb, (ds, 2 * parts[1][1]))

        def out_slot(d):
            return R.h2.at[pl.ds(0, wl), rows_of(d, ds)] if turned else R.box0.at[d, pl.ds(0, wl)]

        RO = unit(2, out_slot, R.zr2, R.vr2, (wl, ds))

        def RQ(g):
            lanes = pl.ds(g * g3, g3) if isinstance(g, int) else rows_of(g, g3)
            return unit(
                3 + g,
                lambda d: R.dt.at[rows_of(d, ds), lanes],
                R.zrq.at[g],
                R.vrq.at[g],
                (ds, g3),
            )

        def free_signal(i):
            pl.semaphore_signal(R.free.at[i], inc=1, device_id=(sib, t), device_id_type=MESH)

        def row_loop(total, cols):
            step = 128 if cols <= 512 else 16

            def over(act):
                @pl.loop(0, total // step)
                def _(i):
                    act(rows_of(i, step))

            return over

        def rs_late(u, d):
            if not has_via:
                return z != z
            if u is RGB or u is RD:
                return z != z
            return (d == 0) | (d == nc - 1) if u is RGA else (z == 0) | (z == nc - 1)

        def rs_direct(u, d):
            remote(
                u.slot(d), u.zr.at[z], R.rz_s.at[u.i, d], R.rz_r.at[u.i, z], dp_of(d), t
            ).start()

        def rs_rest(u):
            for d in range(nc):

                skip = rs_held(d) | rs_merged(z, d)

                @when(rs_late(u, d) & (z != d) & jnp.logical_not(skip))
                def _():
                    rs_direct(u, jnp.int32(d))

        def rs_unit(u, compute, stage, mine, pump=()):
            def finish(d):
                box = u.slot(d)
                arrived(box, R.rb_r.at[u.i, d])

                @row_loop(*u.shape)
                def _(rows):
                    box[rows, :] = (mine[rows] + box[rows, :].astype(F32)).astype(BF)

                @when(z == d)
                def _():
                    pltpu.make_async_copy(box, u.zr.at[z], R.self.at[u.i]).start()

                skip = rs_held(d) | rs_merged(z, d) | rs_late(u, d)

                @when((z != d) & jnp.logical_not(skip))
                def _():
                    rs_direct(u, d)

                for i, (src, mid, dst) in enumerate(merges):

                    @when((z == src) & (d == dst))
                    def _():
                        remote(
                            box, u.vr.at[i], R.rz_s.at[u.i, d], R.rv_r.at[u.i, i], dp_of(mid), t
                        ).start()

            def turn(i):
                return lax.rem(i + nc - 1, nc)

            @pl.loop(0, nc)
            def _(idx):
                d = turn(idx)
                slot = lax.rem(idx, 2)

                @when(idx >= 2)
                def _():
                    sent(stage.at[slot], R.rb_s.at[u.i, turn(idx + nc - 2)])

                def to_stage(lo, size, val):
                    stage[slot, :, lo : lo + size] = val.astype(BF)

                compute(2 * d + oc, to_stage)
                remote(
                    stage.at[slot], u.slot(d), R.rb_s.at[u.i, d], R.rb_r.at[u.i, d], sib, t
                ).start()

                @when(idx >= 1)
                def _():
                    finish(turn(idx + nc - 1))

                for i, act in pump:
                    when(idx == i)(act)

                def to_mine(lo, size, val):
                    mine[:, lo : lo + size] = val

                compute(2 * d + c, to_mine)

            finish(jnp.int32(nc - 2 if nc > 1 else 0))
            for i in (nc - 2, nc - 1):
                sent(stage.at[0], R.rb_s.at[u.i, (i + nc - 1) % nc])

        def rs_via(u):
            for i, (src, mid, dst) in enumerate(merges):

                @when(z == mid)
                def _():
                    box = u.slot(jnp.int32(dst))
                    arrived(u.vr.at[i], R.rv_r.at[u.i, i])

                    def add(tmp):
                        local_now(u.vr.at[i], tmp)

                        @row_loop(*u.shape)
                        def _(rows):
                            box[rows, :] = (
                                box[rows, :].astype(F32) + tmp[rows].astype(F32)
                            ).astype(BF)

                    pl.run_scoped(add, pltpu.VMEM(u.shape, BF))
                    remote(
                        box, u.zr.at[mid], R.rz_s.at[u.i, dst], R.rz_r.at[u.i, mid], dp_of(dst), t
                    ).start()

        def rs_arrived(u):
            for k in range(1, nc):
                s = chip(k)

                @when(jnp.logical_not(rs_merged(s, z)))
                def _():
                    arrived(u.zr.at[s], R.rz_r.at[u.i, s])

        def rs_drain(u):
            for k in range(1, nc):
                sent(u.slot(z), R.rz_s.at[u.i, chip(k)])
            pltpu.make_async_copy(u.slot(z), u.zr.at[z], R.self.at[u.i]).wait()

        def x_send(ph, k, src, dst):
            remote(src, dst, R.x_s.at[ph, k], R.x_r.at[ph, k], dpi, peer(k)).start()

        acc, xs, xr = R.acc, R.xs, R.xr
        steps = ((2, 0, 2, 1), (2, 1, 2, 2), (0, 0, 0, 1), (1, 1, 1, 2), (1, 0, 1, 2), (0, 1, 0, 1))

        def half_of(buf, slot, h):
            return buf.at[slot, pl.ds(h * hr, hr)]

        def step_send(ph, i):
            a, h, b, k = steps[i]
            remote(
                half_of(xs, a, h),
                half_of(xr, b, h),
                R.x_s.at[ph, i],
                R.x_r.at[ph, i],
                dpi,
                peer(k),
            ).start()

        def partial_rows(ph, product):
            if ph > 0:
                xs_sent(ph - 1)

            @pl.loop(0, tpn)
            def _(i):
                k = lax.rem(3 * (i + 1), 4) if square else lax.rem(i + 1, tpn)
                value = product(rows_of(peer(k), sr))

                @when(k > 0)
                def _():
                    xs[k - 1] = value.astype(BF)

                @when(k == 0)
                def _():
                    acc[...] = value

                if square:
                    for j, first in ((3, (0, 1)), (1, (2,)), (2, (3,))):

                        @when(k == j)
                        def _():
                            for m in first:
                                step_send(ph, m)
                else:

                    @when(k > 0)
                    def _():
                        x_send(ph, k, xs.at[k - 1], xr.at[k - 1])

        def sum_relay(ph):
            if not square:
                return
            for i, (slot, h) in ((0, (1, 0)), (1, (0, 1))):
                arrived(half_of(xr, 2, h), R.x_r.at[ph, i])
                rows = pl.ds(h * hr, hr)
                xs[slot, rows] = (xs[slot, rows].astype(F32) + xr[2, rows].astype(F32)).astype(BF)
                step_send(ph, 4 + i)

        def sum_arrived(ph):
            if square:
                for i in range(2, 6):
                    arrived(half_of(xr, 0, 0), R.x_r.at[ph, i])
            else:
                for k in range(1, tpn):
                    arrived(xr.at[k - 1], R.x_r.at[ph, k])

        def xs_sent(ph):
            if square:
                for i in range(6):
                    sent(half_of(xs, 0, 0), R.x_s.at[ph, i])
            else:
                for k in range(1, tpn):
                    sent(xs.at[k - 1], R.x_s.at[ph, k])

        def add_peers(rows):
            total = acc[rows]
            for k in range(2 if square else tpn - 1):
                total = total + xr[k, rows].astype(F32)
            return total

        def some_rows(buf, k, h):
            return buf.at[pl.ds(pl.multiple_of(source(k) * sr + h * hr, hr), hr)]

        def rows_copy(ph, buf, i, k, h, to):
            rows = some_rows(buf, k, h)
            return remote(rows, rows, R.g_s.at[ph, i], R.g_r.at[ph, i], dpi, peer(to))

        def rows_gather(ph, buf):
            if square:
                for i, (h, to) in enumerate(((0, 1), (1, 1), (1, 2), (0, 2))):
                    rows_copy(ph, buf, i, 0, h, to).start()
            else:
                mine = buf.at[own_rows]
                for k in range(1, tpn):
                    remote(mine, mine, R.g_s.at[ph, k], R.g_r.at[ph, k], dpi, peer(k)).start()

        def rows_relay(ph, buf):
            if square:
                arrived(some_rows(buf, 1, 0), R.g_r.at[ph, 0])
                rows_copy(ph, buf, 4, 1, 0, 2).start()
                arrived(some_rows(buf, 2, 1), R.g_r.at[ph, 2])
                rows_copy(ph, buf, 5, 2, 1, 1).start()

        def rows_arrived(ph, buf, k):
            if square:
                for j, h, i in ((1, 1, 1), (2, 0, 3), (3, 0, 4), (3, 1, 5)):

                    @when(k == j)
                    def _():
                        arrived(some_rows(buf, j, h), R.g_r.at[ph, i])
            else:

                @when(k > 0)
                def _():
                    arrived(buf.at[rows_of(source(k), sr)], R.g_r.at[ph, k])

            return rows_of(source(k), sr)

        def rows_sent(ph, buf):
            if square:
                for i in range(6):
                    sent(some_rows(buf, 0, 0), R.g_s.at[ph, i])
            else:
                for k in range(1, tpn):
                    sent(buf.at[own_rows], R.g_s.at[ph, k])

        def prepare(fq, fo, fg, fd, bq, bd):
            loads = [local(R.wq_f, fq, 8), local(R.wo_f, fo, 9)]
            loads += [local(R.wgu_f.at[:, h], fg.at[h], 10 + h) for h in range(2)]
            loads.append(local(R.wd_f, fd, 12))
            loads[0].wait()
            for m in range(3):
                bq[:, m * wl : (m + 1) * wl] = fq[m].astype(BF)
            local_now(bq, place(QKV, dpi))
            all_here()
            ag_near(QKV)
            for cp in loads[1:]:
                cp.wait()
            R.wo[:, rows_of(dpi, ds)] = fo[...].astype(BF)
            for lo, size, off in parts:
                for h in range(2):
                    to = off + h * size
                    R.wgu[rows_of(dpi, ds), to : to + size] = fg[h, :, lo : lo + size].astype(BF)
            bd[...] = fd[...].astype(BF)
            local_now(bd, place(DOWN, dpi))

        if cast:
            pl.run_scoped(
                prepare,
                pltpu.VMEM((3, ds, wl), F32),
                pltpu.VMEM((wl, ds), F32),
                pltpu.VMEM((2, ds, fl), F32),
                pltpu.VMEM((fl, ds), F32),
                pltpu.VMEM((ds, w3), BF),
                pltpu.VMEM((fl, ds), BF),
            )
        else:
            all_here()
            ag_near(QKV)

        load_x = local(R.x, R.h2, 1)
        load_y = local(R.cot, R.dt, 2)

        bs = R.bslot
        bs[z] = jnp.broadcast_to(R.brow[...], (8, w3))
        for k in range(1, nc):
            remote(
                bs.at[z], bs.at[z], R.b_s.at[chip(k)], R.b_r.at[z], dp_of(chip(k)), t
            ).start()

        seg = jnp.broadcast_to(R.seg[...].astype(F32), (LANES, n)).T
        start = jnp.zeros((1, LANES), F32)
        lane = lax.broadcasted_iota(jnp.int32, (n, LANES), 1)
        first = jnp.zeros((n, LANES), F32)
        for v in range(4):
            here = jnp.sum(jnp.where(seg == float(v), 1.0, 0.0), axis=0, keepdims=True)
            first = jnp.where(seg == float(v), start, first)
            start = start + here
        pos = lax.broadcasted_iota(jnp.int32, (n, LANES), 0).astype(F32) - first
        angle = pos * R.freq[...]
        entry = lax.rem(lane, HD)
        cosine = jnp.cos(angle)
        sine = jnp.sin(angle)
        part = HD // 8
        R.tc[...] = jnp.where(entry < 2 * part, cosine, 1.0)
        R.ts[...] = jnp.where(entry < part, -sine, jnp.where(entry < 2 * part, sine, 0.0))
        same = seg == lane.astype(F32)
        R.kseg[...] = jnp.where(same, 1.0, 0.0).astype(BF)
        R.qseg[...] = jnp.where(same | (lane >= 4), 0.0, MASKED).astype(BF)

        lane_row = lax.broadcasted_iota(jnp.int32, (1, LANES), 1)
        def rotate(values, rows, sign):
            up = pltpu.roll(values, LANES - part, 1)
            down = pltpu.roll(values, part, 1)
            other = jnp.where(lane_row < part, up, down)
            other = jnp.where((lane_row >= HD) & (lane_row < HD + part), up, other)
            return values * R.tc[rows] + other * (R.ts[rows] * sign)

        head_mask = [
            jnp.where((lane_row >= h * HD) & (lane_row < (h + 1) * HD), 1.0, 0.0).astype(BF)
            for h in range(2)
        ]

        def gain(i):
            return R.norm[i : i + 1, :]

        def no_terms():
            if not has_via:
                return

            @when((z == 0) | (z == nc - 1))
            def _():
                other = nc - 1 - z
                R.box0[0] = jnp.zeros_like(R.box0[0])
                R.box1[0] = jnp.zeros_like(R.box1[0])
                fills = [
                    local(R.box0.at[0], R.zr0.at[other], 8),
                    local(R.box1.at[0, :, cols[0]], R.zr1.at[other], 9),
                    local(R.box1.at[0, :, cols[1]], R.zrb.at[other], 13),
                    local(R.box0.at[0, pl.ds(0, wl)], R.zr2.at[other], 10),
                ]
                for g in range(2):
                    fills.append(
                        local(R.box1.at[0, :, pl.ds(0, g3)], R.zrq.at[g, other], 11 + g)
                    )
                for cp in fills:
                    cp.wait()

        def project(h1, wq):
            ag_far(QKV)
            ag_near(OUT)
            load_x.wait()

            @pl.loop(0, n // lt)
            def _(i):
                rows = rows_of(i, lt)
                hat, _inv = normed(R.h2[rows].astype(F32))
                h1[rows] = (hat * gain(0) + gain(1)).astype(BF)

            keep = local(h1, R.sp_h1, 1)
            no_terms()
            for k in range(1, nc):
                arrived(bs.at[chip(k)], R.b_r.at[chip(k)])
            total = bs[0]
            for s in range(1, nc):
                total = total + bs[s]
            R.bsum[0] = total
            remote(R.bsum.at[0], R.bsum.at[1], R.b_s.at[nc], R.b_r.at[nc], sib, t).start()
            ag_rest(QKV)
            arrived(R.bsum.at[1], R.b_r.at[nc])
            ag_far(OUT)
            ag_near(GU0)
            ag_done(QKV)
            local_now(R.ag_q, wq)
            bias = (R.bsum[0] + R.bsum[1])[0:1]

            @pl.loop(0, n // qb)
            def _(i):
                rows = rows_of(i, qb)
                for m in range(3):
                    for lo, size in chunks(wl, 512):
                        at = m * wl + lo
                        got = dot_nn(h1[rows], wq[:, at : at + size]) + bias[:, at : at + size]
                        if m == 2:
                            R.qkv[rows, at : at + size] = got.astype(BF)
                        else:
                            for p in range(size // LANES):
                                R.qkv[rows, at + p * LANES : at + (p + 1) * LANES] = rotate(
                                    got[:, p * LANES : (p + 1) * LANES], rows, 1.0
                                ).astype(BF)

            keep.wait()

        def scores(p, i, h):
            length = (i + 1) * qb
            rows = pl.ds(i * qb, qb)
            qkv = R.qkv
            lanes = rows_of(p, LANES)
            klanes = pl.ds(pl.multiple_of(wl + p * LANES, LANES), LANES)
            keys = jnp.concatenate([qkv[0:length, klanes], R.kseg[0:length]], axis=1)
            query = qkv[rows, lanes] * head_mask[h] * jnp.asarray(scale, BF)
            s = dot_nt(keys, jnp.concatenate([query, R.qseg[rows]], axis=1))
            low = s[length - qb :]
            causal = lax.broadcasted_iota(jnp.int32, (qb, qb), 0) <= lax.broadcasted_iota(
                jnp.int32, (qb, qb), 1
            )
            low = jnp.where(causal, low, MASKED)
            s = low if i == 0 else jnp.concatenate([s[: length - qb], low], axis=0)
            return s, query

        def attend(p):
            qkv = R.qkv
            lanes = rows_of(p, LANES)
            vlanes = pl.ds(pl.multiple_of(2 * wl + p * LANES, LANES), LANES)
            vt = qkv[:, vlanes].T
            for i in range(nq):
                length = (i + 1) * qb
                outs = []
                for h in range(2):
                    s, _query = scores(p, i, h)
                    top = jnp.max(s, axis=0, keepdims=True)
                    expo = jnp.exp(s - top)
                    total = jnp.sum(expo, axis=0, keepdims=True)
                    mixed = dot_nn(vt[h * HD : (h + 1) * HD, 0:length], expo.astype(BF))
                    outs.append(mixed * (1.0 / total))
                    R.lse[p, h : h + 1, i * qb : (i + 1) * qb] = top + jnp.log(total)
                R.o[i * qb : (i + 1) * qb, lanes] = jnp.concatenate(outs, axis=0).T.astype(BF)

        pl.run_scoped(project, pltpu.VMEM((n, D), BF), pltpu.VMEM((D, w3), BF))

        @pl.loop(0, pairs)
        def _(p):
            attend(p)

        ag_rest(OUT)
        ag_far(GU0)
        ag_near(DOWN)
        ag_done(OUT)

        partial_rows(0, lambda rows: dot_nn(R.o[rows], R.wo[...]))
        sum_relay(0)
        sum_arrived(0)

        def norm_rows(xown):
            local_now(R.x.at[own_rows], xown)

            @pl.loop(0, sr // lt)
            def _(i):
                rows = rows_of(i, lt)
                resid = add_peers(rows) + xown[rows].astype(F32)
                acc[rows] = resid
                hat, _inv = normed(resid)
                R.h2[pl.ds(pl.multiple_of(t * sr + i * lt, lt), lt)] = (
                    hat * gain(2) + gain(3)
                ).astype(BF)

        pl.run_scoped(norm_rows, pltpu.VMEM((sr, D), BF))

        rows_gather(0, R.h2)
        local_now(acc, R.sp_r1)
        ag_rest(GU0)
        ag_far(DOWN)
        ag_done(GU0)
        rows_relay(0, R.h2)
        ag_rest(DOWN)
        ag_near(GU1)
        ag_done(DOWN)

        def feed(sp):
            def both_parts(at):
                def forward(i):
                    lo, size, off = parts[i]

                    def run(wd):
                        load = local(R.ag_d.at[pl.ds(lo, size)], wd, 1)
                        if i == 0:
                            load_y.wait()
                        load.wait()

                        @pl.loop(0, tpn)
                        def _(k):
                            if i == 0:

                                @when(k == 2)
                                def _():
                                    ag_hop(1)

                                rows = rows_arrived(0, R.h2, k)
                            else:
                                rows = rows_of(source(k), sr)
                            for at_col, width in chunks(size, 512):
                                gc = pl.ds(off + at_col, width)
                                uc = pl.ds(off + size + at_col, width)
                                g = dot_nn(R.h2[rows], R.wgu[:, gc])
                                u = dot_nn(R.h2[rows], R.wgu[:, uc])
                                da = dot_nt(R.dt[rows], wd[at_col : at_col + width])
                                sig = 1.0 / (1.0 + jnp.exp(-g))
                                act = g * sig
                                at[pl.ds(lo + at_col, width), rows] = (act * u).astype(BF).T
                                dg = da * u * sig * (1.0 + g * (1.0 - sig))
                                sp[rows, gc] = dg.astype(BF)
                                sp[rows, uc] = (da * act).astype(BF)

                    pl.run_scoped(run, pltpu.VMEM((size, D), BF))

                def gu_grad(i, u, pump):
                    _, size, off = parts[i]

                    def run(stage, mine):
                        def compute(j, put):
                            left = R.h2[:, rows_of(j, ds)].T
                            put(0, 2 * size, dot_nn(left, sp[:, off : off + 2 * size]))

                        rs_unit(u, compute, stage, mine, pump)

                    pl.run_scoped(
                        run, pltpu.VMEM((2, ds, 2 * size), BF), pltpu.VMEM((ds, 2 * size), F32)
                    )

                def down_grad(stage, mine):
                    def compute(j, put):
                        put(0, ds, dot_nn(at[...], R.dt[:, rows_of(j, ds)]))

                    rs_unit(RD, compute, stage, mine)

                forward(0)
                gu_grad(0, RGA, [(nc - 1, lambda: ag_hop(2))])
                for h in range(3, nc):
                    ag_hop(h)
                rs_rest(RGA)
                rs_via(RGA)
                ag_done(GU1)
                forward(1)
                keep = local(at, R.sp_a, 1)
                down = pltpu.VMEM((2, fl, ds), BF), pltpu.VMEM((fl, ds), F32)
                if not square:
                    pl.run_scoped(down_grad, *down)
                partial_rows(1, lambda rows: dot_nt(sp[rows], R.wgu[...]))
                if square:
                    pl.run_scoped(down_grad, *down)
                    sum_relay(1)
                gu_grad(1, RGB, ())
                keep.wait()

            pl.run_scoped(both_parts, pltpu.VMEM((fl, n), BF))

        pl.run_scoped(feed, pltpu.VMEM((n, f2), BF))
        rows_sent(0, R.h2)
        ag_hops_sent()
        for u in (GU0, GU1):
            ag_sent(u)
            ag_drain(u)
        load_h1 = local(R.sp_h1, R.h2, 6)
        load_wq = [
            local(
                R.ag_q.at[:, pl.ds(m * wl + g * gl, gl)],
                R.wgu.at[:, pl.ds(g * g3 + m * gl, gl)],
                16 + nc + 3 * g + m,
            )
            for g in range(2)
            for m in range(3)
        ]

        def norm_two(r1, yown):
            one = local(R.cot.at[own_rows], yown, 1)
            local_now(R.sp_r1, r1)
            one.wait()
            sum_arrived(1)
            R.gsum[...] = jnp.zeros_like(R.gsum)

            @pl.loop(0, sr // lt)
            def _(i):
                rows = rows_of(i, lt)
                grad = add_peers(rows)
                hat, inv = normed(r1[rows])
                out = yown[rows].astype(F32) + norm_back(grad, hat, inv, gain(2))
                acc[rows] = out
                R.dt[pl.ds(pl.multiple_of(t * sr + i * lt, lt), lt)] = out.astype(BF)
                R.gsum[2:3] += jnp.sum(grad * hat, axis=0, keepdims=True)
                R.gsum[3:4] += jnp.sum(grad, axis=0, keepdims=True)

            rows_gather(1, R.dt)
            local_now(acc, R.sp_dr1)

        pl.run_scoped(norm_two, pltpu.VMEM((sr, D), F32), pltpu.VMEM((sr, D), BF))

        load_h1.wait()
        if turned:

            @pl.loop(0, n // qb)
            def _(i):
                R.wgu[:, pl.ds(pl.multiple_of(w3 + i * qb, LANES), qb)] = R.h2[rows_of(i, qb)].T

            free_signal(0)

        rows_relay(1, R.dt)
        rs_via(RD)

        def mlp_out(a, wd, out, own):
            local_now(R.ag_d, wd)

            @pl.loop(1, tpn + 1)
            def _(k):
                local_now(R.sp_a.at[:, rows_of(peer(k), sr)], a)
                value = dot_nn(a[...].T, wd[...])

                @when(k < tpn)
                def _():
                    out[...] = value.astype(BF)
                    local_now(out, R.mlp_p.at[k - 1])

                @when(k == tpn)
                def _():
                    own[...] = value
                    local_now(own, R.sp_mlp)

        pl.run_scoped(
            mlp_out,
            pltpu.VMEM((fl, sr), BF),
            pltpu.VMEM((fl, D), BF),
            pltpu.VMEM((sr, D), BF),
            pltpu.VMEM((sr, D), F32),
        )

        if not turned:
            rs_drain(RD)
            free_signal(0)

        def attention_back(dp):
            def back(do, dk, dv):
                @pl.loop(0, tpn)
                def _(k):
                    rows = rows_arrived(1, R.dt, k)
                    do[rows] = dot_nt(R.dt[rows], R.wo[...]).astype(BF)

                for k in range(1, tpn):
                    x_send(3, k, R.mlp_p.at[k - 1], R.mlp_r.at[k - 1])


                def out_grad(ot, stage, mine):
                    ot[...] = R.o[...].T

                    def compute(j, put):
                        put(0, ds, dot_nn(ot[...], R.dt[:, rows_of(j, ds)]))

                    pl.semaphore_wait(R.free.at[0], 1)
                    rs_unit(RO, compute, stage, mine)

                pl.run_scoped(
                    out_grad,
                    pltpu.VMEM((wl, n), BF),
                    pltpu.VMEM((2, wl, ds), BF),
                    pltpu.VMEM((wl, ds), F32),
                )

                rs_rest(RO)
                rs_via(RGB)
                rows_sent(1, R.dt)
                free_signal(1)
                for copy in load_wq:
                    copy.wait()

                def pair_back(g, own):
                    qkv = R.qkv
                    p = g * (pairs // 2) + own
                    lanes = rows_of(p, LANES)
                    klanes = pl.ds(pl.multiple_of(wl + p * LANES, LANES), LANES)
                    vlanes = pl.ds(pl.multiple_of(2 * wl + p * LANES, LANES), LANES)

                    def out_lanes(m):
                        return pl.ds(pl.multiple_of(g * g3 + m * gl + own * LANES, LANES), LANES)

                    kt = qkv[:, klanes].T
                    dk[...] = jnp.zeros_like(dk)
                    dv[...] = jnp.zeros_like(dv)
                    for i in range(nq):
                        length = (i + 1) * qb
                        rows = pl.ds(i * qb, qb)
                        pbs, dss, qms, doms, dqs = [], [], [], [], []
                        for h in range(2):
                            s, query = scores(p, i, h)
                            prob = jnp.exp(s - R.lse[p, h : h + 1, i * qb : (i + 1) * qb])
                            dom = do[rows, lanes] * head_mask[h]
                            dprob = dot_nt(qkv[0:length, vlanes], dom)
                            weighted = jnp.sum(prob * dprob, axis=0, keepdims=True)
                            dsc = (prob * (dprob - weighted)).astype(BF)
                            pbs.append(prob.astype(BF))
                            dss.append(dsc)
                            qms.append(query)
                            doms.append(dom)
                            dqs.append(dot_nn(kt[h * HD : (h + 1) * HD, 0:length], dsc))
                        dv[0:length] += dot_nn(
                            jnp.concatenate(pbs, axis=1), jnp.concatenate(doms, axis=0)
                        )
                        dk[0:length] += dot_nn(
                            jnp.concatenate(dss, axis=1), jnp.concatenate(qms, axis=0)
                        )
                        dq = jnp.concatenate(dqs, axis=0).T * scale
                        dp[rows, out_lanes(0)] = rotate(dq, rows, -1.0).astype(BF)
                    dp[:, out_lanes(1)] = rotate(dk[...], pl.ds(0, n), -1.0).astype(BF)
                    dp[:, out_lanes(2)] = dv[...].astype(BF)

                @pl.loop(0, 2)
                def _(g):
                    @pl.loop(0, pairs // 2)
                    def _(own):
                        pair_back(g, own)

                    @when(g == 0)
                    def _():
                        rs_via(RO)
                        pl.semaphore_wait(R.free.at[1], 1)

                    @when(g == 1)
                    def _():
                        rs_via(RQ(0))
                        partial_rows(2, lambda rows: dot_nt(dp[rows], R.wgu[:, 0:w3]))

                    def qkv_grad(stage, mine):
                        def compute(j, put):
                            if turned:
                                left = R.wgu[rows_of(j, ds), w3 : w3 + n]
                            else:
                                left = R.h2[:, rows_of(j, ds)].T
                            put(0, g3, dot_nn(left, dp[:, rows_of(g, g3)]))

                        rs_unit(RQ(g), compute, stage, mine)

                    pl.run_scoped(qkv_grad, pltpu.VMEM((2, ds, g3), BF), pltpu.VMEM((ds, g3), F32))
                    rs_rest(RQ(g))

            pl.run_scoped(
                back,
                pltpu.VMEM((n, wl), BF),
                pltpu.VMEM((n, LANES), F32),
                pltpu.VMEM((n, LANES), F32),
            )
            sums = jnp.zeros((1, w3), F32)
            for i in range(n // qb):
                sums = sums + jnp.sum(
                    dp[i * qb : (i + 1) * qb].astype(F32), axis=0, keepdims=True
                )
            R.gbs[0] = jnp.broadcast_to(sums, (8, w3))
            remote(R.gbs.at[0], R.gbs.at[1], R.c_s.at[nc], R.c_r.at[nc], sib, t).start()


        pl.run_scoped(attention_back, pltpu.VMEM((n, w3), BF))

        arrived(R.gbs.at[1], R.c_r.at[nc])
        cslot = R.cslot
        cslot[z] = R.gbs[0] + R.gbs[1]
        for k in range(1, nc):
            remote(
                cslot.at[z], cslot.at[z], R.c_s.at[chip(k)], R.c_r.at[z], dp_of(chip(k)), t
            ).start()

        sum_relay(2)

        def block_rows(r1, own, got, out):
            a = local(R.sp_r1, r1, 1)
            b = local(R.sp_mlp, own, 2)
            for k in range(1, tpn):
                arrived(R.mlp_r.at[k - 1], R.x_r.at[3, k])
            local_now(R.mlp_r, got)
            a.wait()
            b.wait()

            @pl.loop(0, sr // lt)
            def _(i):
                rows = rows_of(i, lt)
                total = own[rows]
                for k in range(1, tpn):
                    total = total + got[k - 1, rows].astype(F32)
                out[rows] = (r1[rows] + total).astype(BF)

            local_now(out, R.block_out)

        pl.run_scoped(
            block_rows,
            pltpu.VMEM((sr, D), F32),
            pltpu.VMEM((sr, D), F32),
            pltpu.VMEM((tpn - 1, sr, D), BF),
            pltpu.VMEM((sr, D), BF),
        )

        rs_via(RQ(1))

        def norm_one(dr1, xown):
            one = local(R.x.at[own_rows], xown, 1)
            local_now(R.sp_dr1, dr1)
            one.wait()
            sum_arrived(2)

            @pl.loop(0, sr // lt)
            def _(i):
                rows = rows_of(i, lt)
                grad = add_peers(rows)
                hat, inv = normed(xown[rows].astype(F32))
                dr1[rows] = dr1[rows] + norm_back(grad, hat, inv, gain(0))
                R.gsum[0:1] += jnp.sum(grad * hat, axis=0, keepdims=True)
                R.gsum[1:2] += jnp.sum(grad, axis=0, keepdims=True)

            keep = local(dr1, R.input_grad, 1)
            ns = R.nsum
            ns[0, 0:4] = R.gsum[0:4, 0 : D // 2]
            ns[0, 4:8] = R.gsum[0:4, D // 2 :]
            remote(ns.at[0], ns.at[1], R.n_s.at[0], R.n_r.at[0], sib, t).start()
            arrived(ns.at[1], R.n_r.at[0])
            zs = R.nz
            zs[z] = ns[0] + ns[1]
            for k in range(1, nc):
                remote(
                    zs.at[z], zs.at[z], R.n_s.at[k], R.n_r.at[1 + z], dp_of(chip(k)), t
                ).start()
            for k in range(1, nc):
                arrived(zs.at[chip(k)], R.n_r.at[1 + chip(k)])
            total = zs[0]
            for s in range(1, nc):
                total = total + zs[s]
            ts = R.nt
            ts[t] = total
            for k in range(1, tpn):
                remote(
                    ts.at[t], ts.at[t], R.n_s.at[nc + k], R.n_r.at[1 + nc + t], dpi, peer(k)
                ).start()
            for k in range(1, tpn):
                arrived(ts.at[peer(k)], R.n_r.at[1 + nc + peer(k)])
            total = ts[0]
            for s in range(1, tpn):
                total = total + ts[s]
            R.gn[...] = total
            keep.wait()

        pl.run_scoped(norm_one, pltpu.VMEM((sr, D), F32), pltpu.VMEM((sr, D), BF))

        for k in range(1, nc):
            arrived(cslot.at[chip(k)], R.c_r.at[chip(k)])
        total = cslot[0]
        for s in range(1, nc):
            total = total + cslot[s]
        R.gb[...] = total

        for u in (RD, RGA, RGB, RO, RQ(0), RQ(1)):
            rs_arrived(u)

        for u in (QKV, OUT, DOWN):
            ag_sent(u)
        for u in (QKV, OUT, DOWN):
            ag_drain(u)
        for u in ([RD] if turned else []) + [RGA, RGB, RO, RQ(0), RQ(1)]:
            rs_drain(u)
        xs_sent(2)
        for k in range(1, tpn):
            sent(R.mlp_p.at[k - 1], R.x_s.at[3, k])
            sent(R.nt.at[0], R.n_s.at[nc + k])
        for k in range(1, nc):
            sent(bs.at[z], R.b_s.at[chip(k)])
            sent(cslot.at[0], R.c_s.at[chip(k)])
            sent(R.nz.at[0], R.n_s.at[k])
        sent(R.bsum.at[0], R.b_s.at[nc])
        sent(R.gbs.at[0], R.c_s.at[nc])
        sent(R.nsum.at[0], R.n_s.at[0])

    return kern


def fused(x, seg, cot, norm, brow, freq, weights, dpn, tpn, cast):
    n = x.shape[0]
    wl = weights[1].shape[0]
    fl = weights[3].shape[0]
    nc = dpn // 2
    ds = D // dpn
    sr = n // tpn
    w3, f2 = 3 * wl, 2 * fl
    pairs = wl // LANES
    g3 = 3 * (wl // 2)
    hbm = pl.BlockSpec(memory_space=pl.ANY)
    vmem = pl.BlockSpec(memory_space=pltpu.VMEM)
    ins = [
        ("x", hbm),
        ("seg", vmem),
        ("cot", hbm),
        ("norm", vmem),
        ("brow", vmem),
        ("freq", vmem),
    ]
    shards = ["wq_s", "wo_s", "wgu_s", "wd_s"]
    ins += [(i, hbm) for i in (["wq_f", "wo_f", "wgu_f", "wd_f"] if cast else shards)]
    parts = hidden_parts(fl)
    boxes = [(fl, ds), (ds, 2 * parts[0][1]), (wl, ds)]
    last = (ds, 2 * parts[1][1])
    outs = [
        ("block_out", (sr, D), BF, hbm),
        ("input_grad", (sr, D), F32, hbm),
        ("gn", (8, D // 2), F32, vmem),
        ("gb", (8, w3), F32, vmem),
    ]
    outs += [("zr%d" % u, (nc,) + s, BF, hbm) for u, s in enumerate(boxes)]
    outs += [("zrq", (2, nc, ds, g3), BF, hbm), ("zrb", (nc,) + last, BF, hbm)]
    outs += [("vrq", (2, 2, ds, g3), BF, hbm), ("vrb", (2,) + last, BF, hbm)]
    outs += [
        ("ag_q", (D, w3), BF, hbm),
        ("ag_d", (fl, D), BF, hbm),
        ("mlp_p", (tpn - 1, sr, D), BF, hbm),
        ("mlp_r", (tpn - 1, sr, D), BF, hbm),
        ("sp_h1", (n, D), BF, hbm),
        ("sp_a", (fl, n), BF, hbm),
        ("sp_r1", (sr, D), F32, hbm),
        ("sp_mlp", (sr, D), F32, hbm),
        ("sp_dr1", (sr, D), F32, hbm),
    ]
    outs += [("vr%d" % u, (2,) + s, BF, hbm) for u, s in enumerate(boxes)]
    dma = pltpu.SemaphoreType.DMA
    scratch = [
        ("wgu", pltpu.VMEM((D, f2), BF)),
        ("wo", pltpu.VMEM((wl, D), BF)),
        ("h2", pltpu.VMEM((n, D), BF)),
        ("dt", pltpu.VMEM((n, D), BF)),
        ("xs", pltpu.VMEM((tpn - 1, sr, D), BF)),
        ("xr", pltpu.VMEM((tpn - 1, sr, D), BF)),
        ("acc", pltpu.VMEM((sr, D), F32)),
        ("qkv", pltpu.VMEM((n, w3), BF)),
        ("o", pltpu.VMEM((n, wl), BF)),
        ("tc", pltpu.VMEM((n, LANES), F32)),
        ("ts", pltpu.VMEM((n, LANES), F32)),
        ("kseg", pltpu.VMEM((n, LANES), BF)),
        ("qseg", pltpu.VMEM((n, LANES), BF)),
        ("lse", pltpu.VMEM((pairs, 2, n), F32)),
        ("bslot", pltpu.VMEM((nc, 8, w3), F32)),
        ("bsum", pltpu.VMEM((2, 8, w3), F32)),
        ("gbs", pltpu.VMEM((2, 8, w3), F32)),
        ("cslot", pltpu.VMEM((nc, 8, w3), F32)),
        ("gsum", pltpu.VMEM((8, D), F32)),
        ("nsum", pltpu.VMEM((2, 8, D // 2), F32)),
        ("nz", pltpu.VMEM((nc, 8, D // 2), F32)),
        ("nt", pltpu.VMEM((tpn, 8, D // 2), F32)),
    ]
    scratch += [("box0", pltpu.VMEM((nc, fl, ds), BF)), ("box1", pltpu.VMEM((nc, ds, f2), BF))]
    scratch += [
        ("dum", dma((1,))),
        ("loc", dma((27 + nc,))),
        ("self", dma((6,))),
        ("hop", dma((nc, 2))),
        ("free", pltpu.SemaphoreType.REGULAR((2,))),
        ("ag_s", dma((5, nc))),
        ("ag_r", dma((5, nc))),
        ("av_s", dma((5, 2))),
        ("sb_s", dma((5, nc))),
        ("sb_r", dma((5, nc))),
        ("rb_s", dma((6, nc))),
        ("rb_r", dma((6, nc))),
        ("rz_s", dma((6, nc))),
        ("rz_r", dma((6, nc))),
        ("rv_r", dma((6, 2))),
        ("x_s", dma((4, max(tpn, 6)))),
        ("x_r", dma((4, max(tpn, 6)))),
        ("g_s", dma((2, max(tpn, 6)))),
        ("g_r", dma((2, max(tpn, 6)))),
        ("b_s", dma((nc + 1,))),
        ("b_r", dma((nc + 1,))),
        ("c_s", dma((nc + 1,))),
        ("c_r", dma((nc + 1,))),
        ("n_s", dma((nc + tpn,))),
        ("n_r", dma((1 + nc + tpn,))),
    ]
    names = [i[0] for i in ins] + [o[0] for o in outs] + [s[0] for s in scratch]
    got = pl.pallas_call(
        make_kernel(names, n, wl, fl, dpn, tpn, cast),
        out_shape=[jax.ShapeDtypeStruct(s, d) for _, s, d, _ in outs],
        in_specs=[s for _, s in ins],
        out_specs=[m for _, _, _, m in outs],
        scratch_shapes=[s for _, s in scratch],
        compiler_params=pltpu.CompilerParams(
            collective_id=0, has_side_effects=True, vmem_limit_bytes=63 * 2**20
        ),
        name="block_step",
    )(x, seg, cot, norm, brow, freq, *weights)
    return got[:9]


def adamw(weight, first, second, grad, rate, decay):
    new_first = BETA_ONE * first + (1.0 - BETA_ONE) * grad
    new_second = BETA_TWO * second + (1.0 - BETA_TWO) * grad * grad
    direction = (
        new_first
        / (1.0 - BETA_ONE**STEP)
        / (jnp.sqrt(new_second / (1.0 - BETA_TWO**STEP)) + ADAM_EPS)
    )
    return (new_first, new_second, weight - rate * (direction + decay * weight))


def update_all(groups, norm_grad, norm_state, passed):
    hbm = pl.BlockSpec(memory_space=pl.ANY)
    f32 = lambda s: pltpu.VMEM(s, F32)
    n_groups = len(groups)
    scratch = []
    for grads, _, _, _, pieces, _ in groups:
        scratch += [pltpu.VMEM(grad.shape, BF) for grad in grads]
        scratch += [f32(piece[2]) for piece in pieces for _ in range(3)]
    n_scratch = len(scratch)
    n_arrays = sum(len(g[0]) + 3 for g in groups)
    count = sum(len(g[0]) + 6 * len(g[4]) for g in groups) + 7 + 2 * len(passed)
    scratch += [f32(norm_grad.shape)] + [f32(x.shape) for x in norm_state]
    scratch += [pltpu.VMEM(x.shape, x.dtype) for x in passed]

    def kern(*refs):
        n_ins = n_arrays + 4 + len(passed)
        n_outs = 3 * n_groups + 3 + len(passed)
        ins, outs = refs[:n_ins], refs[n_ins : n_ins + n_outs]
        bufs, sem = refs[n_ins + n_outs : -1], refs[-1]
        at = iter(range(count))
        loads, plan = [], []

        def start(src, dst):
            cp = pltpu.make_async_copy(src, dst, sem.at[next(at)])
            cp.start()
            return cp

        arrays, spaces = iter(ins[:n_arrays]), iter(bufs[:n_scratch])
        for i, (grads, _, _, _, pieces, rate) in enumerate(groups):
            terms = [next(spaces) for _ in grads]
            got = [start(next(arrays), space) for space in terms]
            whole = [next(arrays) for _ in range(3)]
            state = []
            for _, state_part, _ in pieces:
                state.append([next(spaces) for _ in range(3)])
                got += [start(state_part(a), b) for a, b in zip(whole, state[-1], strict=True)]
            plan.append((got, terms, state, pieces, rate, outs[3 * i : 3 * i + 3]))
        rest = bufs[n_scratch:]
        small = [start(a, b) for a, b in zip(ins[n_arrays:], rest, strict=True)]
        stores = []
        for got, g, state, pieces, rate, dst in plan:
            for cp in got:
                cp.wait()
            for j, (grad_part, state_part, (rows, cols)) in enumerate(pieces):
                step = 64 if cols <= 512 else 16
                terms = grad_part(g)
                w, m, v = state[j]

                @pl.loop(0, rows // step)
                def _(r):
                    at_rows = pl.ds(pl.multiple_of(r * step, step), step)
                    grad = terms[0][at_rows, :].astype(F32)
                    for term in terms[1:]:
                        grad = grad + term[at_rows, :].astype(F32)
                    first, second, new = adamw(
                        w[at_rows, :], m[at_rows, :], v[at_rows, :], grad, rate, DECAY
                    )
                    m[at_rows, :] = first
                    v[at_rows, :] = second
                    w[at_rows, :] = new

                for k, buf in enumerate((m, v, w)):
                    stores.append(start(buf, state_part(dst[k])))
        for cp in small:
            cp.wait()
        g, w, m, v = rest[:4]
        half = w.shape[1] // 2
        for h in range(2):
            cols = slice(h * half, (h + 1) * half)
            first, second, new = adamw(
                w[:, cols], m[:, cols], v[:, cols], g[4 * h : 4 * h + 4], 0.5, 0.0
            )
            m[:, cols] = first
            v[:, cols] = second
            w[:, cols] = new
        for a, b in zip(
            (m, v, w) + tuple(rest[4:]), outs[3 * n_groups :], strict=True
        ):
            stores.append(start(a, b))
        for cp in stores:
            cp.wait()

    out_shape = []
    flat = []
    for grads, weight, first, second, _, _ in groups:
        flat += [*grads, weight, first, second]
        out_shape += [jax.ShapeDtypeStruct(weight.shape, F32)] * 3
    flat += [norm_grad, *norm_state, *passed]
    out_shape += [jax.ShapeDtypeStruct(x.shape, x.dtype) for x in (*norm_state, *passed)]
    got = pl.pallas_call(
        kern,
        out_shape=out_shape,
        in_specs=[hbm] * len(flat),
        out_specs=[hbm] * len(out_shape),
        scratch_shapes=scratch + [pltpu.SemaphoreType.DMA((count,))],
        compiler_params=pltpu.CompilerParams(vmem_limit_bytes=56 * 2**20),
        name="adamw",
    )(*flat)
    return [tuple(got[3 * i : 3 * i + 3]) for i in range(n_groups + 1)], got[3 * n_groups + 3 :]


def body(
    tokens,
    segments,
    cotangent,
    norm_params,
    norm_m,
    norm_v,
    qkv_bias,
    bias_m,
    bias_v,
    w_qkv,
    qkv_m,
    qkv_v,
    w_out,
    out_m,
    out_v,
    w_gateup,
    gateup_m,
    gateup_v,
    w_down,
    down_m,
    down_v,
):
    n_rows, model = tokens.shape
    dpn = lax.axis_size("dp")
    tpn = lax.axis_size("tensor")
    ds, _, wl = w_qkv.shape
    fl = w_down.shape[0]
    pad = -fl % LANES
    heads, cut = qkv_bias.shape[1:]
    assert segments.shape[0] == 1 and model == D
    me = lax.axis_index("dp")

    bias = qkv_bias.astype(BF).astype(F32)
    wide = lax.dynamic_update_slice(jnp.zeros((3, heads, HD), F32), bias, (0, 0, me * cut))
    brow = wide.reshape(1, 3 * wl)
    part = HD // 8
    freq = ROPE_BASE ** (-2.0 * (np.arange(LANES) % part) / (HD // 4))
    freq = jnp.asarray(freq.reshape(1, LANES), F32)
    cast = not pad
    parts = hidden_parts(fl + pad)
    if cast:
        weights = (jnp.transpose(w_qkv, (1, 0, 2)), w_out, w_gateup, w_down)
    else:
        wgu = jnp.pad(w_gateup.astype(BF), ((0, 0), (0, 0), (0, pad)))
        weights = (
            w_qkv.astype(BF).reshape(ds, 3 * wl),
            w_out.astype(BF),
            jnp.concatenate(
                [wgu[:, :, lo : lo + size].reshape(ds, 2 * size) for lo, size, _ in parts], axis=1
            ),
            jnp.pad(w_down.astype(BF), ((0, pad), (0, 0))),
        )
    block_out, input_grad, gn, gb, red_down, red_gu, red_out, red_qkv, red_gub = fused(
        tokens, segments, cotangent, norm_params, brow, freq, weights, dpn, tpn, cast
    )
    red_bias = jnp.swapaxes(gb[0].reshape(2, 3, wl // 2), 0, 1).reshape(3, heads, HD)
    red_bias = lax.dynamic_slice(red_bias, (0, 0, me * cut), (3, heads, cut))
    gl = wl // 2
    nc = dpn // 2
    qkv_pieces = [
        (
            lambda r, g=g, m=m: [r[0].at[g, s, :, pl.ds(m * gl, gl)] for s in range(nc)],
            lambda r, g=g, m=m: r.at[m, :, pl.ds(g * gl, gl)],
            (ds, gl),
        )
        for g in range(2)
        for m in range(3)
    ]
    whole = lambda r: r
    every = lambda r: [r[0].at[s] for s in range(nc)]

    def turn(x):
        return jnp.transpose(x, (1, 0, 2))

    groups = [
        ((red_qkv,), turn(w_qkv), turn(qkv_m), turn(qkv_v), qkv_pieces, D ** (-0.5)),
        ((red_out,), w_out, out_m, out_v, [(every, whole, w_out.shape)], HD ** (-0.5)),
    ]
    if not pad:
        gu_pieces = [
            (
                lambda r, i=i, h=h, c=size: [r[i].at[s, :, pl.ds(h * c, c)] for s in range(nc)],
                lambda r, h=h, lo=lo, c=size: r.at[:, h, pl.ds(lo, c)],
                (ds, size),
            )
            for i, (lo, size, _) in enumerate(parts)
            for h in range(2)
        ]
        groups += [
            ((red_gu, red_gub), w_gateup, gateup_m, gateup_v, gu_pieces, D ** (-0.5)),
            ((red_down,), w_down, down_m, down_v, [(every, whole, w_down.shape)], FF ** (-0.5)),
        ]
    done, (block_out, input_grad) = update_all(
        groups, gn, (norm_params, norm_m, norm_v), (block_out, input_grad)
    )
    new_norm = done.pop()
    new_qkv = tuple(turn(x) for x in done[0])
    if pad:
        both = [
            jnp.sum(r, axis=0, dtype=F32).reshape(ds, 2, size)
            for r, (_, size, _) in zip((red_gu, red_gub), parts, strict=True)
        ]
        red_gu = jnp.concatenate(both, axis=2)[:, :, :fl]
        red_down = jnp.sum(red_down, axis=0, dtype=F32)[:fl]
        done += [
            adamw(w_gateup, gateup_m, gateup_v, red_gu, D ** (-0.5), DECAY),
            adamw(w_down, down_m, down_v, red_down, FF ** (-0.5), DECAY),
        ]
    return (
        (block_out, input_grad)
        + new_norm
        + adamw(qkv_bias, bias_m, bias_v, red_bias, 0.3, 0.0)
        + new_qkv
        + done[1]
        + done[2]
        + done[3]
    )


def solution(mesh):
    rows = P("dp", None)
    bias = P(None, "tensor", "dp")
    wide = P("dp", None, "tensor")
    tall = P("tensor", "dp")
    split = P(("dp", "tensor"), None)
    return jax.shard_map(
        body,
        mesh=mesh,
        in_specs=(rows,) * 3 + (P(),) * 3 + (bias,) * 3 + (wide,) * 3 + (tall,) * 3 + (wide,) * 3
        + (tall,) * 3,
        out_specs=(split,) * 2 + (P(),) * 3 + (bias,) * 3 + (wide,) * 3 + (tall,) * 3 + (wide,) * 3
        + (tall,) * 3,
        check_vma=False,
    )
```
